128 devices in a mesh: expert: 32 (over y, x, core), mp: 4 (over z).
Axes of the slice: x: 4, y: 4, z: 4, core: 2. Of those that a mesh axis runs over, the one named last changes fastest.
Arguments:
- inputs: float32 [64, 512, 768], P('expert', 'mp'), may hold values from -6 to 6
- projection_in: bfloat16 [3, 768, 768], P(None, 'expert', 'mp'), may hold values from -0.3125 to 0.3125
- projection_out: bfloat16 [768, 768], P('mp', 'expert'), may hold values from -0.875 to 0.875
- gain_attention: float32 [768], replicated, may hold values from 0.5 to 1.5
- gain_experts: float32 [768], replicated, may hold values from 0.5 to 1.5
- router_weight: float32 [768, 64], replicated, may hold values from -0.15625 to 0.15625
- bias_table: float32 [32, 12], replicated, may hold values from -3 to 3
- expert_in: bfloat16 [64, 768, 3072], P('expert', None, 'mp'), may hold values from -0.21875 to 0.21875
- expert_out: bfloat16 [64, 3072, 768], P('expert', 'mp'), may hold values from -10 to 10
- routes: int32 [64, 512, 1], P('expert', 'mp'), may hold values from 0 to 63; in each aligned block of 128 rows (0 to 127, 128 to 255, ..., all dimensions but the last counted through in order) at most 4 rows name the same one
- segments: int32 [64, 512], P('expert', 'mp'), may hold values from 0 to 4, as said below
- cotangent: float32 [64, 512, 768], P('expert', 'mp'), may hold values from -6 to 6
Outputs:
- block_out: float32 [64, 512, 768], P('expert', 'mp')
- input_gradient_rows: float32 [64, 512, 768], P('expert', 'mp')
- grad_projection_in: float32 [3, 768, 768], P(None, 'expert', 'mp')
- grad_projection_out: float32 [768, 768], P('mp', 'expert')
- grad_gain_attention: float32 [768], replicated
- grad_gain_experts: float32 [768], replicated
- grad_router: float32 [768, 64], replicated
- grad_table: float32 [32, 12], replicated
- grad_expert_in: float32 [64, 768, 3072], P('expert', None, 'mp')
- grad_expert_out: float32 [64, 3072, 768], P('expert', 'mp')
The draws below stay inside these ranges and needn't reach their ends.
Inputs may be any that keep to these rules, and one draw needn't show every extreme that they name: `routes`: in each aligned block of 128 tokens, at most 4 tokens name the same expert; some block has exactly 4. `segments`: documents are numbered from 0 within each sequence of 512 tokens and never fall along it; every sequence holds five.
All inputs are finite; a program needn't handle non-finite values.
Results may differ from the reference program's by a relative error of at most 0.023.
Values may be sent and summed in bfloat16 or wider, within the bound.
No kernel may reach another device: no remote copies, remote signals or barrier semaphores. Data moves between devices by JAX's collectives and lax.ppermute only.
A program may use at most 128 MiB of HBM per device.

```python
import math
import jax
import jax.numpy as jnp
import numpy as np
from jax import lax

D = 768
HEADS = 12
HEAD_DIM = 64
FF = 3072
EXPERTS = 64
BUCKETS = 32
REACH = 128
SEQ = 512
QUARTER = 128
CAPQ = 4
NSEQ = 64
TOKEN_TOTAL = 32768


def draw_segments(key, part):
    key = jax.random.fold_in(key, 11)
    keys = jax.random.split(key, 4)
    opening = jax.random.randint(keys[0], (NSEQ, 1), 1, SEQ // 16)
    begins = jax.random.randint(keys[1], (NSEQ, 1), SEQ // 16, SEQ // 8)
    closes = jax.random.randint(keys[2], (NSEQ, 1), 7 * SEQ // 8, 15 * SEQ // 16)
    ending = jax.random.randint(keys[3], (NSEQ, 1), 15 * SEQ // 16, SEQ)
    positions = jnp.arange(SEQ, dtype=jnp.int32)[None, :]
    total = (positions >= opening).astype(jnp.int32) + (positions >= begins).astype(jnp.int32)
    total = total + (positions >= closes).astype(jnp.int32) + (positions >= ending).astype(jnp.int32)
    return total.astype(jnp.int32)


def shard_levels(own_key, dims, cuts, least, high):
    level, own = 1.0, jax.random.fold_in(own_key, 6)
    for position, blocks in cuts:
        steps = jnp.exp(jax.random.uniform(jax.random.fold_in(own, position), (blocks,), jnp.float32, least / len(cuts), high / len(cuts)))
        level = level * jnp.repeat(steps, dims[position] // blocks).reshape([-1 if axis == position else 1 for axis in range(len(dims))])
    return level


def shared_out(rng, own, number, rows, number_of, top, reach, lean):
    sequence = jax.random.permutation(rng, number_of)
    crowded, common = portions_of(number_of, rows * top, reach, lean, True), portions_of(number_of, rows * top, reach, lean, False)
    places = jnp.arange(number_of)

    def named(tallies, rotation):
        used = int((tallies > 0).sum())
        fixed = max(1, used // 4)
        shifted = fixed + (places - fixed + rotation * (used - fixed)) % max(1, number_of - fixed)
        return jnp.zeros((number_of,), jnp.int32).at[sequence[jnp.where(places < fixed, places, shifted)]].set(jnp.asarray(tallies, jnp.int32))

    tallies = jnp.where(number % 4 == 0, named(crowded, number // 4), named(common, number - number // 4 - 1))
    mixed = jax.random.permutation(jax.random.fold_in(own, 3), number_of)
    giver, sink = mixed[0:number_of // 2 * 2:2], mixed[1:number_of // 2 * 2:2]
    slack = jnp.minimum(tallies[giver] - 1, reach - tallies[sink]) // 2
    slack = jnp.where((giver == sequence[0]) | (sink == sequence[0]) | (tallies[sink] == 0), 0, jnp.maximum(slack, 0))
    shifted = jax.random.randint(jax.random.fold_in(own, 4), (number_of // 2,), 0, 1 << 20) % (slack + 1)
    tallies = tallies.at[giver].add(-shifted).at[sink].add(shifted)
    members = jnp.searchsorted(jnp.cumsum(tallies), jnp.arange(rows * top), side="right").astype(jnp.int32)
    table = members.reshape(top, rows).T
    table = table[jax.random.permutation(jax.random.fold_in(own, 1), rows)]
    rotation = jax.random.randint(jax.random.fold_in(own, 2), (rows, 1), 0, top)
    return jnp.take_along_axis(table, (jnp.arange(top)[None, :] + rotation) % top, axis=1)


def portions_of(count, total, most, skew, full):
    weights = [(1 << 20) // math.isqrt(rank ** skew) + 1 for rank in range(1, count + 1)]
    largest = most if full else min(most, max(-(-total // count), total * weights[0] // sum(weights)))
    least = 1 if total - largest >= count - 1 else 0
    given, surplus = [largest] + [least] * (count - 1), total - largest - least * (count - 1)
    while surplus > 0:
        candidates = [i for i in range(1, count) if given[i] < largest] or [i for i in range(1, count) if given[i] < most]
        whole, budget = sum([weights[i] for i in candidates]), surplus
        for i in candidates:
            extra = min(most - given[i], max(1, budget * weights[i] // whole), surplus)
            given[i] = given[i] + extra
            surplus = surplus - extra
    return np.array(given)


def normal_values(key, shape, deviation, reach, cuts=(), held_as=jnp.bfloat16):
    values = jax.random.normal(key, shape, jnp.float32) * deviation
    if len(cuts) > 0:
        values = shard_levels(key, shape, cuts, -0.22, 0.18) * values
    return jnp.clip(values, min=-reach, max=reach).astype(held_as)


def setup_inputs(seed: int = 0) -> dict:
    arg_keys = jax.random.split(jax.random.key(seed), 13)
    inputs = normal_values(arg_keys[0], (NSEQ, SEQ, D), 1.0, 6.0, ((0, 32), (1, 4)), jnp.float32)
    projection_in = normal_values(arg_keys[1], (3, D, HEADS * HEAD_DIM), (D // 2) ** -0.5, 0.3125, ((1, 32), (2, 4)))
    projection_out = normal_values(arg_keys[2], (HEADS * HEAD_DIM, D), (D // 16) ** -0.5, 0.875, ((0, 4), (1, 32)))
    gain_attention = jnp.clip(1.0 + 0.1 * jax.random.normal(arg_keys[3], (D,), jnp.float32), 0.5, 1.5)
    gain_experts = jnp.clip(1.0 + 0.1 * jax.random.normal(arg_keys[4], (D,), jnp.float32), 0.5, 1.5)
    router_weight = normal_values(arg_keys[5], (D, EXPERTS), (2 * D) ** -0.5, 0.15625, (), jnp.float32)
    bias_table = normal_values(arg_keys[6], (BUCKETS, HEADS), 1.0, 3.0, (), jnp.float32)
    expert_in = normal_values(arg_keys[7], (EXPERTS, D, FF), D ** -0.5, 0.21875, ((0, 32), (2, 4)))
    expert_out = normal_values(arg_keys[8], (EXPERTS, FF, D), (100 / FF ** 0.5), 10.0, ((0, 32), (1, 4)))
    routes_keys = jax.random.split(jax.random.fold_in(arg_keys[9], 1), NSEQ * SEQ // QUARTER)
    routes_turns = jax.random.permutation(jax.random.fold_in(arg_keys[9], 3), NSEQ * SEQ // QUARTER)
    routes = jax.vmap(lambda own, number: shared_out(jax.random.fold_in(arg_keys[9], 2), own, number, QUARTER, EXPERTS, 1, CAPQ, 1))(routes_keys, routes_turns).reshape((NSEQ, SEQ, 1))
    segments = draw_segments(jax.random.fold_in(arg_keys[12], 71), 0)
    cotangent = normal_values(arg_keys[11], (NSEQ, SEQ, D), 1.0, 6.0, ((0, 32), (1, 4)), jnp.float32)
    return dict(inputs=inputs, projection_in=projection_in, projection_out=projection_out, gain_attention=gain_attention, gain_experts=gain_experts, router_weight=router_weight, bias_table=bias_table, expert_in=expert_in, expert_out=expert_out, routes=routes, segments=segments, cotangent=cotangent)


@jax.custom_vjp
def low(v):
    return lax.optimization_barrier(v.astype(jnp.bfloat16)).astype(jnp.float32)

@jax.custom_vjp
def low_back(v):
    return v

def low_keep(v):
    return (low(v), None)

def low_pass(kept, grad):
    return (grad,)

def back_keep(v):
    return (v, None)

def back_low(kept, grad):
    return (low(grad),)
low.defvjp(low_keep, low_pass)
low_back.defvjp(back_keep, back_low)
highest = lax.Precision.HIGHEST
epsilon = 1e-06

def bucket_grid(length):
    halfway = BUCKETS // 2
    exact_span = halfway // 2
    offsets = jnp.arange(length, dtype=jnp.int32)[None, :] - jnp.arange(length, dtype=jnp.int32)[:, None]
    distance = jnp.abs(offsets)
    far_part = jnp.full_like(distance, exact_span)
    for step in range(1, exact_span):
        cutoff_level = math.ceil(exact_span * (REACH / exact_span) ** (step / exact_span) - 1e-09)
        far_part = far_part + (distance >= cutoff_level).astype(jnp.int32)
    nearby = jnp.where(distance < exact_span, distance, far_part)
    return (nearby + jnp.where(offsets > 0, halfway, 0)).astype(jnp.int32)

def norm_rows(values, gain):
    return values * lax.rsqrt(lax.optimization_barrier(jnp.mean(values * values, axis=-1, keepdims=True)) + epsilon) * gain

def attend_group(query, key, value, segment, bias):
    scores = jnp.einsum('gqhd,gkhd->ghqk', query, key, precision=highest) * HEAD_DIM ** (-0.5) + bias[None]
    scores = low_back(scores)
    same = segment[:, None, :, None] == segment[:, None, None, :]
    scores = jnp.where(same, scores, -1000000000.0)
    weights = low(jax.nn.softmax(scores, axis=-1))
    return jnp.einsum('ghqk,gkhd->gqhd', weights, value, precision=highest)

def expert_block(slot_rows, weight_in, weight_out):
    pre_act = low_back(jnp.dot(slot_rows, weight_in, precision=highest))
    active = low(jax.nn.gelu(pre_act))
    return jnp.dot(active, weight_out, precision=highest)

def forward(params, routes, segments):
    inputs, projection_in, projection_out, gain_attention, gain_experts, router_weight, bias_table, expert_in, expert_out = params
    flat = inputs.reshape(TOKEN_TOTAL, D)
    normed = low(norm_rows(flat, gain_attention))
    projected = low(low_back(jnp.einsum('rd,tdc->trc', normed, projection_in, precision=highest)))
    group_size = math.gcd(NSEQ, 8)
    shaped = projected.reshape(3, NSEQ // group_size, group_size, SEQ, HEADS, HEAD_DIM)
    segment_groups = segments.reshape(NSEQ // group_size, group_size, SEQ)
    bias = jnp.transpose(bias_table[bucket_grid(SEQ)], (2, 0, 1))
    block_fn = jax.checkpoint(lambda pieces: attend_group(pieces[0], pieces[1], pieces[2], pieces[3], bias))
    attended = lax.map(block_fn, (shaped[0], shaped[1], shaped[2], segment_groups))
    attended = low(low_back(attended.reshape(TOKEN_TOTAL, HEADS * HEAD_DIM)))
    hidden = flat + low_back(jnp.dot(attended, projection_out, precision=highest))
    mixed_in = norm_rows(hidden, gain_experts)
    logits = jnp.dot(mixed_in, router_weight, precision=highest)
    route_weights = jax.nn.softmax(logits, axis=-1)
    chosen = routes.reshape(TOKEN_TOTAL).astype(jnp.int32)
    chosen_mask = chosen[:, None] == jnp.arange(EXPERTS, dtype=jnp.int32)[None, :]
    gate = lax.optimization_barrier(jnp.sum(jnp.where(chosen_mask, route_weights, 0.0), axis=-1))
    running = jnp.cumsum(chosen_mask.astype(jnp.int32).reshape(TOKEN_TOTAL // QUARTER, QUARTER, EXPERTS), axis=1).astype(jnp.int32)
    rank = lax.optimization_barrier(jnp.sum(jnp.where(chosen_mask.reshape(running.shape), running - 1, 0), axis=-1)).astype(jnp.int32).reshape(TOKEN_TOTAL)
    block = jnp.arange(TOKEN_TOTAL, dtype=jnp.int32) // QUARTER
    slot_count = TOKEN_TOTAL // QUARTER * CAPQ
    place = (chosen * slot_count + block * CAPQ + rank).astype(jnp.int32)
    sent = low_back(low(mixed_in))
    buffer = jnp.zeros((EXPERTS * slot_count, D), jnp.float32).at[place].set(sent)
    expert_fn = jax.checkpoint(lambda pieces: expert_block(pieces[0], pieces[1], pieces[2]))
    results = lax.map(expert_fn, (buffer.reshape(EXPERTS, slot_count, D), expert_in, expert_out))
    expert_back = low(low_back(results.reshape(EXPERTS * slot_count, D)[place]))
    return (hidden + gate[:, None] * expert_back).reshape(NSEQ, SEQ, D)

def reference(inputs, projection_in, projection_out, gain_attention, gain_experts, router_weight, bias_table, expert_in, expert_out, routes, segments, cotangent):
    params = (inputs, projection_in.astype(jnp.float32), projection_out.astype(jnp.float32), gain_attention, gain_experts, router_weight, bias_table, expert_in.astype(jnp.float32), expert_out.astype(jnp.float32))
    result, pullback = jax.vjp(lambda values: forward(values, routes, segments), params)
    grads = pullback(cotangent)[0]
    return (result, grads[0], grads[1], grads[2], grads[3], grads[4], grads[5], grads[6], grads[7], grads[8])
```

```python
import functools
import math

import jax
import jax.numpy as jnp
from jax import lax
from jax.experimental import pallas as pl
from jax.experimental.pallas import tpu as pltpu
from jax.sharding import Mesh
from jax.sharding import PartitionSpec as P

HEADS = 12
HEAD_DIM = 64
EXPERTS = 64
BUCKETS = 32
REACH = 128
EXPERT = ("expert_0", "expert_1", "expert_2")
QUARTER = 128
PARTS = 4
WIDTH = 768
CHANNELS = 192
LOCAL_HEADS = CHANNELS // HEAD_DIM
QKV = 3 * CHANNELS
CAPACITY = 4
SLOTS = 512
HALF_SLOTS = SLOTS // 2
TAGGED = WIDTH + 128
TILE_STEPS = (0, 1, -1, 2, -2)

epsilon = 1e-06
f32 = jnp.float32
bf16 = jnp.bfloat16
VMEM_LIMIT = 56 * 1024 * 1024


def dot(a, b, ca=1, cb=0, precision=None):
    return lax.dot_general(
        a, b, (((ca,), (cb,)), ((), ())), preferred_element_type=f32, precision=precision
    )


def struct(shape, dtype):
    return jax.ShapeDtypeStruct(shape, dtype)


SMEM = pl.BlockSpec(memory_space=pltpu.SMEM)
VMEM = pl.BlockSpec(memory_space=pltpu.VMEM)


def call(kernel, outs, ins, in_specs=None, scratch=(), flops=10**8, moved=4 * 10**6, name=None):
    return pl.pallas_call(
        kernel,
        grid=(1,),
        out_shape=outs,
        in_specs=in_specs or [VMEM] * len(ins),
        out_specs=jax.tree.map(lambda _: VMEM, outs),
        scratch_shapes=scratch,
        cost_estimate=pl.CostEstimate(flops=flops, bytes_accessed=moved, transcendentals=0),
        compiler_params=pltpu.CompilerParams(vmem_limit_bytes=VMEM_LIMIT),
        name=name,
    )(*ins)


def shift(x, step):
    return lax.ppermute(x, "mp", [(i, (i + step) % PARTS) for i in range(PARTS)])


def gather4(x, way):
    left, right = shift(x, 1), shift(x, -1)
    far = shift(left, 1) if way > 0 else shift(right, -1)
    return x, right, far, left


def added(*terms):
    return functools.reduce(lambda a, b: a + b, [t.astype(f32) for t in terms])


def reduce4(pieces, way):
    own, right, far, left = pieces
    if way > 0:
        right = added(right, shift(far, 1)).astype(bf16)
    else:
        left = added(left, shift(far, -1)).astype(bf16)
    return own, shift(right, 1), shift(left, -1)


def to_experts(x):
    pieces = x.reshape(32, -1, x.shape[-1])
    return lax.all_to_all(pieces, EXPERT, 0, 0, tiled=True).reshape(x.shape)


def sent_to_all(x, axis):
    peers = lax.axis_size(axis)
    return lax.all_to_all(jnp.broadcast_to(x[None], (peers, *x.shape)), axis, 0, 0, tiled=True)


def cut_along(x, dim, peers):
    lengths = x.shape
    pieces = x.reshape(*lengths[:dim], peers, lengths[dim] // peers, *lengths[dim + 1 :])
    return jnp.moveaxis(pieces, dim, 0)


def sum_at_owner(x, axis, dim):
    pieces = cut_along(x, dim, lax.axis_size(axis))
    arrived = lax.all_to_all(pieces, axis, split_axis=0, concat_axis=0, tiled=True)
    return arrived.sum(axis=0)


def in_order(pieces, dim):
    lengths = list(pieces.shape[1:])
    lengths[dim] *= pieces.shape[0]
    return jnp.moveaxis(pieces, 0, dim).reshape(lengths)


def rows_for(lines, peers):
    spare = -lines.shape[0] % peers
    if not spare:
        return lines
    return jnp.concatenate([lines, jnp.zeros((spare, *lines.shape[1:]), lines.dtype)])


def gather_axes(x, axes, dim):
    far, near = axes
    pieces = sent_to_all(sent_to_all(x, far), near)
    return in_order(pieces.swapaxes(0, 1).reshape(-1, *x.shape), dim)


def summed_rows(x, axes, dim):
    far, near = axes
    pieces = cut_along(x, dim, lax.axis_size(far))
    nearer = sum_at_owner(pieces, near, dim + 1)
    arrived = lax.all_to_all(nearer, far, split_axis=0, concat_axis=0, tiled=True)
    return arrived.sum(axis=0)


def sum_by_parts(x, axes):
    padded = rows_for(x, lax.axis_size(axes[0]) * lax.axis_size(axes[1]))
    whole = gather_axes(summed_rows(padded, axes, 0), axes, 0)
    return lax.slice_in_dim(whole, 0, len(x)).reshape(x.shape)


def bucket_of(offsets):
    halfway = BUCKETS // 2
    exact_span = halfway // 2
    distance = jnp.abs(offsets)
    far_part = jnp.full_like(distance, exact_span)
    for step in range(1, exact_span):
        cutoff_level = math.ceil(exact_span * (REACH / exact_span) ** (step / exact_span) - 1e-09)
        far_part = far_part + jnp.where(distance >= cutoff_level, 1, 0)
    nearby = jnp.where(distance < exact_span, distance, far_part)
    return nearby + jnp.where(offsets > 0, halfway, 0)


def tile_buckets(step):
    shape = (QUARTER, QUARTER)
    offsets = (
        step * QUARTER
        + lax.broadcasted_iota(jnp.int32, shape, 1)
        - lax.broadcasted_iota(jnp.int32, shape, 0)
    )
    return bucket_of(offsets)


def possible(step):
    if step == 0:
        return range(BUCKETS)
    if step == 1:
        return range(BUCKETS // 2 + 1, BUCKETS)
    if step == -1:
        return range(1, BUCKETS // 2)
    return (BUCKETS - 1,) if step > 0 else (BUCKETS // 2 - 1,)


def tile_at(row_block, key_block):
    step = key_block - row_block
    return TILE_STEPS.index(max(-2, min(2, step)))


def bias_kernel(head_ref, table_ref, out_ref):
    head = head_ref[0]
    for t, step in enumerate(TILE_STEPS):
        buckets = tile_buckets(step)
        tiles = [jnp.zeros((QUARTER, QUARTER), f32)] * LOCAL_HEADS
        for b in possible(step):
            mask = buckets == b
            tiles = [jnp.where(mask, table_ref[b, head + h], tile) for h, tile in enumerate(tiles)]
        for h, tile in enumerate(tiles):
            out_ref[h, t] = tile


def inverse_size(values):
    return lax.rsqrt(jnp.mean(values * values, axis=-1, keepdims=True) + epsilon)


def as_column(row):
    return jnp.transpose(jnp.broadcast_to(row, (QUARTER, QUARTER)))


def start_kernel(x_ref, gain_ref, seg_ref, route_ref, cot_ref, n0, n1, place_ref, c0, c1):
    gain = gain_ref[...]
    tri = (
        lax.broadcasted_iota(jnp.int32, (QUARTER, QUARTER), 0)
        >= lax.broadcasted_iota(jnp.int32, (QUARTER, QUARTER), 1)
    ).astype(bf16)
    for s, out in ((0, n0), (1, n1)):
        x = x_ref[s]
        out[:, :WIDTH] = (x * inverse_size(x) * gain).astype(bf16)
        out[:, WIDTH:] = as_column(seg_ref[s : s + 1].astype(f32)).astype(bf16)
        chosen = as_column(route_ref[s : s + 1].astype(f32)).astype(jnp.int32)
        mask = jnp.where(
            chosen == lax.broadcasted_iota(jnp.int32, (QUARTER, QUARTER), 1), 1.0, 0.0
        )
        running = dot(tri, mask.astype(bf16))
        rank = jnp.sum(mask * running, axis=-1, keepdims=True).astype(jnp.int32) - 1
        column = chosen[:, :1]
        place = (column & 1) * HALF_SLOTS + (column >> 1) * 8 + s * CAPACITY + rank
        slots = lax.broadcasted_iota(jnp.int32, (QUARTER, SLOTS), 1)
        place_ref[s * QUARTER : (s + 1) * QUARTER] = jnp.where(slots == place, 1.0, 0.0).astype(bf16)
    upstream = cot_ref[...].astype(bf16)
    c0[...] = dot(place_ref[:, :HALF_SLOTS], upstream, 0, 0).astype(bf16)
    c1[...] = dot(place_ref[:, HALF_SLOTS:], upstream, 0, 0).astype(bf16)


def position(me, k):
    return pl.multiple_of(lax.rem(me + k, PARTS) * QUARTER, QUARTER)


def same_document(g_ref):
    column = g_ref[:, WIDTH:].astype(f32)
    return column, jnp.transpose(column)[:1]


def bias_row(tiles_ref, h, i):
    return jnp.concatenate([tiles_ref[h, tile_at(i, j)] for j in range(PARTS)], axis=1)


def attend_kernel(
    me_ref, a0, a1, a2, a3, w_ref, tiles_ref, g_ref, qkv_ref, att_ref, lse_ref, p0, p1, p2, p3
):
    me = me_ref[0]
    for k, piece in enumerate((a0, a1, a2, a3)):
        g_ref[pl.ds(position(me, k), QUARTER), :] = piece[...]
    qkv_ref[...] = dot(g_ref[:, :WIDTH], w_ref[:, :QKV]).astype(bf16)
    column, row = same_document(g_ref)
    lse_ref[...] = jnp.zeros_like(lse_ref)
    for h in range(LOCAL_HEADS):
        lo = h * HEAD_DIM
        key = qkv_ref[:, CHANNELS + lo : CHANNELS + lo + HEAD_DIM]
        value = qkv_ref[:, 2 * CHANNELS + lo : 2 * CHANNELS + lo + HEAD_DIM]
        for i in range(PARTS):
            rows = slice(i * QUARTER, (i + 1) * QUARTER)
            query = qkv_ref[rows, lo : lo + HEAD_DIM] * HEAD_DIM ** (-0.5)
            scores = dot(query, key, 1, 1) + bias_row(tiles_ref, h, i)
            scores = jnp.where(column[rows, :1] == row, scores, -1000000000.0)
            row_max = jnp.max(scores, axis=-1, keepdims=True)
            expos = jnp.exp(scores - row_max)
            total = jnp.sum(expos, axis=-1, keepdims=True)
            weights = (expos * (1.0 / total)).astype(bf16)
            att_ref[rows, lo : lo + HEAD_DIM] = dot(weights, value).astype(bf16)
            lse_ref[rows, h : h + 1] = row_max + jnp.log(total)
    for k, out in enumerate((p0, p1, p2, p3)):
        mine = att_ref[pl.ds(position(me, k), QUARTER), :]
        out[...] = dot(mine, w_ref[:, QKV:], 1, 1).astype(bf16)


def dispatch_kernel(
    x_ref, t00, t01, t02, t10, t11, t12, gain_ref, router_ref, route_ref, place_ref,
    hidden_ref, gate_ref, s0, s1,
):
    for s, terms in ((0, (t00, t01, t02)), (1, (t10, t11, t12))):
        rows = slice(s * QUARTER, (s + 1) * QUARTER)
        hidden_ref[rows] = x_ref[s] + added(*[t[...] for t in terms])
    hidden = hidden_ref[...]
    mixed = hidden * inverse_size(hidden) * gain_ref[...]
    low = mixed.astype(bf16)
    s0[...] = dot(place_ref[:, :HALF_SLOTS], low, 0, 0).astype(bf16)
    s1[...] = dot(place_ref[:, HALF_SLOTS:], low, 0, 0).astype(bf16)
    logits = dot(mixed, router_ref[...], precision=lax.Precision.HIGHEST)
    expos = jnp.exp(logits - jnp.max(logits, axis=-1, keepdims=True))
    shares = expos / jnp.sum(expos, axis=-1, keepdims=True)
    for s in range(2):
        rows = slice(s * QUARTER, (s + 1) * QUARTER)
        chosen = as_column(route_ref[s : s + 1].astype(f32)).astype(jnp.int32)[:, :EXPERTS]
        mask = chosen == lax.broadcasted_iota(jnp.int32, (QUARTER, EXPERTS), 1)
        gate = jnp.sum(jnp.where(mask, shares[rows], 0.0), axis=-1, keepdims=True)
        gate_ref[rows] = jnp.broadcast_to(gate, (QUARTER, 128))


def upstream_kernel(c0, c1, c2, c3, w_ref, u_ref):
    for k, c in enumerate((c0, c1, c2, c3)):
        u_ref[k] = dot(c[...], w_ref[0], 1, 1).astype(bf16)


def expert_kernel(
    own_ref, x0, x1, x2, x3, u_ref, w_ref, router_ref,
    active_ref, scaled_ref, grad_ref, logit_ref, s0, s1, s2, s3,
):
    own = own_ref[0]
    router = router_ref[...]
    router_hi = router.astype(bf16)
    router_lo = (router - router_hi.astype(f32)).astype(bf16)
    logit_ref[...] = jnp.zeros_like(logit_ref)
    c = math.sqrt(2.0 / math.pi)
    ca = c * 0.044715
    for k, (x_ref, out) in ((2, (x2, s2)), (1, (x1, s1)), (3, (x3, s3)), (0, (x0, s0))):
        for part in range(2):
            rows = slice(part * 128, (part + 1) * 128)
            x = x_ref[rows, :]
            logits = dot(x, router_hi) + dot(x, router_lo)
            expos = jnp.exp(logits - jnp.max(logits, axis=-1, keepdims=True))
            shares = expos / jnp.sum(expos, axis=-1, keepdims=True)
            chosen = jnp.where(
                lax.broadcasted_iota(jnp.int32, shares.shape, 1) == own, 1.0, 0.0
            )
            gate = jnp.sum(shares * chosen, axis=-1, keepdims=True)
            pre = dot(x, w_ref[0])
            u = u_ref[k, rows, :].astype(f32)
            square = pre * pre
            t = jnp.tanh(pre * (c + ca * square))
            half = 0.5 + 0.5 * t
            active = pre * half
            slope = half + (0.5 * pre) * (1.0 - t * t) * (c + 3.0 * ca * square)
            gate_grad = jnp.sum(active * u, axis=-1, keepdims=True)
            active_ref[k, rows, :] = active.astype(bf16)
            scaled_ref[k, rows, :] = (gate * active).astype(bf16)
            pre_grad = (gate * u * slope).astype(bf16)
            grad_ref[k, rows, :] = pre_grad
            logit_grad = shares * (chosen - gate) * gate_grad
            logit_hi = logit_grad.astype(bf16)
            logit_lo = (logit_grad - logit_hi.astype(f32)).astype(bf16)
            out[rows, :] = (
                dot(pre_grad, w_ref[0], 1, 1) + dot(logit_hi, router_hi, 1, 1)
            ).astype(bf16)
            logit_ref[...] += dot(x, logit_hi, 0, 0) + dot(x, logit_lo, 0, 0)


def output_kernel(active_ref, w_ref, s0, s1, s2, s3):
    for k, out in ((2, s2), (1, s1), (3, s3), (0, s0)):
        out[...] = dot(active_ref[k], w_ref[0]).astype(bf16)


def weights_kernel(scaled_ref, grad_ref, c0, c1, c2, c3, x0, x1, x2, x3, *rest):
    out_ref, in_ref = rest[-2:]
    for k, (c, x) in enumerate(zip((c0, c1, c2, c3), (x0, x1, x2, x3))):
        out_term = dot(scaled_ref[k], c[...], 0, 0)
        in_term = dot(x[...], grad_ref[k], 0, 0)
        if k == 0:
            out_ref[0] = out_term
            in_ref[0] = in_term
        else:
            out_ref[0] += out_term
            in_ref[0] += in_term


def back_kernel(r0, r1, place_ref, hidden_ref, cot_ref, gain_ref, grad_ref, h0, h1, gain_grad_ref):
    mixed_grad = dot(place_ref[:, :HALF_SLOTS], r0[...]) + dot(place_ref[:, HALF_SLOTS:], r1[...])
    hidden = hidden_ref[...]
    r = inverse_size(hidden)
    gain_grad_ref[...] = jnp.sum(mixed_grad * hidden * r, axis=0, keepdims=True)
    u = gain_ref[...] * mixed_grad
    grad = cot_ref[...] + r * u - hidden * (r * r * r * jnp.mean(hidden * u, axis=-1, keepdims=True))
    grad_ref[...] = grad
    h0[...] = grad[:QUARTER].astype(bf16)
    h1[...] = grad[QUARTER:].astype(bf16)


def result_kernel(r0, r1, place_ref, hidden_ref, gate_ref, out_ref):
    back = dot(place_ref[:, :HALF_SLOTS], r0[...]) + dot(place_ref[:, HALF_SLOTS:], r1[...])
    out_ref[...] = hidden_ref[...] + gate_ref[:, :1] * back


def attend_back_kernel(
    me_ref, a0, a1, a2, a3, w_ref, tiles_ref, g_ref, qkv_ref, lse_ref,
    up_ref, dqkv_ref, sums_ref, gain_ref, p0, p1, p2, p3, tile_sums,
):
    me = me_ref[0]
    for k, piece in enumerate((a0, a1, a2, a3)):
        up_ref[pl.ds(position(me, k), QUARTER), :] = piece[...]
    att_grad = dot(up_ref[...], w_ref[:, QKV:]).astype(bf16)
    column, row = same_document(g_ref)
    tile_sums[...] = jnp.zeros_like(tile_sums)
    for h in range(LOCAL_HEADS):
        lo = h * HEAD_DIM
        key = qkv_ref[:, CHANNELS + lo : CHANNELS + lo + HEAD_DIM]
        value = qkv_ref[:, 2 * CHANNELS + lo : 2 * CHANNELS + lo + HEAD_DIM]
        key_grad = jnp.zeros((HEAD_DIM, PARTS * QUARTER), f32)
        value_grad = jnp.zeros((HEAD_DIM, PARTS * QUARTER), f32)
        for i in range(PARTS):
            rows = slice(i * QUARTER, (i + 1) * QUARTER)
            query = qkv_ref[rows, lo : lo + HEAD_DIM] * HEAD_DIM ** (-0.5)
            scores = dot(query, key, 1, 1) + bias_row(tiles_ref, h, i)
            scores = jnp.where(column[rows, :1] == row, scores, -1000000000.0)
            weights = jnp.exp(scores - lse_ref[rows, h : h + 1])
            out_grad = att_grad[rows, lo : lo + HEAD_DIM]
            weights_grad = dot(out_grad, value, 1, 1)
            inner = jnp.sum(weights * weights_grad, axis=-1, keepdims=True)
            score_grad = (weights * (weights_grad - inner)).astype(bf16)
            wide = score_grad.astype(f32)
            for j in range(PARTS):
                tile_sums[h, tile_at(i, j)] += wide[:, j * QUARTER : (j + 1) * QUARTER]
            dqkv_ref[rows, lo : lo + HEAD_DIM] = (
                dot(score_grad, key) * HEAD_DIM ** (-0.5)
            ).astype(bf16)
            key_grad += dot(query, score_grad, 0, 0)
            value_grad += dot(out_grad, weights.astype(bf16), 0, 0)
        dqkv_ref[:, CHANNELS + lo : CHANNELS + lo + HEAD_DIM] = jnp.transpose(key_grad).astype(bf16)
        dqkv_ref[:, 2 * CHANNELS + lo : 2 * CHANNELS + lo + HEAD_DIM] = jnp.transpose(
            value_grad
        ).astype(bf16)
    gain = jnp.zeros((1, WIDTH), f32)
    for k, out in ((2, p2), (1, p1), (3, p3), (0, p0)):
        at = pl.ds(position(me, k), QUARTER)
        normed_grad = dot(dqkv_ref[at, :], w_ref[:, :QKV], 1, 1)
        out[...] = normed_grad.astype(bf16)
        gain += jnp.sum(normed_grad * g_ref[at, :WIDTH].astype(f32), axis=0, keepdims=True)
    gain_ref[...] = gain
    sums_ref[...] = jnp.zeros_like(sums_ref)
    for t, step in enumerate(TILE_STEPS):
        buckets = tile_buckets(step)
        for b in possible(step):
            mask = buckets == b
            for h in range(LOCAL_HEADS):
                sums_ref[h, b : b + 1] += jnp.sum(
                    jnp.where(mask, tile_sums[h, t], 0.0), axis=0, keepdims=True
                )


def projection_kernel(g0, g1, d0, d1, u0, u1, a0, a1, out_ref):
    out_ref[:, :QKV] = (
        dot(g0[:, :WIDTH], d0[...], 0, 0) + dot(g1[:, :WIDTH], d1[...], 0, 0)
    ).astype(bf16)
    out_ref[:, QKV:] = (dot(u0[...], a0[...], 0, 0) + dot(u1[...], a1[...], 0, 0)).astype(bf16)


def input_kernel(x_ref, gain_ref, grad_ref, t00, t01, t02, t10, t11, t12, out_ref):
    for s, terms in ((0, (t00, t01, t02)), (1, (t10, t11, t12))):
        x = x_ref[s]
        r = inverse_size(x)
        u = gain_ref[...] * added(*[t[...] for t in terms])
        out_ref[s] = (
            grad_ref[s * QUARTER : (s + 1) * QUARTER]
            + r * u
            - x * (r * r * r * jnp.mean(x * u, axis=-1, keepdims=True))
        )


def expert_spec(e):
    return pl.BlockSpec((1, WIDTH, WIDTH), lambda i: (e, 0, 0))


def body(
    inputs,
    projection_in,
    projection_out,
    gain_attention,
    gain_experts,
    router_weight,
    bias_table,
    expert_in,
    expert_out,
    routes,
    segments,
    cotangent,
):
    seq_here, quarter, width = inputs.shape
    rows = seq_here * quarter
    me = lax.axis_index("mp").reshape(1).astype(jnp.int32)
    first_head = me * LOCAL_HEADS
    gain1, gain2 = gain_attention.reshape(1, width), gain_experts.reshape(1, width)
    routes = routes.reshape(seq_here, quarter)
    upstream = cotangent.reshape(rows, width)
    piece = struct((QUARTER, WIDTH), bf16)
    slot_piece = struct((HALF_SLOTS, WIDTH), bf16)

    turned = jnp.concatenate(
        [jnp.moveaxis(projection_in, 1, 0).reshape(24, QKV), projection_out.T], axis=1
    )
    weights = sent_to_all(turned, EXPERT).reshape(WIDTH, QKV + CHANNELS)

    tagged = struct((QUARTER, TAGGED), bf16)
    n0, n1, place, c0, c1 = call(
        start_kernel,
        (tagged, tagged, struct((rows, SLOTS), bf16), slot_piece, slot_piece),
        (inputs, gain1, segments, routes, upstream),
        name="start",
    )
    normed = (gather4(n0, 1), gather4(n1, -1))
    tiles = call(
        bias_kernel,
        struct((LOCAL_HEADS, len(TILE_STEPS), QUARTER, QUARTER), f32),
        (first_head, bias_table),
        [SMEM, SMEM],
        name="bias",
    )
    length = PARTS * QUARTER
    attended = [
        call(
            attend_kernel,
            (
                struct((length, TAGGED), bf16),
                struct((length, QKV), bf16),
                struct((length, CHANNELS), bf16),
                struct((length, 128), f32),
                piece, piece, piece, piece,
            ),
            (me, *normed[s], weights, tiles),
            [SMEM] + [VMEM] * 6,
            flops=2 * 10**9,
            name="attend",
        )
        for s in range(2)
    ]
    attention = [reduce4(attended[s][4:], (1, -1)[s]) for s in range(2)]

    c_all = [gather4(to_experts(c), (1, -1)[e]) for e, c in enumerate((c0, c1))]
    u = [
        call(
            upstream_kernel,
            struct((PARTS, HALF_SLOTS, WIDTH), bf16),
            (*c_all[e], expert_out),
            [VMEM] * 4 + [expert_spec(e)],
            flops=12 * 10**8,
            name="upstream",
        )
        for e in range(2)
    ]

    hidden, gate, s0, s1 = call(
        dispatch_kernel,
        (struct((rows, width), f32), struct((rows, 128), f32), slot_piece, slot_piece),
        (inputs, *attention[0], *attention[1], gain2, router_weight, routes, place),
        name="dispatch",
    )
    x_all = [gather4(to_experts(x), (1, -1)[e]) for e, x in enumerate((s0, s1))]
    group = lax.axis_index(EXPERT).astype(jnp.int32)
    acts = struct((PARTS, HALF_SLOTS, WIDTH), bf16)
    worked = [
        call(
            expert_kernel,
            (acts, acts, acts, struct((WIDTH, EXPERTS), f32)) + (slot_piece,) * 4,
            ((group * 2 + e).reshape(1), *x_all[e], u[e], expert_in, router_weight),
            [SMEM] + [VMEM] * 5 + [expert_spec(e), VMEM],
            flops=24 * 10**8,
            moved=2 * 10**7,
            name="expert",
        )
        for e in range(2)
    ]
    returned = [
        to_experts(added(*reduce4(worked[e][4:], (1, -1)[e])).astype(bf16)) for e in range(2)
    ]
    hidden_grad, h0, h1, gain2_grad = call(
        back_kernel,
        (struct((rows, width), f32), piece, piece, struct((1, width), f32)),
        (*returned, place, hidden, upstream, gain2),
        name="back",
    )
    grads = (gather4(h0, 1), gather4(h1, -1))
    attended_back = [
        call(
            attend_back_kernel,
            (
                struct((length, width), bf16),
                struct((length, QKV), bf16),
                struct((LOCAL_HEADS, BUCKETS, 128), f32),
                struct((1, width), f32),
                piece, piece, piece, piece,
            ),
            (me, *grads[s], weights, tiles, *attended[s][:2], attended[s][3]),
            [SMEM] + [VMEM] * 9,
            scratch=[pltpu.VMEM((LOCAL_HEADS, len(TILE_STEPS), QUARTER, QUARTER), f32)],
            flops=4 * 10**9,
            name="attend_back",
        )
        for s in range(2)
    ]
    normed_grad = [reduce4(attended_back[s][4:], (1, -1)[s]) for s in range(2)]
    input_grad = call(
        input_kernel,
        struct(inputs.shape, f32),
        (inputs, gain1, hidden_grad, *normed_grad[0], *normed_grad[1]),
        name="input_gradient",
    )

    outputs = [
        call(
            output_kernel,
            (slot_piece,) * 4,
            (worked[e][0], expert_out),
            [VMEM, expert_spec(e)],
            flops=12 * 10**8,
            name="expert_output",
        )
        for e in range(2)
    ]
    output_back = [
        to_experts(added(*reduce4(outputs[e], (1, -1)[e])).astype(bf16)) for e in range(2)
    ]
    result = call(
        result_kernel,
        struct((rows, width), f32),
        (*output_back, place, hidden, gate),
        name="result",
    )
    whole = struct((2, WIDTH, WIDTH), f32)
    expert_grads = None
    for e in range(2):
        ins = (worked[e][1], worked[e][2], *c_all[e], *x_all[e])
        earlier = () if expert_grads is None else expert_grads
        expert_grads = pl.pallas_call(
            weights_kernel,
            grid=(1,),
            out_shape=(whole, whole),
            in_specs=[VMEM] * 10 + [pl.BlockSpec(memory_space=pl.ANY)] * len(earlier),
            out_specs=(expert_spec(e), expert_spec(e)),
            input_output_aliases={10: 0, 11: 1} if earlier else {},
            cost_estimate=pl.CostEstimate(
                flops=24 * 10**8, bytes_accessed=2 * 10**7, transcendentals=0
            ),
            compiler_params=pltpu.CompilerParams(vmem_limit_bytes=VMEM_LIMIT),
            name="expert_weights",
        )(*ins, *earlier)
    grad_expert_out, grad_expert_in = expert_grads

    partial = call(
        projection_kernel,
        struct((WIDTH, QKV + CHANNELS), bf16),
        (
            attended[0][0], attended[1][0], attended_back[0][1], attended_back[1][1],
            attended_back[0][0], attended_back[1][0], attended[0][2], attended[1][2],
        ),
        flops=16 * 10**8,
        name="projection_gradient",
    )
    arrived = lax.all_to_all(partial.reshape(32, 24, WIDTH), EXPERT, 0, 0, tiled=True)
    projections = jnp.sum(arrived.astype(f32), axis=0)
    grad_projection_in = jnp.moveaxis(projections[:, :QKV].reshape(24, 3, CHANNELS), 1, 0)
    grad_projection_out = projections[:, QKV:].T

    early = jnp.concatenate(
        [(worked[0][3] + worked[1][3]).reshape(-1), gain2_grad.reshape(-1)]
    )
    early = sum_by_parts(early, (("expert_0", "expert_1"), ("expert_2", "mp")))
    grad_router = early[: WIDTH * EXPERTS].reshape(WIDTH, EXPERTS)
    grad_gain_experts = early[WIDTH * EXPERTS :]
    table_local = jnp.sum(attended_back[0][2] + attended_back[1][2], axis=-1).T
    table = lax.dynamic_update_slice(
        jnp.zeros((BUCKETS, HEADS), f32), table_local, (0, first_head[0])
    )
    gain1_grad = (attended_back[0][3] + attended_back[1][3]) / gain1
    late = jnp.concatenate([gain1_grad.reshape(-1), table.reshape(-1)]).reshape(9, 128)
    late = jnp.sum(sent_to_all(late, "mp"), axis=0)
    late = jnp.sum(sent_to_all(late, EXPERT), axis=0).reshape(-1)
    grad_gain_attention = late[:WIDTH]
    grad_table = late[WIDTH:].reshape(BUCKETS, HEADS)
    return (
        result.reshape(seq_here, quarter, width),
        input_grad,
        grad_projection_in,
        grad_projection_out,
        grad_gain_attention,
        grad_gain_experts,
        grad_router,
        grad_table,
        grad_expert_in,
        grad_expert_out,
    )


def solution(mesh):
    split = Mesh(
        mesh.devices.reshape(4, 4, 2, mesh.shape["mp"]), ("expert_0", "expert_1", "expert_2", "mp")
    )
    in_specs = (
        P(EXPERT, "mp", None),
        P(None, EXPERT, "mp"),
        P("mp", EXPERT),
        P(),
        P(),
        P(),
        P(),
        P(EXPERT, None, "mp"),
        P(EXPERT, "mp", None),
        P(EXPERT, "mp", None),
        P(EXPERT, "mp"),
        P(EXPERT, "mp", None),
    )
    out_specs = (
        P(EXPERT, "mp", None),
        P(EXPERT, "mp", None),
        P(None, EXPERT, "mp"),
        P("mp", EXPERT),
        P(),
        P(),
        P(),
        P(),
        P(EXPERT, None, "mp"),
        P(EXPERT, "mp", None),
    )
    return jax.shard_map(body, mesh=split, in_specs=in_specs, out_specs=out_specs, check_vma=False)
```

```python
import functools
import math

import jax
import jax.numpy as jnp
from jax import lax
from jax.experimental import pallas as pl
from jax.experimental.pallas import tpu as pltpu
from jax.sharding import Mesh
from jax.sharding import PartitionSpec as P

HEADS = 12
HEAD_DIM = 64
EXPERTS = 64
BUCKETS = 32
REACH = 128
EXPERT = ("expert_0", "expert_1", "expert_2")
QUARTER = 128
PARTS = 4
WIDTH = 768
CHANNELS = 192
LOCAL_HEADS = CHANNELS // HEAD_DIM
QKV = 3 * CHANNELS
CAPACITY = 4
SLOTS = 512
HALF_SLOTS = SLOTS // 2
TAGGED = WIDTH + 128
TILE_STEPS = (0, 1, -1, 2, -2)

epsilon = 1e-06
f32 = jnp.float32
bf16 = jnp.bfloat16
BLOCK = 512
VMEM_LIMIT = 56 * 1024 * 1024


def dot(a, b, ca=1, cb=0, precision=None):
    return lax.dot_general(
        a, b, (((ca,), (cb,)), ((), ())), preferred_element_type=f32, precision=precision
    )


def struct(shape, dtype):
    return jax.ShapeDtypeStruct(shape, dtype)


SMEM = pl.BlockSpec(memory_space=pltpu.SMEM)
VMEM = pl.BlockSpec(memory_space=pltpu.VMEM)


def call(kernel, outs, ins, in_specs=None, scratch=(), flops=10**8, moved=4 * 10**6, name=None):
    return pl.pallas_call(
        kernel,
        grid=(1,),
        out_shape=outs,
        in_specs=in_specs or [VMEM] * len(ins),
        out_specs=jax.tree.map(lambda _: VMEM, outs),
        scratch_shapes=scratch,
        cost_estimate=pl.CostEstimate(flops=flops, bytes_accessed=moved, transcendentals=0),
        compiler_params=pltpu.CompilerParams(vmem_limit_bytes=VMEM_LIMIT),
        name=name,
    )(*ins)


def shift(x, step):
    return lax.ppermute(x, "mp", [(i, (i + step) % PARTS) for i in range(PARTS)])


def gather4(x, way):
    left, right = shift(x, 1), shift(x, -1)
    far = shift(left, 1) if way > 0 else shift(right, -1)
    return x, right, far, left


def added(*terms):
    return functools.reduce(lambda a, b: a + b, [t.astype(f32) for t in terms])


def reduce4(pieces, way):
    own, right, far, left = pieces
    if way > 0:
        right = added(right, shift(far, 1)).astype(bf16)
    else:
        left = added(left, shift(far, -1)).astype(bf16)
    return own, shift(right, 1), shift(left, -1)


def after(x, *others):
    return lax.optimization_barrier((x, *others))[0]


def to_experts(x):
    return lax.all_to_all(x.reshape(32, -1, x.shape[-1]), EXPERT, 0, 0, tiled=True)


def by_expert(slots):
    return tuple(slots[:, 8 * e : 8 * e + 8, :WIDTH].reshape(HALF_SLOTS, WIDTH) for e in range(2))


def summed_slots(terms):
    pieces = [added(*terms[e]).astype(bf16).reshape(32, 8, WIDTH) for e in range(2)]
    return jnp.concatenate(pieces, axis=1)


def sent_to_all(x, axis):
    peers = lax.axis_size(axis)
    return lax.all_to_all(jnp.broadcast_to(x[None], (peers, *x.shape)), axis, 0, 0, tiled=True)


def bucket_of(offsets):
    halfway = BUCKETS // 2
    exact_span = halfway // 2
    distance = jnp.abs(offsets)
    far_part = jnp.full_like(distance, exact_span)
    for step in range(1, exact_span):
        cutoff_level = math.ceil(exact_span * (REACH / exact_span) ** (step / exact_span) - 1e-09)
        far_part = far_part + jnp.where(distance >= cutoff_level, 1, 0)
    nearby = jnp.where(distance < exact_span, distance, far_part)
    return nearby + jnp.where(offsets > 0, halfway, 0)


def tile_buckets(step):
    shape = (QUARTER, QUARTER)
    offsets = (
        step * QUARTER
        + lax.broadcasted_iota(jnp.int32, shape, 1)
        - lax.broadcasted_iota(jnp.int32, shape, 0)
    )
    return bucket_of(offsets)


def possible(step):
    if step == 0:
        return range(BUCKETS)
    if step == 1:
        return range(BUCKETS // 2 + 1, BUCKETS)
    if step == -1:
        return range(1, BUCKETS // 2)
    return (BUCKETS - 1,) if step > 0 else (BUCKETS // 2 - 1,)


def tile_at(row_block, key_block):
    step = key_block - row_block
    return TILE_STEPS.index(max(-2, min(2, step)))


def bias_kernel(head_ref, table_ref, out_ref):
    head = head_ref[0]
    for t, step in enumerate(TILE_STEPS):
        buckets = tile_buckets(step)
        tiles = [jnp.zeros((QUARTER, QUARTER), f32)] * LOCAL_HEADS
        for b in possible(step):
            mask = buckets == b
            tiles = [jnp.where(mask, table_ref[b, head + h], tile) for h, tile in enumerate(tiles)]
        for h, tile in enumerate(tiles):
            out_ref[h, t] = tile


def inverse_size(values):
    return lax.rsqrt(jnp.mean(values * values, axis=-1, keepdims=True) + epsilon)


def as_column(row):
    return jnp.transpose(jnp.broadcast_to(row, (QUARTER, QUARTER)))


def start_kernel(x_ref, gain_ref, seg_ref, n0, n1):
    gain = gain_ref[...]
    for s, out in ((0, n0), (1, n1)):
        x = x_ref[s]
        out[:, :WIDTH] = (x * inverse_size(x) * gain).astype(bf16)
        out[:, WIDTH:] = as_column(seg_ref[s : s + 1].astype(f32)).astype(bf16)


def place_kernel(route_ref, cot_ref, place_ref, c_ref):
    tri = (
        lax.broadcasted_iota(jnp.int32, (QUARTER, QUARTER), 0)
        >= lax.broadcasted_iota(jnp.int32, (QUARTER, QUARTER), 1)
    ).astype(bf16)
    for s in range(2):
        chosen = as_column(route_ref[s : s + 1].astype(f32)).astype(jnp.int32)
        mask = jnp.where(
            chosen == lax.broadcasted_iota(jnp.int32, (QUARTER, QUARTER), 1), 1.0, 0.0
        )
        running = dot(tri, mask.astype(bf16))
        rank = jnp.sum(mask * running, axis=-1, keepdims=True).astype(jnp.int32) - 1
        place = chosen[:, :1] * 8 + s * CAPACITY + rank
        slots = lax.broadcasted_iota(jnp.int32, (QUARTER, SLOTS), 1)
        place_ref[s * QUARTER : (s + 1) * QUARTER] = jnp.where(slots == place, 1.0, 0.0).astype(bf16)
    c_ref[...] = dot(place_ref[...], cot_ref[...].astype(bf16), 0, 0).astype(bf16)


def position(me, k):
    return pl.multiple_of(lax.rem(me + k, PARTS) * QUARTER, QUARTER)


def same_document(g_ref):
    column = g_ref[:, WIDTH:].astype(f32)
    return column, jnp.transpose(column)[:1]


def bias_rows(tiles_ref, h, i):
    per = BLOCK // QUARTER
    return jnp.concatenate(
        [
            jnp.concatenate([tiles_ref[h, tile_at(r, j)] for j in range(PARTS)], axis=1)
            for r in range(i * per, (i + 1) * per)
        ],
        axis=0,
    )


def attend_kernel(
    me_ref, a0, a1, a2, a3, w_ref, tiles_ref, g_ref, qkv_ref, att_ref, lse_ref, p0, p1, p2, p3
):
    me = me_ref[0]
    for k, piece in enumerate((a0, a1, a2, a3)):
        g_ref[pl.ds(position(me, k), QUARTER), :] = piece[...]
    qkv_ref[...] = dot(g_ref[:, :WIDTH], w_ref[:, :QKV]).astype(bf16)
    column, row = same_document(g_ref)
    lse_ref[...] = jnp.zeros_like(lse_ref)
    for h in range(LOCAL_HEADS):
        lo = h * HEAD_DIM
        key = qkv_ref[:, CHANNELS + lo : CHANNELS + lo + HEAD_DIM]
        value = qkv_ref[:, 2 * CHANNELS + lo : 2 * CHANNELS + lo + HEAD_DIM]
        for i in range(PARTS * QUARTER // BLOCK):
            rows = slice(i * BLOCK, (i + 1) * BLOCK)
            query = qkv_ref[rows, lo : lo + HEAD_DIM] * HEAD_DIM ** (-0.5)
            scores = dot(query, key, 1, 1) + bias_rows(tiles_ref, h, i)
            scores = jnp.where(column[rows, :1] == row, scores, -1000000000.0)
            row_max = jnp.max(scores, axis=-1, keepdims=True)
            expos = jnp.exp(scores - row_max)
            total = jnp.sum(expos, axis=-1, keepdims=True)
            weights = (expos * (1.0 / total)).astype(bf16)
            att_ref[rows, lo : lo + HEAD_DIM] = dot(weights, value).astype(bf16)
            lse_ref[rows, h : h + 1] = row_max + jnp.log(total)
    for k, out in enumerate((p0, p1, p2, p3)):
        mine = att_ref[pl.ds(position(me, k), QUARTER), :]
        out[...] = dot(mine, w_ref[:, QKV:], 1, 1).astype(bf16)


def dispatch_kernel(
    x_ref, t00, t01, t02, t10, t11, t12, gain_ref, router_ref, route_ref, place_ref,
    hidden_ref, gate_ref, slots_ref,
):
    for s, terms in ((0, (t00, t01, t02)), (1, (t10, t11, t12))):
        rows = slice(s * QUARTER, (s + 1) * QUARTER)
        hidden_ref[rows] = x_ref[s] + added(*[t[...] for t in terms])
    hidden = hidden_ref[...]
    mixed = hidden * inverse_size(hidden) * gain_ref[...]
    low = mixed.astype(bf16)
    slots_ref[...] = dot(place_ref[...], low, 0, 0).astype(bf16)
    logits = dot(mixed, router_ref[...], precision=lax.Precision.HIGHEST)
    expos = jnp.exp(logits - jnp.max(logits, axis=-1, keepdims=True))
    shares = expos / jnp.sum(expos, axis=-1, keepdims=True)
    for s in range(2):
        rows = slice(s * QUARTER, (s + 1) * QUARTER)
        chosen = as_column(route_ref[s : s + 1].astype(f32)).astype(jnp.int32)[:, :EXPERTS]
        mask = chosen == lax.broadcasted_iota(jnp.int32, (QUARTER, EXPERTS), 1)
        gate = jnp.sum(jnp.where(mask, shares[rows], 0.0), axis=-1, keepdims=True)
        gate_ref[rows] = jnp.broadcast_to(gate, (QUARTER, 128))


def upstream_kernel(c0, c1, c2, c3, w_ref, u_ref):
    for k, c in enumerate((c0, c1, c2, c3)):
        u_ref[k] = dot(c[...], w_ref[0], 1, 1).astype(bf16)


def expert_kernel(
    own_ref, x0, x1, x2, x3, u_ref, w_ref, router_ref,
    active_ref, scaled_ref, grad_ref, logit_ref, s0, s1, s2, s3, pre_ref,
):
    own = own_ref[0]
    router = router_ref[...]
    router_hi = router.astype(bf16)
    router_lo = (router - router_hi.astype(f32)).astype(bf16)
    logit_ref[...] = jnp.zeros_like(logit_ref)
    c = math.sqrt(2.0 / math.pi)
    ca = c * 0.044715
    for pieces in (((2, x2, s2), (1, x1, s1)), ((3, x3, s3), (0, x0, s0))):
        x = jnp.concatenate([x_ref[...] for _, x_ref, _ in pieces])
        logits = dot(x, router_hi) + dot(x, router_lo)
        expos = jnp.exp(logits - jnp.max(logits, axis=-1, keepdims=True))
        shares = expos / jnp.sum(expos, axis=-1, keepdims=True)
        chosen = jnp.where(lax.broadcasted_iota(jnp.int32, shares.shape, 1) == own, 1.0, 0.0)
        gate = jnp.sum(shares * chosen, axis=-1, keepdims=True)
        pre_ref[...] = dot(x, w_ref[0])
        gate_grads = []
        for n, (k, _, _) in enumerate(pieces):
            for part in range(HALF_SLOTS // 64):
                rows = slice(part * 64, part * 64 + 64)
                at = slice(n * HALF_SLOTS + part * 64, n * HALF_SLOTS + part * 64 + 64)
                pre = pre_ref[at, :]
                u = u_ref[k, rows, :].astype(f32)
                square = pre * pre
                t = jnp.tanh(pre * (c + ca * square))
                half = 0.5 + 0.5 * t
                active = pre * half
                slope = half + (0.5 * pre) * (1.0 - t * t) * (c + 3.0 * ca * square)
                gate_grads.append(jnp.sum(active * u, axis=-1, keepdims=True))
                active_ref[k, rows, :] = active.astype(bf16)
                scaled_ref[k, rows, :] = (gate[at] * active).astype(bf16)
                grad_ref[k, rows, :] = (gate[at] * u * slope).astype(bf16)
        logit_grad = shares * (chosen - gate) * jnp.concatenate(gate_grads)
        logit_hi = logit_grad.astype(bf16)
        logit_lo = (logit_grad - logit_hi.astype(f32)).astype(bf16)
        pre_grad = jnp.concatenate([grad_ref[k] for k, _, _ in pieces])
        slot_grad = dot(pre_grad, w_ref[0], 1, 1) + dot(logit_hi, router_hi, 1, 1)
        for n, (_, _, out) in enumerate(pieces):
            out[...] = slot_grad[n * HALF_SLOTS : (n + 1) * HALF_SLOTS].astype(bf16)
        logit_ref[...] += dot(x, logit_hi, 0, 0) + dot(x, logit_lo, 0, 0)


def output_kernel(active_ref, w_ref, s0, s1, s2, s3):
    for k, out in ((2, s2), (1, s1), (3, s3), (0, s0)):
        out[...] = dot(active_ref[k], w_ref[0]).astype(bf16)


def weights_kernel(scaled_ref, grad_ref, c0, c1, c2, c3, x0, x1, x2, x3, *rest):
    out_ref, in_ref = rest[-2:]
    for k, (c, x) in enumerate(zip((c0, c1, c2, c3), (x0, x1, x2, x3))):
        out_term = dot(scaled_ref[k], c[...], 0, 0)
        in_term = dot(x[...], grad_ref[k], 0, 0)
        if k == 0:
            out_ref[0] = out_term
            in_ref[0] = in_term
        else:
            out_ref[0] += out_term
            in_ref[0] += in_term


def back_kernel(slots_ref, place_ref, hidden_ref, cot_ref, gain_ref, grad_ref, h0, h1, gain_grad_ref):
    mixed_grad = dot(place_ref[...], slots_ref[...])
    hidden = hidden_ref[...]
    r = inverse_size(hidden)
    gain_grad_ref[...] = jnp.sum(mixed_grad * hidden * r, axis=0, keepdims=True)
    u = gain_ref[...] * mixed_grad
    grad = cot_ref[...] + r * u - hidden * (r * r * r * jnp.mean(hidden * u, axis=-1, keepdims=True))
    grad_ref[...] = grad
    h0[...] = grad[:QUARTER].astype(bf16)
    h1[...] = grad[QUARTER:].astype(bf16)


def result_kernel(slots_ref, place_ref, hidden_ref, gate_ref, out_ref):
    back = dot(place_ref[...], slots_ref[...])
    out_ref[...] = hidden_ref[...] + gate_ref[:, :1] * back


def attend_back_kernel(
    me_ref, a0, a1, a2, a3, w_ref, tiles_ref, g_ref, qkv_ref, lse_ref,
    up_ref, dqkv_ref, sums_ref, gain_ref, p0, p1, p2, p3, tile_sums,
):
    me = me_ref[0]
    for k, piece in enumerate((a0, a1, a2, a3)):
        up_ref[pl.ds(position(me, k), QUARTER), :] = piece[...]
    att_grad = dot(up_ref[...], w_ref[:, QKV:]).astype(bf16)
    column, row = same_document(g_ref)
    tile_sums[...] = jnp.zeros_like(tile_sums)
    for h in range(LOCAL_HEADS):
        lo = h * HEAD_DIM
        key = qkv_ref[:, CHANNELS + lo : CHANNELS + lo + HEAD_DIM]
        value = qkv_ref[:, 2 * CHANNELS + lo : 2 * CHANNELS + lo + HEAD_DIM]
        key_grad = jnp.zeros((HEAD_DIM, PARTS * QUARTER), f32)
        value_grad = jnp.zeros((HEAD_DIM, PARTS * QUARTER), f32)
        for i in range(PARTS * QUARTER // BLOCK):
            rows = slice(i * BLOCK, (i + 1) * BLOCK)
            query = qkv_ref[rows, lo : lo + HEAD_DIM] * HEAD_DIM ** (-0.5)
            scores = dot(query, key, 1, 1) + bias_rows(tiles_ref, h, i)
            scores = jnp.where(column[rows, :1] == row, scores, -1000000000.0)
            weights = jnp.exp(scores - lse_ref[rows, h : h + 1])
            out_grad = att_grad[rows, lo : lo + HEAD_DIM]
            weights_grad = dot(out_grad, value, 1, 1)
            inner = jnp.sum(weights * weights_grad, axis=-1, keepdims=True)
            score_grad = (weights * (weights_grad - inner)).astype(bf16)
            wide = score_grad.astype(f32)
            for r in range(BLOCK // QUARTER):
                for j in range(PARTS):
                    tile_sums[h, tile_at(i * (BLOCK // QUARTER) + r, j)] += wide[
                        r * QUARTER : (r + 1) * QUARTER, j * QUARTER : (j + 1) * QUARTER
                    ]
            dqkv_ref[rows, lo : lo + HEAD_DIM] = (
                dot(score_grad, key) * HEAD_DIM ** (-0.5)
            ).astype(bf16)
            key_grad += dot(query, score_grad, 0, 0)
            value_grad += dot(out_grad, weights.astype(bf16), 0, 0)
        dqkv_ref[:, CHANNELS + lo : CHANNELS + lo + HEAD_DIM] = jnp.transpose(key_grad).astype(bf16)
        dqkv_ref[:, 2 * CHANNELS + lo : 2 * CHANNELS + lo + HEAD_DIM] = jnp.transpose(
            value_grad
        ).astype(bf16)
    gain = jnp.zeros((1, WIDTH), f32)
    for k, out in ((2, p2), (1, p1), (3, p3), (0, p0)):
        at = pl.ds(position(me, k), QUARTER)
        normed_grad = dot(dqkv_ref[at, :], w_ref[:, :QKV], 1, 1)
        out[...] = normed_grad.astype(bf16)
        gain += jnp.sum(normed_grad * g_ref[at, :WIDTH].astype(f32), axis=0, keepdims=True)
    gain_ref[...] = gain
    sums_ref[...] = jnp.zeros_like(sums_ref)
    for t, step in enumerate(TILE_STEPS):
        buckets = tile_buckets(step)
        for b in possible(step):
            mask = buckets == b
            for h in range(LOCAL_HEADS):
                sums_ref[h, b : b + 1] += jnp.sum(
                    jnp.where(mask, tile_sums[h, t], 0.0), axis=0, keepdims=True
                )


def projection_kernel(g0, g1, d0, d1, u0, u1, a0, a1, out_ref):
    out_ref[:, :QKV] = (
        dot(g0[:, :WIDTH], d0[...], 0, 0) + dot(g1[:, :WIDTH], d1[...], 0, 0)
    ).astype(bf16)
    out_ref[:, QKV:] = (dot(u0[...], a0[...], 0, 0) + dot(u1[...], a1[...], 0, 0)).astype(bf16)


def input_kernel(x_ref, gain_ref, grad_ref, t00, t01, t02, t10, t11, t12, out_ref):
    for s, terms in ((0, (t00, t01, t02)), (1, (t10, t11, t12))):
        x = x_ref[s]
        r = inverse_size(x)
        u = gain_ref[...] * added(*[t[...] for t in terms])
        out_ref[s] = (
            grad_ref[s * QUARTER : (s + 1) * QUARTER]
            + r * u
            - x * (r * r * r * jnp.mean(x * u, axis=-1, keepdims=True))
        )


def expert_spec(e):
    return pl.BlockSpec((1, WIDTH, WIDTH), lambda i: (e, 0, 0))


def body(
    inputs,
    projection_in,
    projection_out,
    gain_attention,
    gain_experts,
    router_weight,
    bias_table,
    expert_in,
    expert_out,
    routes,
    segments,
    cotangent,
):
    seq_here, quarter, width = inputs.shape
    rows = seq_here * quarter
    me = lax.axis_index("mp").reshape(1).astype(jnp.int32)
    first_head = me * LOCAL_HEADS
    gain1, gain2 = gain_attention.reshape(1, width), gain_experts.reshape(1, width)
    routes = routes.reshape(seq_here, quarter)
    upstream = cotangent.reshape(rows, width)
    piece = struct((QUARTER, WIDTH), bf16)
    slot_piece = struct((HALF_SLOTS, WIDTH), bf16)

    turned = jnp.concatenate(
        [jnp.moveaxis(projection_in, 1, 0).reshape(24, QKV), projection_out.T], axis=1
    )
    weights = sent_to_all(turned, EXPERT).reshape(WIDTH, QKV + CHANNELS)

    tagged = struct((QUARTER, TAGGED), bf16)
    n0, n1 = call(start_kernel, (tagged, tagged), (inputs, gain1, segments), name="start")
    place, c_slots = call(
        place_kernel,
        (struct((rows, SLOTS), bf16), struct((SLOTS, width), bf16)),
        (routes, upstream),
        name="place",
    )
    normed = (gather4(n0, 1), gather4(n1, -1))
    tiles = call(
        bias_kernel,
        struct((LOCAL_HEADS, len(TILE_STEPS), QUARTER, QUARTER), f32),
        (first_head, bias_table),
        [SMEM, SMEM],
        name="bias",
    )
    length = PARTS * QUARTER
    attended = [
        call(
            attend_kernel,
            (
                struct((length, TAGGED), bf16),
                struct((length, QKV), bf16),
                struct((length, CHANNELS), bf16),
                struct((length, 128), f32),
                piece, piece, piece, piece,
            ),
            (me, *normed[s], weights, tiles),
            [SMEM] + [VMEM] * 6,
            flops=2 * 10**9,
            name="attend",
        )
        for s in range(2)
    ]
    attention = [reduce4(attended[s][4:], (1, -1)[s]) for s in range(2)]

    c_slots = by_expert(to_experts(after(c_slots, attended[1][4])))
    c_all = [gather4(c, (1, -1)[e]) for e, c in enumerate(c_slots)]
    u = [
        call(
            upstream_kernel,
            struct((PARTS, HALF_SLOTS, WIDTH), bf16),
            (*c_all[e], expert_out),
            [VMEM] * 4 + [expert_spec(e)],
            flops=12 * 10**8,
            name="upstream",
        )
        for e in range(2)
    ]

    hidden, gate, slots = call(
        dispatch_kernel,
        (struct((rows, width), f32), struct((rows, 128), f32), struct((SLOTS, width), bf16)),
        (inputs, *attention[0], *attention[1], gain2, router_weight, routes, place),
        name="dispatch",
    )
    x_all = [gather4(x, (1, -1)[e]) for e, x in enumerate(by_expert(to_experts(slots)))]
    group = lax.axis_index(EXPERT).astype(jnp.int32)
    acts = struct((PARTS, HALF_SLOTS, WIDTH), bf16)
    worked = [
        call(
            expert_kernel,
            (acts, acts, acts, struct((WIDTH, EXPERTS), f32)) + (slot_piece,) * 4,
            ((group * 2 + e).reshape(1), *x_all[e], u[e], expert_in, router_weight),
            [SMEM] + [VMEM] * 5 + [expert_spec(e), VMEM],
            scratch=[pltpu.VMEM((SLOTS, WIDTH), f32)],
            flops=24 * 10**8,
            moved=2 * 10**7,
            name="expert",
        )
        for e in range(2)
    ]
    returned = to_experts(summed_slots([reduce4(worked[e][4:], (1, -1)[e]) for e in range(2)]))
    hidden_grad, h0, h1, gain2_grad = call(
        back_kernel,
        (struct((rows, width), f32), piece, piece, struct((1, width), f32)),
        (returned.reshape(SLOTS, width), place, hidden, upstream, gain2),
        name="back",
    )
    grads = (gather4(h0, 1), gather4(h1, -1))
    attended_back = [
        call(
            attend_back_kernel,
            (
                struct((length, width), bf16),
                struct((length, QKV), bf16),
                struct((LOCAL_HEADS, BUCKETS, 128), f32),
                struct((1, width), f32),
                piece, piece, piece, piece,
            ),
            (me, *grads[s], weights, tiles, *attended[s][:2], attended[s][3]),
            [SMEM] + [VMEM] * 9,
            scratch=[pltpu.VMEM((LOCAL_HEADS, len(TILE_STEPS), QUARTER, QUARTER), f32)],
            flops=4 * 10**9,
            name="attend_back",
        )
        for s in range(2)
    ]
    normed_grad = [reduce4(attended_back[s][4:], (1, -1)[s]) for s in range(2)]
    input_grad = call(
        input_kernel,
        struct(inputs.shape, f32),
        (inputs, gain1, hidden_grad, *normed_grad[0], *normed_grad[1]),
        name="input_gradient",
    )

    outputs = [
        call(
            output_kernel,
            (slot_piece,) * 4,
            (worked[e][0], expert_out),
            [VMEM, expert_spec(e)],
            flops=12 * 10**8,
            name="expert_output",
        )
        for e in range(2)
    ]
    output_slots = summed_slots([reduce4(outputs[e], (1, -1)[e]) for e in range(2)])
    router = (worked[0][3] + worked[1][3]).astype(bf16).reshape(32, 16, 96)
    router = jnp.pad(router, ((0, 0), (0, 0), (0, 32)))
    output_slots = jnp.concatenate([output_slots, router], axis=2)
    output_back = to_experts(after(output_slots, grads[0][1], grads[1][1]))
    router_rows = jnp.sum(output_back[:, :, width : width + 96].astype(f32), axis=0)
    result = call(
        result_kernel,
        struct((rows, width), f32),
        (output_back[:, :, :width].reshape(SLOTS, width), place, hidden, gate),
        name="result",
    )
    whole = struct((2, WIDTH, WIDTH), f32)
    expert_grads = None
    for e in range(2):
        ins = (worked[e][1], worked[e][2], *c_all[e], *x_all[e])
        earlier = () if expert_grads is None else expert_grads
        expert_grads = pl.pallas_call(
            weights_kernel,
            grid=(1,),
            out_shape=(whole, whole),
            in_specs=[VMEM] * 10 + [pl.BlockSpec(memory_space=pl.ANY)] * len(earlier),
            out_specs=(expert_spec(e), expert_spec(e)),
            input_output_aliases={10: 0, 11: 1} if earlier else {},
            cost_estimate=pl.CostEstimate(
                flops=24 * 10**8, bytes_accessed=2 * 10**7, transcendentals=0
            ),
            compiler_params=pltpu.CompilerParams(vmem_limit_bytes=VMEM_LIMIT),
            name="expert_weights",
        )(*ins, *earlier)
    grad_expert_out, grad_expert_in = expert_grads

    partial = call(
        projection_kernel,
        struct((WIDTH, QKV + CHANNELS), bf16),
        (
            attended[0][0], attended[1][0], attended_back[0][1], attended_back[1][1],
            attended_back[0][0], attended_back[1][0], attended[0][2], attended[1][2],
        ),
        flops=16 * 10**8,
        name="projection_gradient",
    )
    table_local = jnp.sum(attended_back[0][2] + attended_back[1][2], axis=-1).T
    table = lax.dynamic_update_slice(
        jnp.zeros((BUCKETS, HEADS), f32), table_local, (0, first_head[0])
    )
    gain1_grad = (attended_back[0][3] + attended_back[1][3]) / gain1
    small = jnp.concatenate(
        [t.reshape(-1) for t in (router_rows, gain1_grad, gain2_grad, table)]
    ).reshape(27, 128)
    small = added(small, shift(small, 1), shift(small, -1), shift(small, 2)).reshape(-1)
    lines = jnp.pad(small.astype(bf16), (0, 5 * width - small.size)).reshape(1, 5, width)
    lines = jnp.concatenate(
        [partial.reshape(32, 24, width), jnp.broadcast_to(lines, (32, 5, width))], axis=1
    )
    arrived = lax.all_to_all(lines, EXPERT, 0, 0, tiled=True)
    projections = jnp.sum(arrived[:, :24].astype(f32), axis=0)
    grad_projection_in = jnp.moveaxis(projections[:, :QKV].reshape(24, 3, CHANNELS), 1, 0)
    grad_projection_out = projections[:, QKV:].T
    grad_router = arrived[:, 24:26].astype(f32).reshape(WIDTH, EXPERTS)
    late = jnp.sum(arrived[:, 26:].astype(f32), axis=0).reshape(-1)
    grad_gain_attention = late[:width]
    grad_gain_experts = late[width : 2 * width]
    grad_table = late[2 * width : 2 * width + BUCKETS * HEADS].reshape(BUCKETS, HEADS)
    return (
        result.reshape(seq_here, quarter, width),
        input_grad,
        grad_projection_in,
        grad_projection_out,
        grad_gain_attention,
        grad_gain_experts,
        grad_router,
        grad_table,
        grad_expert_in,
        grad_expert_out,
    )


def solution(mesh):
    split = Mesh(
        mesh.devices.reshape(4, 4, 2, mesh.shape["mp"]), ("expert_0", "expert_1", "expert_2", "mp")
    )
    in_specs = (
        P(EXPERT, "mp", None),
        P(None, EXPERT, "mp"),
        P("mp", EXPERT),
        P(),
        P(),
        P(),
        P(),
        P(EXPERT, None, "mp"),
        P(EXPERT, "mp", None),
        P(EXPERT, "mp", None),
        P(EXPERT, "mp"),
        P(EXPERT, "mp", None),
    )
    out_specs = (
        P(EXPERT, "mp", None),
        P(EXPERT, "mp", None),
        P(None, EXPERT, "mp"),
        P("mp", EXPERT),
        P(),
        P(),
        P(),
        P(),
        P(EXPERT, None, "mp"),
        P(EXPERT, "mp", None),
    )
    return jax.shard_map(body, mesh=split, in_specs=in_specs, out_specs=out_specs, check_vma=False)
```

```python
import functools
import math

import jax
import jax.numpy as jnp
from jax import lax
from jax.experimental import pallas as pl
from jax.experimental.pallas import tpu as pltpu
from jax.sharding import Mesh
from jax.sharding import PartitionSpec as P

HEADS = 12
HEAD_DIM = 64
EXPERTS = 64
BUCKETS = 32
REACH = 128
EXPERT = ("expert_0", "expert_1", "expert_2")
QUARTER = 128
PARTS = 4
WIDTH = 768
CHANNELS = 192
LOCAL_HEADS = CHANNELS // HEAD_DIM
QKV = 3 * CHANNELS
CAPACITY = 4
SLOTS = 512
HALF_SLOTS = SLOTS // 2
TAGGED = WIDTH + 128
TILE_STEPS = (0, 1, -1, 2, -2)

epsilon = 1e-06
f32 = jnp.float32
bf16 = jnp.bfloat16
BLOCK = 512
VMEM_LIMIT = 56 * 1024 * 1024


def dot(a, b, ca=1, cb=0, precision=None):
    return lax.dot_general(
        a, b, (((ca,), (cb,)), ((), ())), preferred_element_type=f32, precision=precision
    )


def struct(shape, dtype):
    return jax.ShapeDtypeStruct(shape, dtype)


SMEM = pl.BlockSpec(memory_space=pltpu.SMEM)
VMEM = pl.BlockSpec(memory_space=pltpu.VMEM)


def call(kernel, outs, ins, in_specs=None, scratch=(), flops=10**8, moved=4 * 10**6, name=None):
    return pl.pallas_call(
        kernel,
        grid=(1,),
        out_shape=outs,
        in_specs=in_specs or [VMEM] * len(ins),
        out_specs=jax.tree.map(lambda _: VMEM, outs),
        scratch_shapes=scratch,
        cost_estimate=pl.CostEstimate(flops=flops, bytes_accessed=moved, transcendentals=0),
        compiler_params=pltpu.CompilerParams(vmem_limit_bytes=VMEM_LIMIT),
        name=name,
    )(*ins)


def shift(x, step):
    return lax.ppermute(x, "mp", [(i, (i + step) % PARTS) for i in range(PARTS)])


def gather4(x, way):
    left, right = shift(x, 1), shift(x, -1)
    far = shift(left, 1) if way > 0 else shift(right, -1)
    return x, right, far, left


def added(*terms):
    return functools.reduce(lambda a, b: a + b, [t.astype(f32) for t in terms])


def reduce4(pieces, way):
    own, right, far, left = pieces
    if way > 0:
        right = added(right, shift(far, 1)).astype(bf16)
    else:
        left = added(left, shift(far, -1)).astype(bf16)
    return own, shift(right, 1), shift(left, -1)


def after(x, *others):
    return lax.optimization_barrier((x, *others))[0]


def to_experts(x):
    return lax.all_to_all(x.reshape(32, -1, x.shape[-1]), EXPERT, 0, 0, tiled=True)


def by_expert(slots):
    return tuple(slots[:, 8 * e : 8 * e + 8, :WIDTH].reshape(HALF_SLOTS, WIDTH) for e in range(2))


def summed_slots(terms):
    pieces = [added(*terms[e]).astype(bf16).reshape(32, 8, WIDTH) for e in range(2)]
    return jnp.concatenate(pieces, axis=1)


def sent_to_all(x, axis):
    peers = lax.axis_size(axis)
    return lax.all_to_all(jnp.broadcast_to(x[None], (peers, *x.shape)), axis, 0, 0, tiled=True)


def bucket_of(offsets):
    halfway = BUCKETS // 2
    exact_span = halfway // 2
    distance = jnp.abs(offsets)
    far_part = jnp.full_like(distance, exact_span)
    for step in range(1, exact_span):
        cutoff_level = math.ceil(exact_span * (REACH / exact_span) ** (step / exact_span) - 1e-09)
        far_part = far_part + jnp.where(distance >= cutoff_level, 1, 0)
    nearby = jnp.where(distance < exact_span, distance, far_part)
    return nearby + jnp.where(offsets > 0, halfway, 0)


def tile_buckets(step):
    shape = (QUARTER, QUARTER)
    offsets = (
        step * QUARTER
        + lax.broadcasted_iota(jnp.int32, shape, 1)
        - lax.broadcasted_iota(jnp.int32, shape, 0)
    )
    return bucket_of(offsets)


def possible(step):
    if step == 0:
        return range(BUCKETS)
    if step == 1:
        return range(BUCKETS // 2 + 1, BUCKETS)
    if step == -1:
        return range(1, BUCKETS // 2)
    return (BUCKETS - 1,) if step > 0 else (BUCKETS // 2 - 1,)


def tile_at(row_block, key_block):
    step = key_block - row_block
    return TILE_STEPS.index(max(-2, min(2, step)))


def bias_kernel(head_ref, table_ref, out_ref):
    head = head_ref[0]
    for t, step in enumerate(TILE_STEPS):
        buckets = tile_buckets(step)
        tiles = [jnp.zeros((QUARTER, QUARTER), f32)] * LOCAL_HEADS
        for b in possible(step):
            mask = buckets == b
            tiles = [jnp.where(mask, table_ref[b, head + h], tile) for h, tile in enumerate(tiles)]
        for h, tile in enumerate(tiles):
            out_ref[h, t] = tile


def inverse_size(values):
    return lax.rsqrt(jnp.mean(values * values, axis=-1, keepdims=True) + epsilon)


def as_column(row):
    return jnp.transpose(jnp.broadcast_to(row, (QUARTER, QUARTER)))


def start_kernel(x_ref, gain_ref, seg_ref, n0, n1):
    gain = gain_ref[...]
    for s, out in ((0, n0), (1, n1)):
        x = x_ref[s]
        out[:, :WIDTH] = (x * inverse_size(x) * gain).astype(bf16)
        out[:, WIDTH:] = as_column(seg_ref[s : s + 1].astype(f32)).astype(bf16)


def place_kernel(route_ref, cot_ref, place_ref, c_ref):
    tri = (
        lax.broadcasted_iota(jnp.int32, (QUARTER, QUARTER), 0)
        >= lax.broadcasted_iota(jnp.int32, (QUARTER, QUARTER), 1)
    ).astype(bf16)
    for s in range(2):
        chosen = as_column(route_ref[s : s + 1].astype(f32)).astype(jnp.int32)
        mask = jnp.where(
            chosen == lax.broadcasted_iota(jnp.int32, (QUARTER, QUARTER), 1), 1.0, 0.0
        )
        running = dot(tri, mask.astype(bf16))
        rank = jnp.sum(mask * running, axis=-1, keepdims=True).astype(jnp.int32) - 1
        place = chosen[:, :1] * 8 + s * CAPACITY + rank
        slots = lax.broadcasted_iota(jnp.int32, (QUARTER, SLOTS), 1)
        place_ref[s * QUARTER : (s + 1) * QUARTER] = jnp.where(slots == place, 1.0, 0.0).astype(bf16)
    c_ref[...] = dot(place_ref[...], cot_ref[...].astype(bf16), 0, 0).astype(bf16)


def position(me, k):
    return pl.multiple_of(lax.rem(me + k, PARTS) * QUARTER, QUARTER)


def same_document(g_ref):
    column = g_ref[:, WIDTH:].astype(f32)
    return column, jnp.transpose(column)[:1]


def bias_rows(tiles_ref, h, i):
    per = BLOCK // QUARTER
    return jnp.concatenate(
        [
            jnp.concatenate([tiles_ref[h, tile_at(r, j)] for j in range(PARTS)], axis=1)
            for r in range(i * per, (i + 1) * per)
        ],
        axis=0,
    )


def attend_kernel(
    me_ref, a0, a1, a2, a3, w_ref, tiles_ref, g_ref, qkv_ref, att_ref, lse_ref, p0, p1, p2, p3
):
    me = me_ref[0]
    for k, piece in enumerate((a0, a1, a2, a3)):
        g_ref[pl.ds(position(me, k), QUARTER), :] = piece[...]
    qkv_ref[...] = dot(g_ref[:, :WIDTH], w_ref[:, :QKV]).astype(bf16)
    column, row = same_document(g_ref)
    lse_ref[...] = jnp.zeros_like(lse_ref)
    for h in range(LOCAL_HEADS):
        lo = h * HEAD_DIM
        key = qkv_ref[:, CHANNELS + lo : CHANNELS + lo + HEAD_DIM]
        value = qkv_ref[:, 2 * CHANNELS + lo : 2 * CHANNELS + lo + HEAD_DIM]
        for i in range(PARTS * QUARTER // BLOCK):
            rows = slice(i * BLOCK, (i + 1) * BLOCK)
            query = qkv_ref[rows, lo : lo + HEAD_DIM] * HEAD_DIM ** (-0.5)
            scores = dot(query, key, 1, 1) + bias_rows(tiles_ref, h, i)
            scores = jnp.where(column[rows, :1] == row, scores, -1000000000.0)
            row_max = jnp.max(scores, axis=-1, keepdims=True)
            expos = jnp.exp(scores - row_max)
            total = jnp.sum(expos, axis=-1, keepdims=True)
            weights = (expos * (1.0 / total)).astype(bf16)
            att_ref[rows, lo : lo + HEAD_DIM] = dot(weights, value).astype(bf16)
            lse_ref[rows, h : h + 1] = row_max + jnp.log(total)
    for k, out in enumerate((p0, p1, p2, p3)):
        mine = att_ref[pl.ds(position(me, k), QUARTER), :]
        out[...] = dot(mine, w_ref[:, QKV:], 1, 1).astype(bf16)


def dispatch_kernel(
    x_ref, t00, t01, t02, t10, t11, t12, gain_ref, router_ref, route_ref, place_ref,
    hidden_ref, gate_ref, slots_ref,
):
    for s, terms in ((0, (t00, t01, t02)), (1, (t10, t11, t12))):
        rows = slice(s * QUARTER, (s + 1) * QUARTER)
        hidden_ref[rows] = x_ref[s] + added(*[t[...] for t in terms])
    hidden = hidden_ref[...]
    mixed = hidden * inverse_size(hidden) * gain_ref[...]
    low = mixed.astype(bf16)
    slots_ref[...] = dot(place_ref[...], low, 0, 0).astype(bf16)
    logits = dot(mixed, router_ref[...], precision=lax.Precision.HIGHEST)
    expos = jnp.exp(logits - jnp.max(logits, axis=-1, keepdims=True))
    shares = expos / jnp.sum(expos, axis=-1, keepdims=True)
    for s in range(2):
        rows = slice(s * QUARTER, (s + 1) * QUARTER)
        chosen = as_column(route_ref[s : s + 1].astype(f32)).astype(jnp.int32)[:, :EXPERTS]
        mask = chosen == lax.broadcasted_iota(jnp.int32, (QUARTER, EXPERTS), 1)
        gate = jnp.sum(jnp.where(mask, shares[rows], 0.0), axis=-1, keepdims=True)
        gate_ref[rows] = jnp.broadcast_to(gate, (QUARTER, 128))


WORK_ORDER = (2, 1, 3, 0)


def upstream_kernel(c0, c1, c2, c3, w_ref, u_ref):
    pieces = (c0, c1, c2, c3)
    for n, k in enumerate(WORK_ORDER):
        u_ref[n] = dot(pieces[k][...], w_ref[0], 1, 1).astype(bf16)


def expert_kernel(
    own_ref, x0, x1, x2, x3, u_ref, w_ref, router_ref,
    active_ref, scaled_ref, grad_ref, logit_ref, s0, s1, s2, s3, pre_ref,
):
    own = own_ref[0]
    router = router_ref[...]
    router_hi = router.astype(bf16)
    router_lo = (router - router_hi.astype(f32)).astype(bf16)
    router_both = jnp.concatenate([router_hi, router_lo], axis=1)
    c = math.sqrt(2.0 / math.pi)
    ca = c * 0.044715

    def work(xs, outs, first):
        x = jnp.concatenate([x_ref[...] for x_ref in xs])
        logits = dot(x, router_both)
        logits = logits[:, :EXPERTS] + logits[:, EXPERTS:]
        expos = jnp.exp(logits - jnp.max(logits, axis=-1, keepdims=True))
        shares = expos / jnp.sum(expos, axis=-1, keepdims=True)
        chosen = jnp.where(lax.broadcasted_iota(jnp.int32, shares.shape, 1) == own, 1.0, 0.0)
        gate = jnp.sum(shares * chosen, axis=-1, keepdims=True)
        pre_ref[...] = dot(x, w_ref[0])
        gate_grads = []
        for n in range(2):
            for part in range(HALF_SLOTS // 64):
                rows = slice(part * 64, part * 64 + 64)
                at = slice(n * HALF_SLOTS + part * 64, n * HALF_SLOTS + part * 64 + 64)
                pre = pre_ref[at, :]
                u = u_ref[n, rows, :].astype(f32)
                square = pre * pre
                t = jnp.tanh(pre * (c + ca * square))
                half = 0.5 + 0.5 * t
                active = pre * half
                slope = half + (0.5 * pre) * (1.0 - t * t) * (c + 3.0 * ca * square)
                gate_grads.append(jnp.sum(active * u, axis=-1, keepdims=True))
                active_ref[n, rows, :] = active.astype(bf16)
                scaled_ref[n, rows, :] = (gate[at] * active).astype(bf16)
                grad_ref[n, rows, :] = (gate[at] * u * slope).astype(bf16)
        logit_grad = shares * (chosen - gate) * jnp.concatenate(gate_grads)
        logit_hi = logit_grad.astype(bf16)
        logit_lo = (logit_grad - logit_hi.astype(f32)).astype(bf16)
        pre_grad = jnp.concatenate([grad_ref[0], grad_ref[1]])
        slot_grad = dot(pre_grad, w_ref[0], 1, 1) + dot(logit_hi, router_hi, 1, 1)
        for n, out in enumerate(outs):
            out[...] = slot_grad[n * HALF_SLOTS : (n + 1) * HALF_SLOTS].astype(bf16)
        term = dot(jnp.concatenate([logit_hi, logit_lo], axis=1), x, 0, 0)
        if first:
            logit_ref[...] = term
        else:
            logit_ref[...] += term

    pl.when(pl.program_id(0) == 0)(lambda: work((x2, x1), (s2, s1), True))
    pl.when(pl.program_id(0) == 1)(lambda: work((x3, x0), (s3, s0), False))


def output_kernel(active_ref, w_ref, s0, s1, s2, s3):
    outs = (s0, s1, s2, s3)
    for n, k in enumerate(WORK_ORDER):
        outs[k][...] = dot(active_ref[n], w_ref[0]).astype(bf16)


def weights_kernel(scaled_ref, grad_ref, c0, c1, c2, c3, x0, x1, x2, x3, *rest):
    out_ref, in_ref, token_ref = rest[-3:]
    token_ref[...] = jnp.zeros_like(token_ref)
    upstream, entered = (c0, c1, c2, c3), (x0, x1, x2, x3)
    for n, k in enumerate(WORK_ORDER):
        out_term = dot(scaled_ref[n], upstream[k][...], 0, 0)
        in_term = dot(entered[k][...], grad_ref[n], 0, 0)
        if n == 0:
            out_ref[0] = out_term
            in_ref[0] = in_term
        else:
            out_ref[0] += out_term
            in_ref[0] += in_term


def back_kernel(slots_ref, place_ref, hidden_ref, cot_ref, gain_ref, grad_ref, h0, h1, gain_grad_ref):
    mixed_grad = dot(place_ref[...], slots_ref[...])
    hidden = hidden_ref[...]
    r = inverse_size(hidden)
    gain_grad_ref[...] = jnp.sum(mixed_grad * hidden * r, axis=0, keepdims=True)
    u = gain_ref[...] * mixed_grad
    grad = cot_ref[...] + r * u - hidden * (r * r * r * jnp.mean(hidden * u, axis=-1, keepdims=True))
    grad_ref[...] = grad
    h0[...] = grad[:QUARTER].astype(bf16)
    h1[...] = grad[QUARTER:].astype(bf16)


def result_kernel(slots_ref, place_ref, hidden_ref, gate_ref, out_ref):
    back = dot(place_ref[...], slots_ref[...])
    out_ref[...] = hidden_ref[...] + gate_ref[:, :1] * back


def attend_back_kernel(
    me_ref, a0, a1, a2, a3, w_ref, tiles_ref, g_ref, qkv_ref, lse_ref,
    up_ref, dqkv_ref, sums_ref, gain_ref, p0, p1, p2, p3, tile_sums,
):
    me = me_ref[0]
    for k, piece in enumerate((a0, a1, a2, a3)):
        up_ref[pl.ds(position(me, k), QUARTER), :] = piece[...]
    att_grad = dot(up_ref[...], w_ref[:, QKV:]).astype(bf16)
    column, row = same_document(g_ref)
    tile_sums[...] = jnp.zeros_like(tile_sums)
    for h in range(LOCAL_HEADS):
        lo = h * HEAD_DIM
        key = qkv_ref[:, CHANNELS + lo : CHANNELS + lo + HEAD_DIM]
        value = qkv_ref[:, 2 * CHANNELS + lo : 2 * CHANNELS + lo + HEAD_DIM]
        key_grad = jnp.zeros((HEAD_DIM, PARTS * QUARTER), f32)
        value_grad = jnp.zeros((HEAD_DIM, PARTS * QUARTER), f32)
        for i in range(PARTS * QUARTER // BLOCK):
            rows = slice(i * BLOCK, (i + 1) * BLOCK)
            query = qkv_ref[rows, lo : lo + HEAD_DIM] * HEAD_DIM ** (-0.5)
            scores = dot(query, key, 1, 1) + bias_rows(tiles_ref, h, i)
            scores = jnp.where(column[rows, :1] == row, scores, -1000000000.0)
            weights = jnp.exp(scores - lse_ref[rows, h : h + 1])
            out_grad = att_grad[rows, lo : lo + HEAD_DIM]
            weights_grad = dot(out_grad, value, 1, 1)
            inner = jnp.sum(weights * weights_grad, axis=-1, keepdims=True)
            score_grad = (weights * (weights_grad - inner)).astype(bf16)
            wide = score_grad.astype(f32)
            for r in range(BLOCK // QUARTER):
                for j in range(PARTS):
                    tile_sums[h, tile_at(i * (BLOCK // QUARTER) + r, j)] += wide[
                        r * QUARTER : (r + 1) * QUARTER, j * QUARTER : (j + 1) * QUARTER
                    ]
            dqkv_ref[rows, lo : lo + HEAD_DIM] = (
                dot(score_grad, key) * HEAD_DIM ** (-0.5)
            ).astype(bf16)
            key_grad += dot(query, score_grad, 0, 0)
            value_grad += dot(out_grad, weights.astype(bf16), 0, 0)
        dqkv_ref[:, CHANNELS + lo : CHANNELS + lo + HEAD_DIM] = jnp.transpose(key_grad).astype(bf16)
        dqkv_ref[:, 2 * CHANNELS + lo : 2 * CHANNELS + lo + HEAD_DIM] = jnp.transpose(
            value_grad
        ).astype(bf16)
    gain = jnp.zeros((1, WIDTH), f32)
    for k, out in ((2, p2), (1, p1), (3, p3), (0, p0)):
        at = pl.ds(position(me, k), QUARTER)
        normed_grad = dot(dqkv_ref[at, :], w_ref[:, :QKV], 1, 1)
        out[...] = normed_grad.astype(bf16)
        gain += jnp.sum(normed_grad * g_ref[at, :WIDTH].astype(f32), axis=0, keepdims=True)
    gain_ref[...] = gain
    sums_ref[...] = jnp.zeros_like(sums_ref)
    for t, step in enumerate(TILE_STEPS):
        buckets = tile_buckets(step)
        for b in possible(step):
            mask = buckets == b
            for h in range(LOCAL_HEADS):
                sums_ref[h, b : b + 1] += jnp.sum(
                    jnp.where(mask, tile_sums[h, t], 0.0), axis=0, keepdims=True
                )


def projection_kernel(g0, g1, d0, d1, u0, u1, a0, a1, out_ref):
    out_ref[:, :QKV] = (
        dot(g0[:, :WIDTH], d0[...], 0, 0) + dot(g1[:, :WIDTH], d1[...], 0, 0)
    ).astype(bf16)
    out_ref[:, QKV:] = (dot(u0[...], a0[...], 0, 0) + dot(u1[...], a1[...], 0, 0)).astype(bf16)


def input_kernel(x_ref, gain_ref, grad_ref, t00, t01, t02, t10, t11, t12, out_ref):
    for s, terms in ((0, (t00, t01, t02)), (1, (t10, t11, t12))):
        x = x_ref[s]
        r = inverse_size(x)
        u = gain_ref[...] * added(*[t[...] for t in terms])
        out_ref[s] = (
            grad_ref[s * QUARTER : (s + 1) * QUARTER]
            + r * u
            - x * (r * r * r * jnp.mean(x * u, axis=-1, keepdims=True))
        )


def expert_spec(e):
    return pl.BlockSpec((1, WIDTH, WIDTH), lambda i: (e, 0, 0))


def body(
    inputs,
    projection_in,
    projection_out,
    gain_attention,
    gain_experts,
    router_weight,
    bias_table,
    expert_in,
    expert_out,
    routes,
    segments,
    cotangent,
):
    seq_here, quarter, width = inputs.shape
    rows = seq_here * quarter
    me = lax.axis_index("mp").reshape(1).astype(jnp.int32)
    first_head = me * LOCAL_HEADS
    gain1, gain2 = gain_attention.reshape(1, width), gain_experts.reshape(1, width)
    routes = routes.reshape(seq_here, quarter)
    upstream = cotangent.reshape(rows, width)
    piece = struct((QUARTER, WIDTH), bf16)
    slot_piece = struct((HALF_SLOTS, WIDTH), bf16)

    turned = jnp.concatenate(
        [jnp.moveaxis(projection_in, 1, 0).reshape(24, QKV), projection_out.T], axis=1
    )
    weights = sent_to_all(turned, EXPERT).reshape(WIDTH, QKV + CHANNELS)

    tagged = struct((QUARTER, TAGGED), bf16)
    n0, n1 = call(start_kernel, (tagged, tagged), (inputs, gain1, segments), name="start")
    place, c_slots = call(
        place_kernel,
        (struct((rows, SLOTS), bf16), struct((SLOTS, width), bf16)),
        (routes, upstream),
        name="place",
    )
    normed = (gather4(n0, 1), gather4(n1, -1))
    tiles = call(
        bias_kernel,
        struct((LOCAL_HEADS, len(TILE_STEPS), QUARTER, QUARTER), f32),
        (first_head, bias_table),
        [SMEM, SMEM],
        name="bias",
    )
    length = PARTS * QUARTER
    attended = [
        call(
            attend_kernel,
            (
                struct((length, TAGGED), bf16),
                struct((length, QKV), bf16),
                struct((length, CHANNELS), bf16),
                struct((length, 128), f32),
                piece, piece, piece, piece,
            ),
            (me, *normed[s], weights, after(tiles, place)),
            [SMEM] + [VMEM] * 6,
            flops=2 * 10**9,
            name="attend",
        )
        for s in range(2)
    ]
    attention = [reduce4(attended[s][4:], (1, -1)[s]) for s in range(2)]

    c_slots = by_expert(to_experts(after(c_slots, attended[0][4], attended[1][4])))
    c_all = [gather4(c, (1, -1)[e]) for e, c in enumerate(c_slots)]
    u = [
        call(
            upstream_kernel,
            struct((PARTS, HALF_SLOTS, WIDTH), bf16),
            (*c_all[e], expert_out),
            [VMEM] * 4 + [expert_spec(e)],
            flops=12 * 10**8,
            name="upstream",
        )
        for e in range(2)
    ]

    hidden, gate, slots = call(
        dispatch_kernel,
        (struct((rows, width), f32), struct((rows, 128), f32), struct((SLOTS, width), bf16)),
        (inputs, *attention[0], *attention[1], gain2, router_weight, routes, place),
        name="dispatch",
    )
    x_slots = [after(x, c_all[0][2], c_all[1][2]) for x in by_expert(to_experts(slots))]
    x_all = [gather4(x, (1, -1)[e]) for e, x in enumerate(x_slots)]
    group = lax.axis_index(EXPERT).astype(jnp.int32)
    acts = struct((PARTS, HALF_SLOTS, WIDTH), bf16)
    pair = pl.BlockSpec((2, HALF_SLOTS, WIDTH), lambda i: (i, 0, 0))
    worked = []
    for e in range(2):
        u_here = after(u[1], worked[0][4]) if e else u[0]
        outs = pl.pallas_call(
            expert_kernel,
            grid=(2,),
            out_shape=(acts, acts, acts, struct((2 * EXPERTS, WIDTH), f32)) + (slot_piece,) * 4,
            in_specs=[SMEM] + [VMEM] * 4 + [pair, expert_spec(e), VMEM],
            out_specs=(pair, pair, pair) + (VMEM,) * 5,
            scratch_shapes=[pltpu.VMEM((SLOTS, WIDTH), f32)],
            cost_estimate=pl.CostEstimate(
                flops=24 * 10**8, bytes_accessed=2 * 10**7, transcendentals=0
            ),
            compiler_params=pltpu.CompilerParams(vmem_limit_bytes=VMEM_LIMIT),
            name="expert",
        )((group * 2 + e).reshape(1), *x_all[e], u_here, expert_in, router_weight)
        worked.append(outs)
    outputs = [
        call(
            output_kernel,
            (slot_piece,) * 4,
            (worked[e][0], expert_out),
            [VMEM, expert_spec(e)],
            flops=12 * 10**8,
            name="expert_output",
        )
        for e in range(2)
    ]
    whole = struct((2, WIDTH, WIDTH), f32)
    expert_grads, tokens = (), []
    for e in range(2):
        ins = (worked[e][1], worked[e][2], *c_all[e], *x_all[e])
        *expert_grads, token = pl.pallas_call(
            weights_kernel,
            grid=(1,),
            out_shape=(whole, whole, struct((8, 128), f32)),
            in_specs=[VMEM] * 10 + [pl.BlockSpec(memory_space=pl.ANY)] * len(expert_grads),
            out_specs=(expert_spec(e), expert_spec(e), VMEM),
            input_output_aliases={10: 0, 11: 1} if expert_grads else {},
            cost_estimate=pl.CostEstimate(
                flops=24 * 10**8, bytes_accessed=2 * 10**7, transcendentals=0
            ),
            compiler_params=pltpu.CompilerParams(vmem_limit_bytes=VMEM_LIMIT),
            name="expert_weights",
        )(*ins, *expert_grads)
        tokens.append(token)
    grad_expert_out, grad_expert_in = expert_grads

    own, near, far, left = worked[1][4:]
    left = after(left, outputs[0][0], outputs[1][0])
    own = after(own, tokens[0])
    slot_terms = [reduce4(worked[0][4:], 1), reduce4((own, near, far, left), -1)]
    slot_sums = summed_slots(slot_terms)
    returned = to_experts(slot_sums)
    returned = after(returned, tokens[1])
    output_slots = summed_slots(
        [
            reduce4([after(piece, slot_sums) for piece in outputs[e]], (1, -1)[e])
            for e in range(2)
        ]
    )
    hidden_grad, h0, h1, gain2_grad = call(
        back_kernel,
        (struct((rows, width), f32), piece, piece, struct((1, width), f32)),
        (returned.reshape(SLOTS, width), place, hidden, upstream, gain2),
        name="back",
    )
    grads = (gather4(h0, 1), gather4(h1, -1))
    attended_back = [
        call(
            attend_back_kernel,
            (
                struct((length, width), bf16),
                struct((length, QKV), bf16),
                struct((LOCAL_HEADS, BUCKETS, 128), f32),
                struct((1, width), f32),
                piece, piece, piece, piece,
            ),
            (me, *grads[s], weights, tiles, *attended[s][:2], attended[s][3]),
            [SMEM] + [VMEM] * 9,
            scratch=[pltpu.VMEM((LOCAL_HEADS, len(TILE_STEPS), QUARTER, QUARTER), f32)],
            flops=4 * 10**9,
            name="attend_back",
        )
        for s in range(2)
    ]
    normed_grad = [reduce4(attended_back[s][4:], (1, -1)[s]) for s in range(2)]
    input_grad = call(
        input_kernel,
        struct(inputs.shape, f32),
        (inputs, gain1, hidden_grad, *normed_grad[0], *normed_grad[1]),
        name="input_gradient",
    )

    router = worked[0][3] + worked[1][3]
    router = (router[:EXPERTS] + router[EXPERTS:]).T.astype(bf16).reshape(32, 16, 96)
    router = jnp.pad(router, ((0, 0), (0, 0), (0, 32)))
    output_slots = jnp.concatenate([output_slots, router], axis=2)
    output_back = to_experts(after(output_slots, h0))
    router_rows = jnp.sum(output_back[:, :, width : width + 96].astype(f32), axis=0)
    result = call(
        result_kernel,
        struct((rows, width), f32),
        (output_back[:, :, :width].reshape(SLOTS, width), place, hidden, gate),
        name="result",
    )
    partial = call(
        projection_kernel,
        struct((WIDTH, QKV + CHANNELS), bf16),
        (
            attended[0][0], attended[1][0], attended_back[0][1], attended_back[1][1],
            attended_back[0][0], attended_back[1][0], attended[0][2], attended[1][2],
        ),
        flops=16 * 10**8,
        name="projection_gradient",
    )
    table_local = jnp.sum(attended_back[0][2] + attended_back[1][2], axis=-1).T
    table = lax.dynamic_update_slice(
        jnp.zeros((BUCKETS, HEADS), f32), table_local, (0, first_head[0])
    )
    gain1_grad = (attended_back[0][3] + attended_back[1][3]) / gain1
    small = jnp.concatenate(
        [t.reshape(-1) for t in (router_rows, gain1_grad, gain2_grad, table)]
    ).reshape(27, 128)
    small = added(small, shift(small, 1), shift(small, -1), shift(small, 2)).reshape(-1)
    lines = jnp.pad(small.astype(bf16), (0, 5 * width - small.size)).reshape(1, 5, width)
    lines = jnp.concatenate(
        [partial.reshape(32, 24, width), jnp.broadcast_to(lines, (32, 5, width))], axis=1
    )
    arrived = lax.all_to_all(lines, EXPERT, 0, 0, tiled=True)
    projections = jnp.sum(arrived[:, :24].astype(f32), axis=0)
    grad_projection_in = jnp.moveaxis(projections[:, :QKV].reshape(24, 3, CHANNELS), 1, 0)
    grad_projection_out = projections[:, QKV:].T
    grad_router = arrived[:, 24:26].astype(f32).reshape(WIDTH, EXPERTS)
    late = jnp.sum(arrived[:, 26:].astype(f32), axis=0).reshape(-1)
    grad_gain_attention = late[:width]
    grad_gain_experts = late[width : 2 * width]
    grad_table = late[2 * width : 2 * width + BUCKETS * HEADS].reshape(BUCKETS, HEADS)
    return (
        result.reshape(seq_here, quarter, width),
        input_grad,
        grad_projection_in,
        grad_projection_out,
        grad_gain_attention,
        grad_gain_experts,
        grad_router,
        grad_table,
        grad_expert_in,
        grad_expert_out,
    )


def solution(mesh):
    split = Mesh(
        mesh.devices.reshape(4, 4, 2, mesh.shape["mp"]), ("expert_0", "expert_1", "expert_2", "mp")
    )
    in_specs = (
        P(EXPERT, "mp", None),
        P(None, EXPERT, "mp"),
        P("mp", EXPERT),
        P(),
        P(),
        P(),
        P(),
        P(EXPERT, None, "mp"),
        P(EXPERT, "mp", None),
        P(EXPERT, "mp", None),
        P(EXPERT, "mp"),
        P(EXPERT, "mp", None),
    )
    out_specs = (
        P(EXPERT, "mp", None),
        P(EXPERT, "mp", None),
        P(None, EXPERT, "mp"),
        P("mp", EXPERT),
        P(),
        P(),
        P(),
        P(),
        P(EXPERT, None, "mp"),
        P(EXPERT, "mp", None),
    )
    return jax.shard_map(body, mesh=split, in_specs=in_specs, out_specs=out_specs, check_vma=False)
```

```python
import functools
import math

import jax
import jax.numpy as jnp
from jax import lax
from jax.experimental import pallas as pl
from jax.experimental.pallas import tpu as pltpu
from jax.sharding import Mesh
from jax.sharding import PartitionSpec as P

HEADS = 12
HEAD_DIM = 64
EXPERTS = 64
BUCKETS = 32
REACH = 128
EXPERT = ("expert_0", "expert_1", "expert_2")
QUARTER = 128
PARTS = 4
WIDTH = 768
CHANNELS = 192
LOCAL_HEADS = CHANNELS // HEAD_DIM
QKV = 3 * CHANNELS
CAPACITY = 4
SLOTS = 512
HALF_SLOTS = SLOTS // 2
TAGGED = WIDTH + 128
TILE_STEPS = (0, 1, -1, 2, -2)

epsilon = 1e-06
f32 = jnp.float32
bf16 = jnp.bfloat16
BLOCK = 512
VMEM_LIMIT = 56 * 1024 * 1024


def dot(a, b, ca=1, cb=0, precision=None):
    return lax.dot_general(
        a, b, (((ca,), (cb,)), ((), ())), preferred_element_type=f32, precision=precision
    )


def struct(shape, dtype):
    return jax.ShapeDtypeStruct(shape, dtype)


ANY = pl.BlockSpec(memory_space=pl.ANY)
SMEM = pl.BlockSpec(memory_space=pltpu.SMEM)
VMEM = pl.BlockSpec(memory_space=pltpu.VMEM)


def call(kernel, outs, ins, in_specs=None, scratch=(), flops=10**8, moved=4 * 10**6, name=None):
    return pl.pallas_call(
        kernel,
        grid=(1,),
        out_shape=outs,
        in_specs=in_specs or [VMEM] * len(ins),
        out_specs=jax.tree.map(lambda _: VMEM, outs),
        scratch_shapes=scratch,
        cost_estimate=pl.CostEstimate(flops=flops, bytes_accessed=moved, transcendentals=0),
        compiler_params=pltpu.CompilerParams(vmem_limit_bytes=VMEM_LIMIT),
        name=name,
    )(*ins)


def shift(x, step):
    return lax.ppermute(x, "mp", [(i, (i + step) % PARTS) for i in range(PARTS)])


def gather4(x):
    left, right = shift(x, 1), shift(x, -1)
    return x, right, left, (shift(left[0], 1), shift(right[1], -1))


def added(*terms):
    return functools.reduce(lambda a, b: a + b, [t.astype(f32) for t in terms])


def reduce4(pieces, way):
    own, right, far, left = pieces
    if way > 0:
        right = added(right, shift(far, 1)).astype(bf16)
    else:
        left = added(left, shift(far, -1)).astype(bf16)
    return own, shift(right, 1), shift(left, -1)


def to_experts(x):
    return lax.all_to_all(x.reshape(32, -1, x.shape[-1]), EXPERT, 0, 0, tiled=True)


def by_expert(lines):
    halves = jnp.moveaxis(lines.reshape(32, 2, 8, lines.shape[-1]), 1, 0)
    return halves.reshape(2, HALF_SLOTS, lines.shape[-1])


def summed_slots(terms):
    pieces = [added(*terms[e]).astype(bf16).reshape(32, 8, WIDTH) for e in range(2)]
    return jnp.concatenate(pieces, axis=1)


def sent_to_all(x, axis):
    peers = lax.axis_size(axis)
    return lax.all_to_all(jnp.broadcast_to(x[None], (peers, *x.shape)), axis, 0, 0, tiled=True)


def bucket_of(offsets):
    halfway = BUCKETS // 2
    exact_span = halfway // 2
    distance = jnp.abs(offsets)
    far_part = jnp.full_like(distance, exact_span)
    for step in range(1, exact_span):
        cutoff_level = math.ceil(exact_span * (REACH / exact_span) ** (step / exact_span) - 1e-09)
        far_part = far_part + jnp.where(distance >= cutoff_level, 1, 0)
    nearby = jnp.where(distance < exact_span, distance, far_part)
    return nearby + jnp.where(offsets > 0, halfway, 0)


def tile_buckets(step):
    shape = (QUARTER, QUARTER)
    offsets = (
        step * QUARTER
        + lax.broadcasted_iota(jnp.int32, shape, 1)
        - lax.broadcasted_iota(jnp.int32, shape, 0)
    )
    return bucket_of(offsets)


def possible(step):
    if step == 0:
        return range(BUCKETS)
    if step == 1:
        return range(BUCKETS // 2 + 1, BUCKETS)
    if step == -1:
        return range(1, BUCKETS // 2)
    return (BUCKETS - 1,) if step > 0 else (BUCKETS // 2 - 1,)


def tile_at(row_block, key_block):
    step = key_block - row_block
    return TILE_STEPS.index(max(-2, min(2, step)))


def bias_kernel(head_ref, table_ref, out_ref):
    head = head_ref[0]
    for t, step in enumerate(TILE_STEPS):
        buckets = tile_buckets(step)
        tiles = [jnp.zeros((QUARTER, QUARTER), f32)] * LOCAL_HEADS
        for b in possible(step):
            mask = buckets == b
            tiles = [jnp.where(mask, table_ref[b, head + h], tile) for h, tile in enumerate(tiles)]
        for h, tile in enumerate(tiles):
            out_ref[h, t] = tile


def inverse_size(values):
    return lax.rsqrt(jnp.mean(values * values, axis=-1, keepdims=True) + epsilon)


def as_column(row):
    return jnp.transpose(jnp.broadcast_to(row, (QUARTER, QUARTER)))


def start_kernel(x_ref, gain_ref, seg_ref, n_ref):
    gain = gain_ref[...]
    for s in range(2):
        x = x_ref[s]
        n_ref[s, :, :WIDTH] = (x * inverse_size(x) * gain).astype(bf16)
        n_ref[s, :, WIDTH:] = as_column(seg_ref[s : s + 1].astype(f32)).astype(bf16)


def place_kernel(route_ref, cot_ref, _, __, place_ref, c_ref):
    tri = (
        lax.broadcasted_iota(jnp.int32, (QUARTER, QUARTER), 0)
        >= lax.broadcasted_iota(jnp.int32, (QUARTER, QUARTER), 1)
    ).astype(bf16)
    for s in range(2):
        chosen = as_column(route_ref[s : s + 1].astype(f32)).astype(jnp.int32)
        mask = jnp.where(
            chosen == lax.broadcasted_iota(jnp.int32, (QUARTER, QUARTER), 1), 1.0, 0.0
        )
        running = dot(tri, mask.astype(bf16))
        rank = jnp.sum(mask * running, axis=-1, keepdims=True).astype(jnp.int32) - 1
        place = chosen[:, :1] * 8 + s * CAPACITY + rank
        slots = lax.broadcasted_iota(jnp.int32, (QUARTER, SLOTS), 1)
        place_ref[s * QUARTER : (s + 1) * QUARTER] = jnp.where(slots == place, 1.0, 0.0).astype(bf16)
    c_ref[...] = dot(place_ref[...], cot_ref[...].astype(bf16), 0, 0).astype(bf16)


def position(me, k):
    return pl.multiple_of(lax.rem(me + k, PARTS) * QUARTER, QUARTER)


def same_document(g_ref):
    column = g_ref[:, WIDTH:].astype(f32)
    return column, jnp.transpose(column)[:1]


def bias_rows(tiles_ref, h, i):
    per = BLOCK // QUARTER
    return jnp.concatenate(
        [
            jnp.concatenate([tiles_ref[h, tile_at(r, j)] for j in range(PARTS)], axis=1)
            for r in range(i * per, (i + 1) * per)
        ],
        axis=0,
    )


def attend_kernel(
    me_ref, a0, a1, a2, a3, w_ref, tiles_ref, g_ref, qkv_ref, att_ref, lse_ref, p0, p1, p2, p3
):
    me = me_ref[0]
    for k, piece in enumerate((a0, a1, a2, a3)):
        g_ref[pl.ds(position(me, k), QUARTER), :] = piece[...].reshape(QUARTER, TAGGED)
    qkv_ref[...] = dot(g_ref[:, :WIDTH], w_ref[:, :QKV]).astype(bf16)
    column, row = same_document(g_ref)
    lse_ref[...] = jnp.zeros_like(lse_ref)
    for h in range(LOCAL_HEADS):
        lo = h * HEAD_DIM
        key = qkv_ref[:, CHANNELS + lo : CHANNELS + lo + HEAD_DIM]
        value = qkv_ref[:, 2 * CHANNELS + lo : 2 * CHANNELS + lo + HEAD_DIM]
        for i in range(PARTS * QUARTER // BLOCK):
            rows = slice(i * BLOCK, (i + 1) * BLOCK)
            query = qkv_ref[rows, lo : lo + HEAD_DIM] * HEAD_DIM ** (-0.5)
            scores = dot(query, key, 1, 1) + bias_rows(tiles_ref, h, i)
            scores = jnp.where(column[rows, :1] == row, scores, -1000000000.0)
            row_max = jnp.max(scores, axis=-1, keepdims=True)
            expos = jnp.exp(scores - row_max)
            total = jnp.sum(expos, axis=-1, keepdims=True)
            weights = (expos * (1.0 / total)).astype(bf16)
            att_ref[rows, lo : lo + HEAD_DIM] = dot(weights, value).astype(bf16)
            lse_ref[rows, h : h + 1] = row_max + jnp.log(total)
    for k, out in enumerate((p0, p1, p2, p3)):
        mine = att_ref[pl.ds(position(me, k), QUARTER), :]
        out[...] = dot(mine, w_ref[:, QKV:], 1, 1).astype(bf16)


def dispatch_kernel(
    x_ref, t00, t01, t02, t10, t11, t12, gain_ref, router_ref, route_ref, place_ref, _,
    hidden_ref, gate_ref, slots_ref,
):
    for s, terms in ((0, (t00, t01, t02)), (1, (t10, t11, t12))):
        rows = slice(s * QUARTER, (s + 1) * QUARTER)
        hidden_ref[rows] = x_ref[s] + added(*[t[...] for t in terms])
    hidden = hidden_ref[...]
    mixed = hidden * inverse_size(hidden) * gain_ref[...]
    low = mixed.astype(bf16)
    slots_ref[...] = dot(place_ref[...], low, 0, 0).astype(bf16)
    logits = dot(mixed, router_ref[...], precision=lax.Precision.HIGHEST)
    expos = jnp.exp(logits - jnp.max(logits, axis=-1, keepdims=True))
    shares = expos / jnp.sum(expos, axis=-1, keepdims=True)
    for s in range(2):
        rows = slice(s * QUARTER, (s + 1) * QUARTER)
        chosen = as_column(route_ref[s : s + 1].astype(f32)).astype(jnp.int32)[:, :EXPERTS]
        mask = chosen == lax.broadcasted_iota(jnp.int32, (QUARTER, EXPERTS), 1)
        gate = jnp.sum(jnp.where(mask, shares[rows], 0.0), axis=-1, keepdims=True)
        gate_ref[rows] = jnp.broadcast_to(gate, (QUARTER, 128))


WORK_ORDER = (2, 1, 3, 0)


def expert_kernel(
    at_ref, x0, x1, x2, x3, c_ref, w_ref, w_out_ref, router_ref, _,
    active_ref, scaled_ref, grad_ref, logit_ref, s0, s1, s2, s3, pre_ref, u_ref,
):
    own, me = at_ref[0], at_ref[1]
    router = router_ref[...]
    router_hi = router.astype(bf16)
    router_lo = (router - router_hi.astype(f32)).astype(bf16)
    router_both = jnp.concatenate([router_hi, router_lo], axis=1)
    c = math.sqrt(2.0 / math.pi)
    ca = c * 0.044715

    def work(pieces, outs, first):
        x = jnp.concatenate([x_ref[...].reshape(HALF_SLOTS, WIDTH) for x_ref, _ in pieces])
        up = jnp.concatenate([c_ref[lax.rem(me + k, PARTS), 0] for _, k in pieces])
        u_ref[...] = dot(up, w_out_ref[0], 1, 1)
        logits = dot(x, router_both)
        logits = logits[:, :EXPERTS] + logits[:, EXPERTS:]
        expos = jnp.exp(logits - jnp.max(logits, axis=-1, keepdims=True))
        shares = expos / jnp.sum(expos, axis=-1, keepdims=True)
        chosen = jnp.where(lax.broadcasted_iota(jnp.int32, shares.shape, 1) == own, 1.0, 0.0)
        gate = jnp.sum(shares * chosen, axis=-1, keepdims=True)
        pre_ref[...] = dot(x, w_ref[0])
        gate_grads = []
        for n in range(2):
            for part in range(HALF_SLOTS // 64):
                rows = slice(part * 64, part * 64 + 64)
                at = slice(n * HALF_SLOTS + part * 64, n * HALF_SLOTS + part * 64 + 64)
                pre = pre_ref[at, :]
                u = u_ref[at, :]
                square = pre * pre
                t = jnp.tanh(pre * (c + ca * square))
                half = 0.5 + 0.5 * t
                active = pre * half
                slope = half + (0.5 * pre) * (1.0 - t * t) * (c + 3.0 * ca * square)
                gate_grads.append(jnp.sum(active * u, axis=-1, keepdims=True))
                active_ref[n, rows, :] = active.astype(bf16)
                scaled_ref[n, rows, :] = (gate[at] * active).astype(bf16)
                grad_ref[n, rows, :] = (gate[at] * u * slope).astype(bf16)
        logit_grad = shares * (chosen - gate) * jnp.concatenate(gate_grads)
        logit_hi = logit_grad.astype(bf16)
        logit_lo = (logit_grad - logit_hi.astype(f32)).astype(bf16)
        pre_grad = jnp.concatenate([grad_ref[0], grad_ref[1]])
        slot_grad = dot(pre_grad, w_ref[0], 1, 1) + dot(logit_hi, router_hi, 1, 1)
        for n, out in enumerate(outs):
            out[...] = slot_grad[n * HALF_SLOTS : (n + 1) * HALF_SLOTS].astype(bf16)
        term = dot(jnp.concatenate([logit_hi, logit_lo], axis=1), x, 0, 0)
        if first:
            logit_ref[...] = term
        else:
            logit_ref[...] += term

    pl.when(pl.program_id(0) == 0)(lambda: work(((x2, 2), (x1, 1)), (s2, s1), True))
    pl.when(pl.program_id(0) == 1)(lambda: work(((x3, 3), (x0, 0)), (s3, s0), False))


def output_kernel(me_ref, active0, active1, w_ref, out_ref):
    me = me_ref[0]

    def work(active_ref):
        for n, k in enumerate(WORK_ORDER):
            out_ref[lax.rem(me + k, PARTS), 0] = dot(active_ref[n], w_ref[0]).astype(bf16)

    pl.when(pl.program_id(0) == 0)(lambda: work(active0))
    pl.when(pl.program_id(0) == 1)(lambda: work(active1))


def weights_kernel(me_ref, scaled_ref, grad_ref, c_ref, x0, x1, x2, x3, *rest):
    out_ref, in_ref, token_ref = rest[-3:]
    me = me_ref[0]
    token_ref[...] = jnp.zeros_like(token_ref)
    entered = (x0, x1, x2, x3)
    for n, k in enumerate(WORK_ORDER):
        x = entered[k][...].reshape(HALF_SLOTS, WIDTH)
        out_term = dot(scaled_ref[n], c_ref[lax.rem(me + k, PARTS), 0], 0, 0)
        in_term = dot(x, grad_ref[n], 0, 0)
        if n == 0:
            out_ref[0] = out_term
            in_ref[0] = in_term
        else:
            out_ref[0] += out_term
            in_ref[0] += in_term


def back_kernel(
    slots_ref, place_ref, hidden_ref, cot_ref, gain_ref, _, grad_ref, h_ref, gain_grad_ref
):
    mixed_grad = dot(place_ref[...], slots_ref[...])
    hidden = hidden_ref[...]
    r = inverse_size(hidden)
    gain_grad_ref[...] = jnp.sum(mixed_grad * hidden * r, axis=0, keepdims=True)
    u = gain_ref[...] * mixed_grad
    grad = cot_ref[...] + r * u - hidden * (r * r * r * jnp.mean(hidden * u, axis=-1, keepdims=True))
    grad_ref[...] = grad
    h_ref[0] = grad[:QUARTER].astype(bf16)
    h_ref[1] = grad[QUARTER:].astype(bf16)


def result_kernel(slots_ref, place_ref, hidden_ref, gate_ref, out_ref):
    back = dot(place_ref[...], slots_ref[...])
    out_ref[...] = hidden_ref[...] + gate_ref[:, :1] * back


def attend_back_kernel(
    me_ref, a0, a1, a2, a3, w_ref, tiles_ref, g_ref, qkv_ref, lse_ref,
    up_ref, dqkv_ref, sums_ref, gain_ref, out_ref, tile_sums,
):
    me = me_ref[0]
    for k, piece in enumerate((a0, a1, a2, a3)):
        up_ref[pl.ds(position(me, k), QUARTER), :] = piece[...].reshape(QUARTER, WIDTH)
    att_grad = dot(up_ref[...], w_ref[:, QKV:]).astype(bf16)
    column, row = same_document(g_ref)
    tile_sums[...] = jnp.zeros_like(tile_sums)
    for h in range(LOCAL_HEADS):
        lo = h * HEAD_DIM
        key = qkv_ref[:, CHANNELS + lo : CHANNELS + lo + HEAD_DIM]
        value = qkv_ref[:, 2 * CHANNELS + lo : 2 * CHANNELS + lo + HEAD_DIM]
        key_grad = jnp.zeros((HEAD_DIM, PARTS * QUARTER), f32)
        value_grad = jnp.zeros((HEAD_DIM, PARTS * QUARTER), f32)
        for i in range(PARTS * QUARTER // BLOCK):
            rows = slice(i * BLOCK, (i + 1) * BLOCK)
            query = qkv_ref[rows, lo : lo + HEAD_DIM] * HEAD_DIM ** (-0.5)
            scores = dot(query, key, 1, 1) + bias_rows(tiles_ref, h, i)
            scores = jnp.where(column[rows, :1] == row, scores, -1000000000.0)
            weights = jnp.exp(scores - lse_ref[rows, h : h + 1])
            out_grad = att_grad[rows, lo : lo + HEAD_DIM]
            weights_grad = dot(out_grad, value, 1, 1)
            inner = jnp.sum(weights * weights_grad, axis=-1, keepdims=True)
            score_grad = (weights * (weights_grad - inner)).astype(bf16)
            wide = score_grad.astype(f32)
            for r in range(BLOCK // QUARTER):
                for j in range(PARTS):
                    tile_sums[h, tile_at(i * (BLOCK // QUARTER) + r, j)] += wide[
                        r * QUARTER : (r + 1) * QUARTER, j * QUARTER : (j + 1) * QUARTER
                    ]
            dqkv_ref[rows, lo : lo + HEAD_DIM] = (
                dot(score_grad, key) * HEAD_DIM ** (-0.5)
            ).astype(bf16)
            key_grad += dot(query, score_grad, 0, 0)
            value_grad += dot(out_grad, weights.astype(bf16), 0, 0)
        dqkv_ref[:, CHANNELS + lo : CHANNELS + lo + HEAD_DIM] = jnp.transpose(key_grad).astype(bf16)
        dqkv_ref[:, 2 * CHANNELS + lo : 2 * CHANNELS + lo + HEAD_DIM] = jnp.transpose(
            value_grad
        ).astype(bf16)
    normed_grad = dot(dqkv_ref[...], w_ref[:, :QKV], 1, 1)
    out_ref[...] = normed_grad.astype(bf16)
    gain_ref[...] = jnp.sum(normed_grad * g_ref[:, :WIDTH].astype(f32), axis=0, keepdims=True)
    sums_ref[...] = jnp.zeros_like(sums_ref)
    for t, step in enumerate(TILE_STEPS):
        buckets = tile_buckets(step)
        for b in possible(step):
            mask = buckets == b
            for h in range(LOCAL_HEADS):
                sums_ref[h, b : b + 1] += jnp.sum(
                    jnp.where(mask, tile_sums[h, t], 0.0), axis=0, keepdims=True
                )


def projection_kernel(g0, g1, d0, d1, u0, u1, a0, a1, out_ref):
    out_ref[:, :QKV] = dot(g0[:, :WIDTH], d0[...], 0, 0) + dot(g1[:, :WIDTH], d1[...], 0, 0)
    out_ref[:, QKV:] = dot(u0[...], a0[...], 0, 0) + dot(u1[...], a1[...], 0, 0)


def lines_kernel(partial_ref, small_ref, out_ref):
    small = small_ref[...]
    for n in range(32):
        rows = partial_ref[24 * n : 24 * n + 24]
        out_ref[n] = jnp.concatenate([rows, small]).astype(bf16)


def input_kernel(x_ref, gain_ref, grad_ref, t0, t1, out_ref):
    for s, term in ((0, t0), (1, t1)):
        x = x_ref[s]
        r = inverse_size(x)
        u = gain_ref[...] * term[...].astype(f32)
        out_ref[s] = (
            grad_ref[s * QUARTER : (s + 1) * QUARTER]
            + r * u
            - x * (r * r * r * jnp.mean(x * u, axis=-1, keepdims=True))
        )


def half_spec(n, array):
    return pl.BlockSpec((1, *array.shape[1:]), lambda i: (n, 0, 0))


def expert_spec(e):
    return pl.BlockSpec((1, WIDTH, WIDTH), lambda i: (e, 0, 0))


def body(
    inputs,
    projection_in,
    projection_out,
    gain_attention,
    gain_experts,
    router_weight,
    bias_table,
    expert_in,
    expert_out,
    routes,
    segments,
    cotangent,
):
    seq_here, quarter, width = inputs.shape
    rows = seq_here * quarter
    me = lax.axis_index("mp").reshape(1).astype(jnp.int32)
    first_head = me * LOCAL_HEADS
    gain1, gain2 = gain_attention.reshape(1, width), gain_experts.reshape(1, width)
    routes = routes.reshape(seq_here, quarter)
    upstream = cotangent.reshape(rows, width)
    piece = struct((QUARTER, WIDTH), bf16)
    slot_piece = struct((HALF_SLOTS, WIDTH), bf16)

    turned = jnp.concatenate(
        [jnp.moveaxis(projection_in, 1, 0).reshape(24, QKV), projection_out.T], axis=1
    )
    weights = sent_to_all(turned, EXPERT).reshape(WIDTH, QKV + CHANNELS)

    normed = call(
        start_kernel,
        struct((seq_here, QUARTER, TAGGED), bf16),
        (inputs, gain1, segments),
        name="start",
    )
    n_own, n_right, n_left, n_far = gather4(normed)
    tiles = call(
        bias_kernel,
        struct((LOCAL_HEADS, len(TILE_STEPS), QUARTER, QUARTER), f32),
        (first_head, bias_table),
        [SMEM, SMEM],
        name="bias",
    )
    length = PARTS * QUARTER
    attended = [
        call(
            attend_kernel,
            (
                struct((length, TAGGED), bf16),
                struct((length, QKV), bf16),
                struct((length, CHANNELS), bf16),
                struct((length, 128), f32),
                piece, piece, piece, piece,
            ),
            (me, n_own, n_right, n_far[s], n_left, weights, tiles),
            [SMEM, half_spec(s, n_own), half_spec(s, n_own), VMEM, half_spec(s, n_own), VMEM, VMEM],
            flops=2 * 10**9,
            name="attend",
        )
        for s in range(2)
    ]
    attention = [reduce4(attended[s][4:], (1, -1)[s]) for s in range(2)]

    place, c_slots = call(
        place_kernel,
        (struct((rows, SLOTS), bf16), struct((SLOTS, width), bf16)),
        (routes, upstream, attended[0][4], attended[1][4]),
        [VMEM, VMEM, ANY, ANY],
        name="place",
    )
    c_lines = to_experts(c_slots)
    c_all = lax.all_gather(by_expert(c_lines), "mp", axis=0)

    hidden, gate, slots = call(
        dispatch_kernel,
        (struct((rows, width), f32), struct((rows, 128), f32), struct((SLOTS, width), bf16)),
        (inputs, *attention[0], *attention[1], gain2, router_weight, routes, place, c_lines),
        [VMEM] * 11 + [ANY],
        name="dispatch",
    )
    x_own, x_right, x_left, x_far = gather4(by_expert(to_experts(slots)))
    group = lax.axis_index(EXPERT).astype(jnp.int32)
    acts = struct((PARTS, HALF_SLOTS, WIDTH), bf16)
    pair = pl.BlockSpec((2, HALF_SLOTS, WIDTH), lambda i: (i, 0, 0))

    def quarter_spec(e):
        return pl.BlockSpec((PARTS, 1, HALF_SLOTS, WIDTH), lambda i: (0, e, 0, 0))

    def x_specs(e):
        return [expert_half[e], expert_half[e], VMEM, expert_half[e]]

    expert_half = [half_spec(e, x_own) for e in range(2)]
    worked = []
    for e in range(2):
        outs = pl.pallas_call(
            expert_kernel,
            grid=(2,),
            out_shape=(acts, acts, acts, struct((2 * EXPERTS, WIDTH), f32)) + (slot_piece,) * 4,
            in_specs=[SMEM, *x_specs(e), quarter_spec(e), expert_spec(e), expert_spec(e), VMEM, ANY],
            out_specs=(pair, pair, pair) + (VMEM,) * 5,
            scratch_shapes=[pltpu.VMEM((SLOTS, WIDTH), f32)] * 2,
            cost_estimate=pl.CostEstimate(
                flops=36 * 10**8, bytes_accessed=2 * 10**7, transcendentals=0
            ),
            compiler_params=pltpu.CompilerParams(vmem_limit_bytes=VMEM_LIMIT),
            name="expert",
        )(
            jnp.concatenate([(group * 2 + e).reshape(1), me]),
            x_own, x_right, x_far[e], x_left, c_all, expert_in, expert_out, router_weight,
            worked[0][4] if worked else x_own,
        )
        worked.append(outs)
    slot_terms = [reduce4(worked[0][4:], 1), reduce4(worked[1][4:], -1)]
    returned = to_experts(summed_slots(slot_terms))

    outputs = pl.pallas_call(
        output_kernel,
        grid=(2,),
        out_shape=struct((PARTS, 2, HALF_SLOTS, WIDTH), bf16),
        in_specs=[SMEM, VMEM, VMEM, pl.BlockSpec((1, WIDTH, WIDTH), lambda i: (i, 0, 0))],
        out_specs=pl.BlockSpec((PARTS, 1, HALF_SLOTS, WIDTH), lambda i: (0, i, 0, 0)),
        cost_estimate=pl.CostEstimate(flops=24 * 10**8, bytes_accessed=10**7, transcendentals=0),
        compiler_params=pltpu.CompilerParams(vmem_limit_bytes=VMEM_LIMIT),
        name="expert_output",
    )(me, worked[0][0], worked[1][0], expert_out)
    output_slots = lax.psum_scatter(
        outputs.reshape(PARTS * SLOTS, width), "mp", scatter_dimension=0, tiled=True
    )
    output_slots = jnp.moveaxis(output_slots.reshape(2, 32, 8, width), 0, 1).reshape(32, 16, width)

    whole = struct((2, WIDTH, WIDTH), f32)
    expert_grads, tokens = (), []
    for e in range(2):
        ins = (me, worked[e][1], worked[e][2], c_all, x_own, x_right, x_far[e], x_left)
        *expert_grads, token = pl.pallas_call(
            weights_kernel,
            grid=(1,),
            out_shape=(whole, whole, struct((8, 128), f32)),
            in_specs=[SMEM, VMEM, VMEM, quarter_spec(e), *x_specs(e)] + [ANY] * len(expert_grads),
            out_specs=(expert_spec(e), expert_spec(e), VMEM),
            input_output_aliases={8: 0, 9: 1} if expert_grads else {},
            cost_estimate=pl.CostEstimate(
                flops=24 * 10**8, bytes_accessed=2 * 10**7, transcendentals=0
            ),
            compiler_params=pltpu.CompilerParams(vmem_limit_bytes=VMEM_LIMIT),
            name="expert_weights",
        )(*ins, *expert_grads)
        tokens.append(token)
    grad_expert_out, grad_expert_in = expert_grads

    hidden_grad, low_grad, gain2_grad = call(
        back_kernel,
        (
            struct((rows, width), f32),
            struct((seq_here, QUARTER, width), bf16),
            struct((1, width), f32),
        ),
        (returned.reshape(SLOTS, width), place, hidden, upstream, gain2, tokens[0]),
        [VMEM] * 5 + [ANY],
        name="back",
    )
    h_own, h_right, h_left, h_far = gather4(low_grad)
    attended_back = [
        call(
            attend_back_kernel,
            (
                struct((length, width), bf16),
                struct((length, QKV), bf16),
                struct((LOCAL_HEADS, BUCKETS, 128), f32),
                struct((1, width), f32),
                struct((length, width), bf16),
            ),
            (me, h_own, h_right, h_far[s], h_left, weights, tiles, *attended[s][:2], attended[s][3]),
            [SMEM, half_spec(s, h_own), half_spec(s, h_own), VMEM, half_spec(s, h_own)] + [VMEM] * 5,
            scratch=[pltpu.VMEM((LOCAL_HEADS, len(TILE_STEPS), QUARTER, QUARTER), f32)],
            flops=4 * 10**9,
            name="attend_back",
        )
        for s in range(2)
    ]
    normed_grad = [
        lax.psum_scatter(attended_back[s][4], "mp", scatter_dimension=0, tiled=True)
        for s in range(2)
    ]
    input_grad = call(
        input_kernel,
        struct(inputs.shape, f32),
        (inputs, gain1, hidden_grad, *normed_grad),
        name="input_gradient",
    )

    router = worked[0][3] + worked[1][3]
    router = (router[:EXPERTS] + router[EXPERTS:]).T.astype(bf16).reshape(32, 16, 96)
    router = jnp.pad(router, ((0, 0), (0, 0), (0, 32)))
    output_slots = jnp.concatenate([output_slots, router], axis=2)
    output_back = to_experts(output_slots)
    router_rows = jnp.sum(output_back[:, :, width : width + 96].astype(f32), axis=0)
    result = call(
        result_kernel,
        struct((rows, width), f32),
        (output_back[:, :, :width].reshape(SLOTS, width), place, hidden, gate),
        name="result",
    )
    partial = call(
        projection_kernel,
        struct((WIDTH, QKV + CHANNELS), f32),
        (
            attended[0][0], attended[1][0], attended_back[0][1], attended_back[1][1],
            attended_back[0][0], attended_back[1][0], attended[0][2], attended[1][2],
        ),
        flops=16 * 10**8,
        name="projection_gradient",
    )
    table_local = jnp.sum(attended_back[0][2] + attended_back[1][2], axis=-1).T
    table = lax.dynamic_update_slice(
        jnp.zeros((BUCKETS, HEADS), f32), table_local, (0, first_head[0])
    )
    gain1_grad = (attended_back[0][3] + attended_back[1][3]) / gain1
    small = jnp.concatenate(
        [t.reshape(-1) for t in (router_rows, gain1_grad, gain2_grad, table)]
    ).reshape(27, 128)
    small = added(small, shift(small, 1), shift(small, -1), shift(small, 2)).reshape(-1)
    lines = call(
        lines_kernel,
        struct((32, 32, width), bf16),
        (partial, jnp.pad(small, (0, 8 * width - small.size)).reshape(8, width)),
        name="lines",
    )
    arrived = lax.all_to_all(lines, EXPERT, 0, 0, tiled=True)
    projections = jnp.sum(arrived[:, :24].astype(f32), axis=0)
    grad_projection_in = jnp.moveaxis(projections[:, :QKV].reshape(24, 3, CHANNELS), 1, 0)
    grad_projection_out = projections[:, QKV:].T
    grad_router = arrived[:, 24:26].astype(f32).reshape(WIDTH, EXPERTS)
    late = jnp.sum(arrived[:, 26:29].astype(f32), axis=0).reshape(-1)
    grad_gain_attention = late[:width]
    grad_gain_experts = late[width : 2 * width]
    grad_table = late[2 * width : 2 * width + BUCKETS * HEADS].reshape(BUCKETS, HEADS)
    return (
        result.reshape(seq_here, quarter, width),
        input_grad,
        grad_projection_in,
        grad_projection_out,
        grad_gain_attention,
        grad_gain_experts,
        grad_router,
        grad_table,
        grad_expert_in,
        grad_expert_out,
    )


def solution(mesh):
    split = Mesh(
        mesh.devices.reshape(4, 4, 2, mesh.shape["mp"]), ("expert_0", "expert_1", "expert_2", "mp")
    )
    in_specs = (
        P(EXPERT, "mp", None),
        P(None, EXPERT, "mp"),
        P("mp", EXPERT),
        P(),
        P(),
        P(),
        P(),
        P(EXPERT, None, "mp"),
        P(EXPERT, "mp", None),
        P(EXPERT, "mp", None),
        P(EXPERT, "mp"),
        P(EXPERT, "mp", None),
    )
    out_specs = (
        P(EXPERT, "mp", None),
        P(EXPERT, "mp", None),
        P(None, EXPERT, "mp"),
        P("mp", EXPERT),
        P(),
        P(),
        P(),
        P(),
        P(EXPERT, None, "mp"),
        P(EXPERT, "mp", None),
    )
    return jax.shard_map(body, mesh=split, in_specs=in_specs, out_specs=out_specs, check_vma=False)
```

```python
import functools
import math

import jax
import jax.numpy as jnp
from jax import lax
from jax.experimental import pallas as pl
from jax.experimental.pallas import tpu as pltpu
from jax.sharding import Mesh
from jax.sharding import PartitionSpec as P

HEADS = 12
HEAD_DIM = 64
EXPERTS = 64
BUCKETS = 32
REACH = 128
EXPERT = ("expert_0", "expert_1", "expert_2")
QUARTER = 128
PARTS = 4
WIDTH = 768
CHANNELS = 192
LOCAL_HEADS = CHANNELS // HEAD_DIM
QKV = 3 * CHANNELS
CAPACITY = 4
SLOTS = 512
HALF_SLOTS = SLOTS // 2
TAGGED = WIDTH + 128
TILE_STEPS = (0, 1, -1, 2, -2)

epsilon = 1e-06
f32 = jnp.float32
bf16 = jnp.bfloat16
BLOCK = 512
VMEM_LIMIT = 56 * 1024 * 1024


def dot(a, b, ca=1, cb=0, precision=None):
    return lax.dot_general(
        a, b, (((ca,), (cb,)), ((), ())), preferred_element_type=f32, precision=precision
    )


def struct(shape, dtype):
    return jax.ShapeDtypeStruct(shape, dtype)


ANY = pl.BlockSpec(memory_space=pl.ANY)
SMEM = pl.BlockSpec(memory_space=pltpu.SMEM)
VMEM = pl.BlockSpec(memory_space=pltpu.VMEM)


def call(kernel, outs, ins, in_specs=None, scratch=(), flops=10**8, moved=4 * 10**6, name=None):
    return pl.pallas_call(
        kernel,
        grid=(1,),
        out_shape=outs,
        in_specs=in_specs or [VMEM] * len(ins),
        out_specs=jax.tree.map(lambda _: VMEM, outs),
        scratch_shapes=scratch,
        cost_estimate=pl.CostEstimate(flops=flops, bytes_accessed=moved, transcendentals=0),
        compiler_params=pltpu.CompilerParams(vmem_limit_bytes=VMEM_LIMIT),
        name=name,
    )(*ins)


def shift(x, step):
    return lax.ppermute(x, "mp", [(i, (i + step) % PARTS) for i in range(PARTS)])


def gather4(x, way):
    left, right = shift(x, 1), shift(x, -1)
    far = shift(left, 1) if way > 0 else shift(right, -1)
    return x, right, far, left


def added(*terms):
    return functools.reduce(lambda a, b: a + b, [t.astype(f32) for t in terms])


def reduce4(pieces, way):
    own, right, far, left = pieces
    if way > 0:
        right = added(right, shift(far, 1)).astype(bf16)
    else:
        left = added(left, shift(far, -1)).astype(bf16)
    return own, shift(right, 1), shift(left, -1)


def to_experts(x):
    return lax.all_to_all(x.reshape(32, -1, x.shape[-1]), EXPERT, 0, 0, tiled=True)


def by_expert(slots):
    return tuple(slots[:, 8 * e : 8 * e + 8, :WIDTH].reshape(HALF_SLOTS, WIDTH) for e in range(2))


def summed_slots(terms):
    pieces = [added(*terms[e]).astype(bf16).reshape(32, 8, WIDTH) for e in range(2)]
    return jnp.concatenate(pieces, axis=1)


def sent_to_all(x, axis):
    peers = lax.axis_size(axis)
    return lax.all_to_all(jnp.broadcast_to(x[None], (peers, *x.shape)), axis, 0, 0, tiled=True)


def bucket_of(offsets):
    halfway = BUCKETS // 2
    exact_span = halfway // 2
    distance = jnp.abs(offsets)
    far_part = jnp.full_like(distance, exact_span)
    for step in range(1, exact_span):
        cutoff_level = math.ceil(exact_span * (REACH / exact_span) ** (step / exact_span) - 1e-09)
        far_part = far_part + jnp.where(distance >= cutoff_level, 1, 0)
    nearby = jnp.where(distance < exact_span, distance, far_part)
    return nearby + jnp.where(offsets > 0, halfway, 0)


def tile_buckets(step):
    shape = (QUARTER, QUARTER)
    offsets = (
        step * QUARTER
        + lax.broadcasted_iota(jnp.int32, shape, 1)
        - lax.broadcasted_iota(jnp.int32, shape, 0)
    )
    return bucket_of(offsets)


def possible(step):
    if step == 0:
        return range(BUCKETS)
    if step == 1:
        return range(BUCKETS // 2 + 1, BUCKETS)
    if step == -1:
        return range(1, BUCKETS // 2)
    return (BUCKETS - 1,) if step > 0 else (BUCKETS // 2 - 1,)


def tile_at(row_block, key_block):
    step = key_block - row_block
    return TILE_STEPS.index(max(-2, min(2, step)))


def bias_kernel(head_ref, table_ref, out_ref):
    head = head_ref[0]
    for t, step in enumerate(TILE_STEPS):
        buckets = tile_buckets(step)
        tiles = [jnp.zeros((QUARTER, QUARTER), f32)] * LOCAL_HEADS
        for b in possible(step):
            mask = buckets == b
            tiles = [jnp.where(mask, table_ref[b, head + h], tile) for h, tile in enumerate(tiles)]
        for h, tile in enumerate(tiles):
            out_ref[h, t] = tile


def inverse_size(values):
    return lax.rsqrt(jnp.mean(values * values, axis=-1, keepdims=True) + epsilon)


def as_column(row):
    return jnp.transpose(jnp.broadcast_to(row, (QUARTER, QUARTER)))


def start_kernel(x_ref, gain_ref, seg_ref, n0, n1):
    gain = gain_ref[...]
    for s, out in ((0, n0), (1, n1)):
        x = x_ref[s]
        out[:, :WIDTH] = (x * inverse_size(x) * gain).astype(bf16)
        out[:, WIDTH:] = as_column(seg_ref[s : s + 1].astype(f32)).astype(bf16)


def place_kernel(route_ref, cot_ref, weights_ref, place_ref, lines_ref):
    tri = (
        lax.broadcasted_iota(jnp.int32, (QUARTER, QUARTER), 0)
        >= lax.broadcasted_iota(jnp.int32, (QUARTER, QUARTER), 1)
    ).astype(bf16)
    for s in range(2):
        chosen = as_column(route_ref[s : s + 1].astype(f32)).astype(jnp.int32)
        mask = jnp.where(
            chosen == lax.broadcasted_iota(jnp.int32, (QUARTER, QUARTER), 1), 1.0, 0.0
        )
        running = dot(tri, mask.astype(bf16))
        rank = jnp.sum(mask * running, axis=-1, keepdims=True).astype(jnp.int32) - 1
        place = chosen[:, :1] * 8 + s * CAPACITY + rank
        slots = lax.broadcasted_iota(jnp.int32, (QUARTER, SLOTS), 1)
        place_ref[s * QUARTER : (s + 1) * QUARTER] = jnp.where(slots == place, 1.0, 0.0).astype(bf16)
    slots = dot(place_ref[...], cot_ref[...].astype(bf16), 0, 0)
    weights = weights_ref[...].astype(f32)
    for n in range(32):
        lines_ref[n] = jnp.concatenate([weights, slots[16 * n : 16 * n + 16]]).astype(bf16)


def position(me, k):
    return pl.multiple_of(lax.rem(me + k, PARTS) * QUARTER, QUARTER)


def same_document(g_ref):
    column = g_ref[:, WIDTH:].astype(f32)
    return column, jnp.transpose(column)[:1]


def bias_rows(tiles_ref, h, i):
    per = BLOCK // QUARTER
    return jnp.concatenate(
        [
            jnp.concatenate([tiles_ref[h, tile_at(r, j)] for j in range(PARTS)], axis=1)
            for r in range(i * per, (i + 1) * per)
        ],
        axis=0,
    )


def attend_kernel(
    me_ref, a0, a1, a2, a3, w_ref, tiles_ref, _, g_ref, qkv_ref, att_ref, lse_ref, p0, p1, p2, p3
):
    me = me_ref[0]
    for k, piece in enumerate((a0, a1, a2, a3)):
        g_ref[pl.ds(position(me, k), QUARTER), :] = piece[...]
    qkv_ref[...] = dot(g_ref[:, :WIDTH], w_ref[:, :QKV]).astype(bf16)
    column, row = same_document(g_ref)
    lse_ref[...] = jnp.zeros_like(lse_ref)
    for h in range(LOCAL_HEADS):
        lo = h * HEAD_DIM
        key = qkv_ref[:, CHANNELS + lo : CHANNELS + lo + HEAD_DIM]
        value = qkv_ref[:, 2 * CHANNELS + lo : 2 * CHANNELS + lo + HEAD_DIM]
        for i in range(PARTS * QUARTER // BLOCK):
            rows = slice(i * BLOCK, (i + 1) * BLOCK)
            query = qkv_ref[rows, lo : lo + HEAD_DIM] * HEAD_DIM ** (-0.5)
            scores = dot(query, key, 1, 1) + bias_rows(tiles_ref, h, i)
            scores = jnp.where(column[rows, :1] == row, scores, -1000000000.0)
            row_max = jnp.max(scores, axis=-1, keepdims=True)
            expos = jnp.exp(scores - row_max)
            total = jnp.sum(expos, axis=-1, keepdims=True)
            weights = (expos * (1.0 / total)).astype(bf16)
            att_ref[rows, lo : lo + HEAD_DIM] = dot(weights, value).astype(bf16)
            lse_ref[rows, h : h + 1] = row_max + jnp.log(total)
    for k, out in enumerate((p0, p1, p2, p3)):
        mine = att_ref[pl.ds(position(me, k), QUARTER), :]
        out[...] = dot(mine, w_ref[:, QKV:], 1, 1).astype(bf16)


def dispatch_kernel(
    x_ref, t00, t01, t02, t10, t11, t12, gain_ref, router_ref, route_ref, place_ref, _, __, ___, ____,
    hidden_ref, gate_ref, slots_ref,
):
    for s, terms in ((0, (t00, t01, t02)), (1, (t10, t11, t12))):
        rows = slice(s * QUARTER, (s + 1) * QUARTER)
        hidden_ref[rows] = x_ref[s] + added(*[t[...] for t in terms])
    hidden = hidden_ref[...]
    mixed = hidden * inverse_size(hidden) * gain_ref[...]
    low = mixed.astype(bf16)
    slots_ref[...] = dot(place_ref[...], low, 0, 0).astype(bf16)
    logits = dot(mixed, router_ref[...], precision=lax.Precision.HIGHEST)
    expos = jnp.exp(logits - jnp.max(logits, axis=-1, keepdims=True))
    shares = expos / jnp.sum(expos, axis=-1, keepdims=True)
    for s in range(2):
        rows = slice(s * QUARTER, (s + 1) * QUARTER)
        chosen = as_column(route_ref[s : s + 1].astype(f32)).astype(jnp.int32)[:, :EXPERTS]
        mask = chosen == lax.broadcasted_iota(jnp.int32, (QUARTER, EXPERTS), 1)
        gate = jnp.sum(jnp.where(mask, shares[rows], 0.0), axis=-1, keepdims=True)
        gate_ref[rows] = jnp.broadcast_to(gate, (QUARTER, 128))


WORK_ORDER = (2, 1, 3, 0)


def upstream_kernel(c0, c1, c2, c3, w_ref, u_ref):
    pieces = (c0, c1, c2, c3)
    for n, k in enumerate(WORK_ORDER):
        u_ref[n] = dot(pieces[k][...], w_ref[0], 1, 1).astype(bf16)


def expert_kernel(
    own_ref, x0, x1, x2, x3, u_ref, w_ref, router_ref, _, __,
    active_ref, scaled_ref, grad_ref, logit_ref, s0, s1, s2, s3, pre_ref,
):
    own = own_ref[0]
    router = router_ref[...]
    router_hi = router.astype(bf16)
    router_lo = (router - router_hi.astype(f32)).astype(bf16)
    router_both = jnp.concatenate([router_hi, router_lo], axis=1)
    c = math.sqrt(2.0 / math.pi)
    ca = c * 0.044715

    def work(xs, outs, first):
        x = jnp.concatenate([x_ref[...] for x_ref in xs])
        logits = dot(x, router_both)
        logits = logits[:, :EXPERTS] + logits[:, EXPERTS:]
        expos = jnp.exp(logits - jnp.max(logits, axis=-1, keepdims=True))
        shares = expos / jnp.sum(expos, axis=-1, keepdims=True)
        chosen = jnp.where(lax.broadcasted_iota(jnp.int32, shares.shape, 1) == own, 1.0, 0.0)
        gate = jnp.sum(shares * chosen, axis=-1, keepdims=True)
        pre_ref[...] = dot(x, w_ref[0])
        gate_grads = []
        for n in range(2):
            for part in range(HALF_SLOTS // 64):
                rows = slice(part * 64, part * 64 + 64)
                at = slice(n * HALF_SLOTS + part * 64, n * HALF_SLOTS + part * 64 + 64)
                pre = pre_ref[at, :]
                u = u_ref[n, rows, :].astype(f32)
                square = pre * pre
                t = jnp.tanh(pre * (c + ca * square))
                half = 0.5 + 0.5 * t
                active = pre * half
                slope = half + (0.5 * pre) * (1.0 - t * t) * (c + 3.0 * ca * square)
                gate_grads.append(jnp.sum(active * u, axis=-1, keepdims=True))
                active_ref[n, rows, :] = active.astype(bf16)
                scaled_ref[n, rows, :] = (gate[at] * active).astype(bf16)
                grad_ref[n, rows, :] = (gate[at] * u * slope).astype(bf16)
        logit_grad = shares * (chosen - gate) * jnp.concatenate(gate_grads)
        logit_hi = logit_grad.astype(bf16)
        logit_lo = (logit_grad - logit_hi.astype(f32)).astype(bf16)
        pre_grad = jnp.concatenate([grad_ref[0], grad_ref[1]])
        slot_grad = dot(pre_grad, w_ref[0], 1, 1) + dot(logit_hi, router_hi, 1, 1)
        for n, out in enumerate(outs):
            out[...] = slot_grad[n * HALF_SLOTS : (n + 1) * HALF_SLOTS].astype(bf16)
        term = dot(jnp.concatenate([logit_hi, logit_lo], axis=1), x, 0, 0)
        if first:
            logit_ref[...] = term
        else:
            logit_ref[...] += term

    pl.when(pl.program_id(0) == 0)(lambda: work((x2, x1), (s2, s1), True))
    pl.when(pl.program_id(0) == 1)(lambda: work((x3, x0), (s3, s0), False))


def output_kernel(active_ref, w_ref, s0, s1, s2, s3):
    outs = (s0, s1, s2, s3)
    for n, k in enumerate(WORK_ORDER):
        outs[k][...] = dot(active_ref[n], w_ref[0]).astype(bf16)


def weights_kernel(scaled_ref, grad_ref, c0, c1, c2, c3, x0, x1, x2, x3, *rest):
    out_ref, in_ref, token_ref = rest[-3:]
    token_ref[...] = jnp.zeros_like(token_ref)
    upstream, entered = (c0, c1, c2, c3), (x0, x1, x2, x3)
    for n, k in enumerate(WORK_ORDER):
        out_term = dot(scaled_ref[n], upstream[k][...], 0, 0)
        in_term = dot(entered[k][...], grad_ref[n], 0, 0)
        if n == 0:
            out_ref[0] = out_term
            in_ref[0] = in_term
        else:
            out_ref[0] += out_term
            in_ref[0] += in_term


def back_kernel(
    slots_ref, place_ref, hidden_ref, cot_ref, gain_ref, _, grad_ref, h0, h1, gain_grad_ref
):
    mixed_grad = dot(place_ref[...], slots_ref[...])
    hidden = hidden_ref[...]
    r = inverse_size(hidden)
    gain_grad_ref[...] = jnp.sum(mixed_grad * hidden * r, axis=0, keepdims=True)
    u = gain_ref[...] * mixed_grad
    grad = cot_ref[...] + r * u - hidden * (r * r * r * jnp.mean(hidden * u, axis=-1, keepdims=True))
    grad_ref[...] = grad
    h0[...] = grad[:QUARTER].astype(bf16)
    h1[...] = grad[QUARTER:].astype(bf16)


def result_kernel(slots_ref, place_ref, hidden_ref, gate_ref, out_ref):
    back = dot(place_ref[...], slots_ref[...])
    out_ref[...] = hidden_ref[...] + gate_ref[:, :1] * back


def attend_back_kernel(
    me_ref, a0, a1, a2, a3, w_ref, tiles_ref, g_ref, qkv_ref, lse_ref, _,
    up_ref, dqkv_ref, sums_ref, gain_ref, out_ref, tile_sums,
):
    me = me_ref[0]
    for k, piece in enumerate((a0, a1, a2, a3)):
        up_ref[pl.ds(position(me, k), QUARTER), :] = piece[...]
    att_grad = dot(up_ref[...], w_ref[:, QKV:]).astype(bf16)
    column, row = same_document(g_ref)
    tile_sums[...] = jnp.zeros_like(tile_sums)
    for h in range(LOCAL_HEADS):
        lo = h * HEAD_DIM
        key = qkv_ref[:, CHANNELS + lo : CHANNELS + lo + HEAD_DIM]
        value = qkv_ref[:, 2 * CHANNELS + lo : 2 * CHANNELS + lo + HEAD_DIM]
        key_grad = jnp.zeros((HEAD_DIM, PARTS * QUARTER), f32)
        value_grad = jnp.zeros((HEAD_DIM, PARTS * QUARTER), f32)
        for i in range(PARTS * QUARTER // BLOCK):
            rows = slice(i * BLOCK, (i + 1) * BLOCK)
            query = qkv_ref[rows, lo : lo + HEAD_DIM] * HEAD_DIM ** (-0.5)
            scores = dot(query, key, 1, 1) + bias_rows(tiles_ref, h, i)
            scores = jnp.where(column[rows, :1] == row, scores, -1000000000.0)
            weights = jnp.exp(scores - lse_ref[rows, h : h + 1])
            out_grad = att_grad[rows, lo : lo + HEAD_DIM]
            weights_grad = dot(out_grad, value, 1, 1)
            inner = jnp.sum(weights * weights_grad, axis=-1, keepdims=True)
            score_grad = (weights * (weights_grad - inner)).astype(bf16)
            wide = score_grad.astype(f32)
            for r in range(BLOCK // QUARTER):
                for j in range(PARTS):
                    tile_sums[h, tile_at(i * (BLOCK // QUARTER) + r, j)] += wide[
                        r * QUARTER : (r + 1) * QUARTER, j * QUARTER : (j + 1) * QUARTER
                    ]
            dqkv_ref[rows, lo : lo + HEAD_DIM] = (
                dot(score_grad, key) * HEAD_DIM ** (-0.5)
            ).astype(bf16)
            key_grad += dot(query, score_grad, 0, 0)
            value_grad += dot(out_grad, weights.astype(bf16), 0, 0)
        dqkv_ref[:, CHANNELS + lo : CHANNELS + lo + HEAD_DIM] = jnp.transpose(key_grad).astype(bf16)
        dqkv_ref[:, 2 * CHANNELS + lo : 2 * CHANNELS + lo + HEAD_DIM] = jnp.transpose(
            value_grad
        ).astype(bf16)
    normed_grad = dot(dqkv_ref[...], w_ref[:, :QKV], 1, 1)
    out_ref[...] = normed_grad.astype(bf16)
    gain_ref[...] = jnp.sum(normed_grad * g_ref[:, :WIDTH].astype(f32), axis=0, keepdims=True)
    sums_ref[...] = jnp.zeros_like(sums_ref)
    for t, step in enumerate(TILE_STEPS):
        buckets = tile_buckets(step)
        for b in possible(step):
            mask = buckets == b
            for h in range(LOCAL_HEADS):
                sums_ref[h, b : b + 1] += jnp.sum(
                    jnp.where(mask, tile_sums[h, t], 0.0), axis=0, keepdims=True
                )


def projection_kernel(g0, g1, d0, d1, u0, u1, a0, a1, out_ref):
    out_ref[:, :QKV] = (
        dot(g0[:, :WIDTH], d0[...], 0, 0) + dot(g1[:, :WIDTH], d1[...], 0, 0)
    ).astype(bf16)
    out_ref[:, QKV:] = (dot(u0[...], a0[...], 0, 0) + dot(u1[...], a1[...], 0, 0)).astype(bf16)


def input_kernel(x_ref, gain_ref, grad_ref, t0, t1, out_ref):
    for s, term in ((0, t0), (1, t1)):
        x = x_ref[s]
        r = inverse_size(x)
        u = gain_ref[...] * term[...].astype(f32)
        out_ref[s] = (
            grad_ref[s * QUARTER : (s + 1) * QUARTER]
            + r * u
            - x * (r * r * r * jnp.mean(x * u, axis=-1, keepdims=True))
        )


def expert_spec(e):
    return pl.BlockSpec((1, WIDTH, WIDTH), lambda i: (e, 0, 0))


def body(
    inputs,
    projection_in,
    projection_out,
    gain_attention,
    gain_experts,
    router_weight,
    bias_table,
    expert_in,
    expert_out,
    routes,
    segments,
    cotangent,
):
    seq_here, quarter, width = inputs.shape
    rows = seq_here * quarter
    me = lax.axis_index("mp").reshape(1).astype(jnp.int32)
    first_head = me * LOCAL_HEADS
    gain1, gain2 = gain_attention.reshape(1, width), gain_experts.reshape(1, width)
    routes = routes.reshape(seq_here, quarter)
    upstream = cotangent.reshape(rows, width)
    piece = struct((QUARTER, WIDTH), bf16)
    slot_piece = struct((HALF_SLOTS, WIDTH), bf16)

    turned = jnp.concatenate(
        [jnp.moveaxis(projection_in, 1, 0).reshape(24, QKV), projection_out.T], axis=1
    )
    place, lines = call(
        place_kernel,
        (struct((rows, SLOTS), bf16), struct((32, 40, width), bf16)),
        (routes, upstream, turned),
        name="place",
    )
    lines = lax.all_to_all(lines, EXPERT, 0, 0, tiled=True)
    weights = lines[:, :24].reshape(WIDTH, QKV + CHANNELS)
    c_slots = by_expert(lines[:, 24:])

    tagged = struct((QUARTER, TAGGED), bf16)
    n0, n1 = call(start_kernel, (tagged, tagged), (inputs, gain1, segments), name="start")
    normed = (gather4(n0, 1), gather4(n1, -1))
    tiles = call(
        bias_kernel,
        struct((LOCAL_HEADS, len(TILE_STEPS), QUARTER, QUARTER), f32),
        (first_head, bias_table),
        [SMEM, SMEM],
        name="bias",
    )
    length = PARTS * QUARTER
    attended = [
        call(
            attend_kernel,
            (
                struct((length, TAGGED), bf16),
                struct((length, QKV), bf16),
                struct((length, CHANNELS), bf16),
                struct((length, 128), f32),
                piece, piece, piece, piece,
            ),
            (me, *normed[s], weights, tiles, normed[1 - s][2]),
            [SMEM] + [VMEM] * 6 + [ANY],
            flops=2 * 10**9,
            name="attend",
        )
        for s in range(2)
    ]
    attention = [reduce4(attended[s][4:], (1, -1)[s]) for s in range(2)]

    c_all = [gather4(c, (1, -1)[e]) for e, c in enumerate(c_slots)]
    u = [
        call(
            upstream_kernel,
            struct((PARTS, HALF_SLOTS, WIDTH), bf16),
            (*c_all[e], expert_out),
            [VMEM] * 4 + [expert_spec(e)],
            flops=12 * 10**8,
            name="upstream",
        )
        for e in range(2)
    ]

    hidden, gate, slots = call(
        dispatch_kernel,
        (struct((rows, width), f32), struct((rows, 128), f32), struct((SLOTS, width), bf16)),
        (
            inputs, *attention[0], *attention[1], gain2, router_weight, routes, place,
            c_all[0][1], c_all[0][3], c_all[1][1], c_all[1][3],
        ),
        [VMEM] * 11 + [ANY] * 4,
        name="dispatch",
    )
    x_all = [gather4(x, (1, -1)[e]) for e, x in enumerate(by_expert(to_experts(slots)))]
    group = lax.axis_index(EXPERT).astype(jnp.int32)
    acts = struct((PARTS, HALF_SLOTS, WIDTH), bf16)
    pair = pl.BlockSpec((2, HALF_SLOTS, WIDTH), lambda i: (i, 0, 0))
    worked = []
    for e in range(2):
        earlier = (worked[0][4], u[0]) if e else (x_all[1][2], u[1])
        outs = pl.pallas_call(
            expert_kernel,
            grid=(2,),
            out_shape=(acts, acts, acts, struct((2 * EXPERTS, WIDTH), f32)) + (slot_piece,) * 4,
            in_specs=[SMEM] + [VMEM] * 4 + [pair, expert_spec(e), VMEM, ANY, ANY],
            out_specs=(pair, pair, pair) + (VMEM,) * 5,
            scratch_shapes=[pltpu.VMEM((SLOTS, WIDTH), f32)],
            cost_estimate=pl.CostEstimate(
                flops=24 * 10**8, bytes_accessed=2 * 10**7, transcendentals=0
            ),
            compiler_params=pltpu.CompilerParams(vmem_limit_bytes=VMEM_LIMIT),
            name="expert",
        )((group * 2 + e).reshape(1), *x_all[e], u[e], expert_in, router_weight, *earlier)
        worked.append(outs)
    outputs = [
        call(
            output_kernel,
            (slot_piece,) * 4,
            (worked[e][0], expert_out),
            [VMEM, expert_spec(e)],
            flops=12 * 10**8,
            name="expert_output",
        )
        for e in range(2)
    ]
    whole = struct((2, WIDTH, WIDTH), f32)
    expert_grads, tokens = (), []
    for e in range(2):
        ins = (worked[e][1], worked[e][2], *c_all[e], *x_all[e])
        *expert_grads, token = pl.pallas_call(
            weights_kernel,
            grid=(1,),
            out_shape=(whole, whole, struct((8, 128), f32)),
            in_specs=[VMEM] * 10 + [pl.BlockSpec(memory_space=pl.ANY)] * len(expert_grads),
            out_specs=(expert_spec(e), expert_spec(e), VMEM),
            input_output_aliases={10: 0, 11: 1} if expert_grads else {},
            cost_estimate=pl.CostEstimate(
                flops=24 * 10**8, bytes_accessed=2 * 10**7, transcendentals=0
            ),
            compiler_params=pltpu.CompilerParams(vmem_limit_bytes=VMEM_LIMIT),
            name="expert_weights",
        )(*ins, *expert_grads)
        tokens.append(token)
    grad_expert_out, grad_expert_in = expert_grads

    slot_terms = [reduce4(worked[0][4:], 1), reduce4(worked[1][4:], -1)]
    returned = to_experts(summed_slots(slot_terms))
    output_slots = summed_slots([reduce4(outputs[e], (1, -1)[e]) for e in range(2)])
    hidden_grad, h0, h1, gain2_grad = call(
        back_kernel,
        (struct((rows, width), f32), piece, piece, struct((1, width), f32)),
        (returned.reshape(SLOTS, width), place, hidden, upstream, gain2, tokens[0]),
        [VMEM] * 5 + [ANY],
        name="back",
    )
    grads = (gather4(h0, 1), gather4(h1, -1))
    attended_back = [
        call(
            attend_back_kernel,
            (
                struct((length, width), bf16),
                struct((length, QKV), bf16),
                struct((LOCAL_HEADS, BUCKETS, 128), f32),
                struct((1, width), f32),
                struct((length, width), bf16),
            ),
            (me, *grads[s], weights, tiles, *attended[s][:2], attended[s][3], grads[1 - s][2]),
            [SMEM] + [VMEM] * 9 + [ANY],
            scratch=[pltpu.VMEM((LOCAL_HEADS, len(TILE_STEPS), QUARTER, QUARTER), f32)],
            flops=4 * 10**9,
            name="attend_back",
        )
        for s in range(2)
    ]
    normed_grad = [
        lax.psum_scatter(attended_back[s][4], "mp", scatter_dimension=0, tiled=True)
        for s in range(2)
    ]
    input_grad = call(
        input_kernel,
        struct(inputs.shape, f32),
        (inputs, gain1, hidden_grad, *normed_grad),
        name="input_gradient",
    )

    router = worked[0][3] + worked[1][3]
    router = (router[:EXPERTS] + router[EXPERTS:]).T.astype(bf16).reshape(32, 16, 96)
    router = jnp.pad(router, ((0, 0), (0, 0), (0, 32)))
    output_slots = jnp.concatenate([output_slots, router], axis=2)
    output_back = to_experts(output_slots)
    router_rows = jnp.sum(output_back[:, :, width : width + 96].astype(f32), axis=0)
    result = call(
        result_kernel,
        struct((rows, width), f32),
        (output_back[:, :, :width].reshape(SLOTS, width), place, hidden, gate),
        name="result",
    )
    partial = call(
        projection_kernel,
        struct((WIDTH, QKV + CHANNELS), bf16),
        (
            attended[0][0], attended[1][0], attended_back[0][1], attended_back[1][1],
            attended_back[0][0], attended_back[1][0], attended[0][2], attended[1][2],
        ),
        flops=16 * 10**8,
        name="projection_gradient",
    )
    table_local = jnp.sum(attended_back[0][2] + attended_back[1][2], axis=-1).T
    table = lax.dynamic_update_slice(
        jnp.zeros((BUCKETS, HEADS), f32), table_local, (0, first_head[0])
    )
    gain1_grad = (attended_back[0][3] + attended_back[1][3]) / gain1
    small = jnp.concatenate(
        [t.reshape(-1) for t in (router_rows, gain1_grad, gain2_grad, table)]
    ).reshape(27, 128)
    small = added(small, shift(small, 1), shift(small, -1), shift(small, 2)).reshape(-1)
    lines = jnp.pad(small.astype(bf16), (0, 5 * width - small.size)).reshape(1, 5, width)
    lines = jnp.concatenate(
        [partial.reshape(32, 24, width), jnp.broadcast_to(lines, (32, 5, width))], axis=1
    )
    arrived = lax.all_to_all(lines, EXPERT, 0, 0, tiled=True)
    projections = jnp.sum(arrived[:, :24].astype(f32), axis=0)
    grad_projection_in = jnp.moveaxis(projections[:, :QKV].reshape(24, 3, CHANNELS), 1, 0)
    grad_projection_out = projections[:, QKV:].T
    grad_router = arrived[:, 24:26].astype(f32).reshape(WIDTH, EXPERTS)
    late = jnp.sum(arrived[:, 26:].astype(f32), axis=0).reshape(-1)
    grad_gain_attention = late[:width]
    grad_gain_experts = late[width : 2 * width]
    grad_table = late[2 * width : 2 * width + BUCKETS * HEADS].reshape(BUCKETS, HEADS)
    return (
        result.reshape(seq_here, quarter, width),
        input_grad,
        grad_projection_in,
        grad_projection_out,
        grad_gain_attention,
        grad_gain_experts,
        grad_router,
        grad_table,
        grad_expert_in,
        grad_expert_out,
    )


def solution(mesh):
    split = Mesh(
        mesh.devices.reshape(4, 4, 2, mesh.shape["mp"]), ("expert_0", "expert_1", "expert_2", "mp")
    )
    in_specs = (
        P(EXPERT, "mp", None),
        P(None, EXPERT, "mp"),
        P("mp", EXPERT),
        P(),
        P(),
        P(),
        P(),
        P(EXPERT, None, "mp"),
        P(EXPERT, "mp", None),
        P(EXPERT, "mp", None),
        P(EXPERT, "mp"),
        P(EXPERT, "mp", None),
    )
    out_specs = (
        P(EXPERT, "mp", None),
        P(EXPERT, "mp", None),
        P(None, EXPERT, "mp"),
        P("mp", EXPERT),
        P(),
        P(),
        P(),
        P(),
        P(EXPERT, None, "mp"),
        P(EXPERT, "mp", None),
    )
    return jax.shard_map(body, mesh=split, in_specs=in_specs, out_specs=out_specs, check_vma=False)
```

```python
import functools
import math

import jax
import jax.numpy as jnp
from jax import lax
from jax.experimental import pallas as pl
from jax.experimental.pallas import tpu as pltpu
from jax.sharding import Mesh
from jax.sharding import PartitionSpec as P

HEADS = 12
HEAD_DIM = 64
EXPERTS = 64
BUCKETS = 32
REACH = 128
EXPERT = ("expert_0", "expert_1", "expert_2")
QUARTER = 128
PARTS = 4
WIDTH = 768
CHANNELS = 192
LOCAL_HEADS = CHANNELS // HEAD_DIM
QKV = 3 * CHANNELS
CAPACITY = 4
SLOTS = 512
HALF_SLOTS = SLOTS // 2
TAGGED = WIDTH + 128
TILE_STEPS = (0, 1, -1, 2, -2)

epsilon = 1e-06
f32 = jnp.float32
bf16 = jnp.bfloat16
BLOCK = 512
VMEM_LIMIT = 56 * 1024 * 1024


def dot(a, b, ca=1, cb=0, precision=None):
    return lax.dot_general(
        a, b, (((ca,), (cb,)), ((), ())), preferred_element_type=f32, precision=precision
    )


def struct(shape, dtype):
    return jax.ShapeDtypeStruct(shape, dtype)


ANY = pl.BlockSpec(memory_space=pl.ANY)
SMEM = pl.BlockSpec(memory_space=pltpu.SMEM)
VMEM = pl.BlockSpec(memory_space=pltpu.VMEM)


def call(kernel, outs, ins, in_specs=None, scratch=(), flops=10**8, moved=4 * 10**6, name=None):
    return pl.pallas_call(
        kernel,
        grid=(1,),
        out_shape=outs,
        in_specs=in_specs or [VMEM] * len(ins),
        out_specs=jax.tree.map(lambda _: VMEM, outs),
        scratch_shapes=scratch,
        cost_estimate=pl.CostEstimate(flops=flops, bytes_accessed=moved, transcendentals=0),
        compiler_params=pltpu.CompilerParams(vmem_limit_bytes=VMEM_LIMIT),
        name=name,
    )(*ins)


def shift(x, step):
    return lax.ppermute(x, "mp", [(i, (i + step) % PARTS) for i in range(PARTS)])


def gather4(x, way):
    left, right = shift(x, 1), shift(x, -1)
    far = shift(left, 1) if way > 0 else shift(right, -1)
    return x, right, far, left


def added(*terms):
    return functools.reduce(lambda a, b: a + b, [t.astype(f32) for t in terms])


def reduce4(pieces, way):
    own, right, far, left = pieces
    if way > 0:
        middle = right = added(right, shift(far, 1)).astype(bf16)
    else:
        middle = left = added(left, shift(far, -1)).astype(bf16)
    return (own, shift(right, 1), shift(left, -1)), middle


def to_experts(x):
    return lax.all_to_all(x.reshape(32, -1, x.shape[-1]), EXPERT, 0, 0, tiled=True)


def by_expert(slots):
    return tuple(slots[:, 8 * e : 8 * e + 8, :WIDTH].reshape(HALF_SLOTS, WIDTH) for e in range(2))


def summed_slots(terms):
    pieces = [added(*terms[e]).astype(bf16).reshape(32, 8, WIDTH) for e in range(2)]
    return jnp.concatenate(pieces, axis=1)


def sent_to_all(x, axis):
    peers = lax.axis_size(axis)
    return lax.all_to_all(jnp.broadcast_to(x[None], (peers, *x.shape)), axis, 0, 0, tiled=True)


def bucket_of(offsets):
    halfway = BUCKETS // 2
    exact_span = halfway // 2
    distance = jnp.abs(offsets)
    far_part = jnp.full_like(distance, exact_span)
    for step in range(1, exact_span):
        cutoff_level = math.ceil(exact_span * (REACH / exact_span) ** (step / exact_span) - 1e-09)
        far_part = far_part + jnp.where(distance >= cutoff_level, 1, 0)
    nearby = jnp.where(distance < exact_span, distance, far_part)
    return nearby + jnp.where(offsets > 0, halfway, 0)


def tile_buckets(step):
    shape = (QUARTER, QUARTER)
    offsets = (
        step * QUARTER
        + lax.broadcasted_iota(jnp.int32, shape, 1)
        - lax.broadcasted_iota(jnp.int32, shape, 0)
    )
    return bucket_of(offsets)


def possible(step):
    if step == 0:
        return range(BUCKETS)
    if step == 1:
        return range(BUCKETS // 2 + 1, BUCKETS)
    if step == -1:
        return range(1, BUCKETS // 2)
    return (BUCKETS - 1,) if step > 0 else (BUCKETS // 2 - 1,)


def tile_at(row_block, key_block):
    step = key_block - row_block
    return TILE_STEPS.index(max(-2, min(2, step)))


def bias_kernel(head_ref, table_ref, out_ref):
    head = head_ref[0]
    for t, step in enumerate(TILE_STEPS):
        buckets = tile_buckets(step)
        tiles = [jnp.zeros((QUARTER, QUARTER), f32)] * LOCAL_HEADS
        for b in possible(step):
            mask = buckets == b
            tiles = [jnp.where(mask, table_ref[b, head + h], tile) for h, tile in enumerate(tiles)]
        for h, tile in enumerate(tiles):
            out_ref[h, t] = tile


def inverse_size(values):
    return lax.rsqrt(jnp.mean(values * values, axis=-1, keepdims=True) + epsilon)


def as_column(row):
    return jnp.transpose(jnp.broadcast_to(row, (QUARTER, QUARTER)))


def start_kernel(x_ref, gain_ref, seg_ref, n0, n1):
    gain = gain_ref[...]
    for s, out in ((0, n0), (1, n1)):
        x = x_ref[s]
        out[:, :WIDTH] = (x * inverse_size(x) * gain).astype(bf16)
        out[:, WIDTH:] = as_column(seg_ref[s : s + 1].astype(f32)).astype(bf16)


def place_kernel(route_ref, cot_ref, weights_ref, place_ref, lines_ref):
    tri = (
        lax.broadcasted_iota(jnp.int32, (QUARTER, QUARTER), 0)
        >= lax.broadcasted_iota(jnp.int32, (QUARTER, QUARTER), 1)
    ).astype(bf16)
    for s in range(2):
        chosen = as_column(route_ref[s : s + 1].astype(f32)).astype(jnp.int32)
        mask = jnp.where(
            chosen == lax.broadcasted_iota(jnp.int32, (QUARTER, QUARTER), 1), 1.0, 0.0
        )
        running = dot(tri, mask.astype(bf16))
        rank = jnp.sum(mask * running, axis=-1, keepdims=True).astype(jnp.int32) - 1
        place = chosen[:, :1] * 8 + s * CAPACITY + rank
        slots = lax.broadcasted_iota(jnp.int32, (QUARTER, SLOTS), 1)
        place_ref[s * QUARTER : (s + 1) * QUARTER] = jnp.where(slots == place, 1.0, 0.0).astype(bf16)
    slots = dot(place_ref[...], cot_ref[...].astype(bf16), 0, 0)
    weights = weights_ref[...].astype(f32)
    for n in range(32):
        lines_ref[n] = jnp.concatenate([weights, slots[16 * n : 16 * n + 16]]).astype(bf16)


def position(me, k):
    return pl.multiple_of(lax.rem(me + k, PARTS) * QUARTER, QUARTER)


def same_document(g_ref):
    column = g_ref[:, WIDTH:].astype(f32)
    return column, jnp.transpose(column)[:1]


def bias_rows(tiles_ref, h, i):
    per = BLOCK // QUARTER
    return jnp.concatenate(
        [
            jnp.concatenate([tiles_ref[h, tile_at(r, j)] for j in range(PARTS)], axis=1)
            for r in range(i * per, (i + 1) * per)
        ],
        axis=0,
    )


def attend_kernel(
    me_ref, a0, a1, a2, a3, w_ref, tiles_ref, g_ref, qkv_ref, att_ref, lse_ref, p0, p1, p2, p3
):
    me = me_ref[0]
    for k, piece in enumerate((a0, a1, a2, a3)):
        g_ref[pl.ds(position(me, k), QUARTER), :] = piece[...]
    qkv_ref[...] = dot(g_ref[:, :WIDTH], w_ref[:, :QKV]).astype(bf16)
    column, row = same_document(g_ref)
    lse_ref[...] = jnp.zeros_like(lse_ref)
    for h in range(LOCAL_HEADS):
        lo = h * HEAD_DIM
        key = qkv_ref[:, CHANNELS + lo : CHANNELS + lo + HEAD_DIM]
        value = qkv_ref[:, 2 * CHANNELS + lo : 2 * CHANNELS + lo + HEAD_DIM]
        for i in range(PARTS * QUARTER // BLOCK):
            rows = slice(i * BLOCK, (i + 1) * BLOCK)
            query = qkv_ref[rows, lo : lo + HEAD_DIM] * HEAD_DIM ** (-0.5)
            scores = dot(query, key, 1, 1) + bias_rows(tiles_ref, h, i)
            scores = jnp.where(column[rows, :1] == row, scores, -1000000000.0)
            row_max = jnp.max(scores, axis=-1, keepdims=True)
            expos = jnp.exp(scores - row_max)
            total = jnp.sum(expos, axis=-1, keepdims=True)
            weights = (expos * (1.0 / total)).astype(bf16)
            att_ref[rows, lo : lo + HEAD_DIM] = dot(weights, value).astype(bf16)
            lse_ref[rows, h : h + 1] = row_max + jnp.log(total)
    for k, out in enumerate((p0, p1, p2, p3)):
        mine = att_ref[pl.ds(position(me, k), QUARTER), :]
        out[...] = dot(mine, w_ref[:, QKV:], 1, 1).astype(bf16)


def dispatch_kernel(
    x_ref, t00, t01, t02, t10, t11, t12, gain_ref, router_ref, route_ref, place_ref,
    hidden_ref, gate_ref, slots_ref,
):
    for s, terms in ((0, (t00, t01, t02)), (1, (t10, t11, t12))):
        rows = slice(s * QUARTER, (s + 1) * QUARTER)
        hidden_ref[rows] = x_ref[s] + added(*[t[...] for t in terms])
    hidden = hidden_ref[...]
    mixed = hidden * inverse_size(hidden) * gain_ref[...]
    low = mixed.astype(bf16)
    slots_ref[...] = dot(place_ref[...], low, 0, 0).astype(bf16)
    logits = dot(mixed, router_ref[...], precision=lax.Precision.HIGHEST)
    expos = jnp.exp(logits - jnp.max(logits, axis=-1, keepdims=True))
    shares = expos / jnp.sum(expos, axis=-1, keepdims=True)
    for s in range(2):
        rows = slice(s * QUARTER, (s + 1) * QUARTER)
        chosen = as_column(route_ref[s : s + 1].astype(f32)).astype(jnp.int32)[:, :EXPERTS]
        mask = chosen == lax.broadcasted_iota(jnp.int32, (QUARTER, EXPERTS), 1)
        gate = jnp.sum(jnp.where(mask, shares[rows], 0.0), axis=-1, keepdims=True)
        gate_ref[rows] = jnp.broadcast_to(gate, (QUARTER, 128))


WORK_ORDER = (2, 1, 3, 0)


def upstream_kernel(c0, c1, c2, c3, w_ref, u_ref):
    pieces = (c0, c1, c2, c3)
    for n, k in enumerate(WORK_ORDER):
        u_ref[n] = dot(pieces[k][...], w_ref[0], 1, 1).astype(bf16)


def expert_kernel(
    own_ref, x0, x1, x2, x3, u_ref, w_ref, router_ref, _, __,
    active_ref, scaled_ref, grad_ref, logit_ref, s0, s1, s2, s3, pre_ref,
):
    own = own_ref[0]
    router = router_ref[...]
    router_hi = router.astype(bf16)
    router_lo = (router - router_hi.astype(f32)).astype(bf16)
    router_both = jnp.concatenate([router_hi, router_lo], axis=1)
    c = math.sqrt(2.0 / math.pi)
    ca = c * 0.044715

    def work(xs, outs, first):
        x = jnp.concatenate([x_ref[...] for x_ref in xs])
        logits = dot(x, router_both)
        logits = logits[:, :EXPERTS] + logits[:, EXPERTS:]
        expos = jnp.exp(logits - jnp.max(logits, axis=-1, keepdims=True))
        shares = expos / jnp.sum(expos, axis=-1, keepdims=True)
        chosen = jnp.where(lax.broadcasted_iota(jnp.int32, shares.shape, 1) == own, 1.0, 0.0)
        gate = jnp.sum(shares * chosen, axis=-1, keepdims=True)
        pre_ref[...] = dot(x, w_ref[0])
        gate_grads = []
        for n in range(2):
            for part in range(HALF_SLOTS // 64):
                rows = slice(part * 64, part * 64 + 64)
                at = slice(n * HALF_SLOTS + part * 64, n * HALF_SLOTS + part * 64 + 64)
                pre = pre_ref[at, :]
                u = u_ref[n, rows, :].astype(f32)
                square = pre * pre
                t = jnp.tanh(pre * (c + ca * square))
                half = 0.5 + 0.5 * t
                active = pre * half
                slope = half + (0.5 * pre) * (1.0 - t * t) * (c + 3.0 * ca * square)
                gate_grads.append(jnp.sum(active * u, axis=-1, keepdims=True))
                active_ref[n, rows, :] = active.astype(bf16)
                scaled_ref[n, rows, :] = (gate[at] * active).astype(bf16)
                grad_ref[n, rows, :] = (gate[at] * u * slope).astype(bf16)
        logit_grad = shares * (chosen - gate) * jnp.concatenate(gate_grads)
        logit_hi = logit_grad.astype(bf16)
        logit_lo = (logit_grad - logit_hi.astype(f32)).astype(bf16)
        pre_grad = jnp.concatenate([grad_ref[0], grad_ref[1]])
        slot_grad = dot(pre_grad, w_ref[0], 1, 1) + dot(logit_hi, router_hi, 1, 1)
        for n, out in enumerate(outs):
            out[...] = slot_grad[n * HALF_SLOTS : (n + 1) * HALF_SLOTS].astype(bf16)
        term = dot(jnp.concatenate([logit_hi, logit_lo], axis=1), x, 0, 0)
        if first:
            logit_ref[...] = term
        else:
            logit_ref[...] += term

    pl.when(pl.program_id(0) == 0)(lambda: work((x2, x1), (s2, s1), True))
    pl.when(pl.program_id(0) == 1)(lambda: work((x3, x0), (s3, s0), False))


def output_kernel(active_ref, w_ref, _, __, s0, s1, s2, s3):
    outs = (s0, s1, s2, s3)
    for n, k in enumerate(WORK_ORDER):
        outs[k][...] = dot(active_ref[n], w_ref[0]).astype(bf16)


def weights_kernel(scaled_ref, grad_ref, c0, c1, c2, c3, x0, x1, x2, x3, *rest):
    out_ref, in_ref, token_ref = rest[-3:]
    token_ref[...] = jnp.zeros_like(token_ref)
    upstream, entered = (c0, c1, c2, c3), (x0, x1, x2, x3)
    for n, k in enumerate(WORK_ORDER):
        out_term = dot(scaled_ref[n], upstream[k][...], 0, 0)
        in_term = dot(entered[k][...], grad_ref[n], 0, 0)
        if n == 0:
            out_ref[0] = out_term
            in_ref[0] = in_term
        else:
            out_ref[0] += out_term
            in_ref[0] += in_term


def router_kernel(a_ref, b_ref, _, out_ref):
    both = a_ref[...] + b_ref[...]
    out_ref[...] = jnp.transpose(both[:EXPERTS] + both[EXPERTS:]).astype(bf16)


def back_kernel(
    slots_ref, place_ref, hidden_ref, cot_ref, gain_ref, _, grad_ref, h0, h1, gain_grad_ref
):
    mixed_grad = dot(place_ref[...], slots_ref[...])
    hidden = hidden_ref[...]
    r = inverse_size(hidden)
    gain_grad_ref[...] = jnp.sum(mixed_grad * hidden * r, axis=0, keepdims=True)
    u = gain_ref[...] * mixed_grad
    grad = cot_ref[...] + r * u - hidden * (r * r * r * jnp.mean(hidden * u, axis=-1, keepdims=True))
    grad_ref[...] = grad
    h0[...] = grad[:QUARTER].astype(bf16)
    h1[...] = grad[QUARTER:].astype(bf16)


def result_kernel(slots_ref, place_ref, hidden_ref, gate_ref, out_ref):
    back = dot(place_ref[...], slots_ref[...])
    out_ref[...] = hidden_ref[...] + gate_ref[:, :1] * back


def attend_back_kernel(
    me_ref, a0, a1, a2, a3, w_ref, tiles_ref, g_ref, qkv_ref, lse_ref, _,
    up_ref, dqkv_ref, sums_ref, gain_ref, out_ref, tile_sums,
):
    me = me_ref[0]
    for k, piece in enumerate((a0, a1, a2, a3)):
        up_ref[pl.ds(position(me, k), QUARTER), :] = piece[...]
    att_grad = dot(up_ref[...], w_ref[:, QKV:]).astype(bf16)
    column, row = same_document(g_ref)
    tile_sums[...] = jnp.zeros_like(tile_sums)
    for h in range(LOCAL_HEADS):
        lo = h * HEAD_DIM
        key = qkv_ref[:, CHANNELS + lo : CHANNELS + lo + HEAD_DIM]
        value = qkv_ref[:, 2 * CHANNELS + lo : 2 * CHANNELS + lo + HEAD_DIM]
        key_grad = jnp.zeros((HEAD_DIM, PARTS * QUARTER), f32)
        value_grad = jnp.zeros((HEAD_DIM, PARTS * QUARTER), f32)
        for i in range(PARTS * QUARTER // BLOCK):
            rows = slice(i * BLOCK, (i + 1) * BLOCK)
            query = qkv_ref[rows, lo : lo + HEAD_DIM] * HEAD_DIM ** (-0.5)
            scores = dot(query, key, 1, 1) + bias_rows(tiles_ref, h, i)
            scores = jnp.where(column[rows, :1] == row, scores, -1000000000.0)
            weights = jnp.exp(scores - lse_ref[rows, h : h + 1])
            out_grad = att_grad[rows, lo : lo + HEAD_DIM]
            weights_grad = dot(out_grad, value, 1, 1)
            inner = jnp.sum(weights * weights_grad, axis=-1, keepdims=True)
            score_grad = (weights * (weights_grad - inner)).astype(bf16)
            wide = score_grad.astype(f32)
            for r in range(BLOCK // QUARTER):
                for j in range(PARTS):
                    tile_sums[h, tile_at(i * (BLOCK // QUARTER) + r, j)] += wide[
                        r * QUARTER : (r + 1) * QUARTER, j * QUARTER : (j + 1) * QUARTER
                    ]
            dqkv_ref[rows, lo : lo + HEAD_DIM] = (
                dot(score_grad, key) * HEAD_DIM ** (-0.5)
            ).astype(bf16)
            key_grad += dot(query, score_grad, 0, 0)
            value_grad += dot(out_grad, weights.astype(bf16), 0, 0)
        dqkv_ref[:, CHANNELS + lo : CHANNELS + lo + HEAD_DIM] = jnp.transpose(key_grad).astype(bf16)
        dqkv_ref[:, 2 * CHANNELS + lo : 2 * CHANNELS + lo + HEAD_DIM] = jnp.transpose(
            value_grad
        ).astype(bf16)
    normed_grad = dot(dqkv_ref[...], w_ref[:, :QKV], 1, 1)
    out_ref[...] = normed_grad.astype(bf16)
    gain_ref[...] = jnp.sum(normed_grad * g_ref[:, :WIDTH].astype(f32), axis=0, keepdims=True)
    sums_ref[...] = jnp.zeros_like(sums_ref)
    for t, step in enumerate(TILE_STEPS):
        buckets = tile_buckets(step)
        for b in possible(step):
            mask = buckets == b
            for h in range(LOCAL_HEADS):
                sums_ref[h, b : b + 1] += jnp.sum(
                    jnp.where(mask, tile_sums[h, t], 0.0), axis=0, keepdims=True
                )


def projection_kernel(g0, g1, d0, d1, u0, u1, a0, a1, out_ref):
    out_ref[:, :QKV] = (
        dot(g0[:, :WIDTH], d0[...], 0, 0) + dot(g1[:, :WIDTH], d1[...], 0, 0)
    ).astype(bf16)
    out_ref[:, QKV:] = (dot(u0[...], a0[...], 0, 0) + dot(u1[...], a1[...], 0, 0)).astype(bf16)


def input_kernel(x_ref, gain_ref, grad_ref, t0, t1, out_ref):
    for s, term in ((0, t0), (1, t1)):
        x = x_ref[s]
        r = inverse_size(x)
        u = gain_ref[...] * term[...].astype(f32)
        out_ref[s] = (
            grad_ref[s * QUARTER : (s + 1) * QUARTER]
            + r * u
            - x * (r * r * r * jnp.mean(x * u, axis=-1, keepdims=True))
        )


def expert_spec(e):
    return pl.BlockSpec((1, WIDTH, WIDTH), lambda i: (e, 0, 0))


def body(
    inputs,
    projection_in,
    projection_out,
    gain_attention,
    gain_experts,
    router_weight,
    bias_table,
    expert_in,
    expert_out,
    routes,
    segments,
    cotangent,
):
    seq_here, quarter, width = inputs.shape
    rows = seq_here * quarter
    me = lax.axis_index("mp").reshape(1).astype(jnp.int32)
    first_head = me * LOCAL_HEADS
    gain1, gain2 = gain_attention.reshape(1, width), gain_experts.reshape(1, width)
    routes = routes.reshape(seq_here, quarter)
    upstream = cotangent.reshape(rows, width)
    piece = struct((QUARTER, WIDTH), bf16)
    slot_piece = struct((HALF_SLOTS, WIDTH), bf16)

    turned = jnp.concatenate(
        [jnp.moveaxis(projection_in, 1, 0).reshape(24, QKV), projection_out.T], axis=1
    )
    place, lines = call(
        place_kernel,
        (struct((rows, SLOTS), bf16), struct((32, 40, width), bf16)),
        (routes, upstream, turned),
        name="place",
    )
    lines = lax.all_to_all(lines, EXPERT, 0, 0, tiled=True)
    weights = lines[:, :24].reshape(WIDTH, QKV + CHANNELS)
    c_slots = by_expert(lines[:, 24:])

    tagged = struct((QUARTER, TAGGED), bf16)
    n0, n1 = call(start_kernel, (tagged, tagged), (inputs, gain1, segments), name="start")
    normed = (gather4(n0, 1), gather4(n1, -1))
    tiles = call(
        bias_kernel,
        struct((LOCAL_HEADS, len(TILE_STEPS), QUARTER, QUARTER), f32),
        (first_head, bias_table),
        [SMEM, SMEM],
        name="bias",
    )
    length = PARTS * QUARTER
    attended = [
        call(
            attend_kernel,
            (
                struct((length, TAGGED), bf16),
                struct((length, QKV), bf16),
                struct((length, CHANNELS), bf16),
                struct((length, 128), f32),
                piece, piece, piece, piece,
            ),
            (me, *normed[s], weights, tiles),
            [SMEM] + [VMEM] * 6,
            flops=2 * 10**9,
            name="attend",
        )
        for s in range(2)
    ]
    attention = [reduce4(attended[s][4:], (1, -1)[s])[0] for s in range(2)]

    c_all = [gather4(c, (1, -1)[e]) for e, c in enumerate(c_slots)]
    u = [
        call(
            upstream_kernel,
            struct((PARTS, HALF_SLOTS, WIDTH), bf16),
            (*c_all[e], expert_out),
            [VMEM] * 4 + [expert_spec(e)],
            flops=12 * 10**8,
            name="upstream",
        )
        for e in range(2)
    ]

    hidden, gate, slots = call(
        dispatch_kernel,
        (struct((rows, width), f32), struct((rows, 128), f32), struct((SLOTS, width), bf16)),
        (inputs, *attention[0], *attention[1], gain2, router_weight, routes, place),
        name="dispatch",
    )
    x_all = [gather4(x, (1, -1)[e]) for e, x in enumerate(by_expert(to_experts(slots)))]
    group = lax.axis_index(EXPERT).astype(jnp.int32)
    acts = struct((PARTS, HALF_SLOTS, WIDTH), bf16)
    pair = pl.BlockSpec((2, HALF_SLOTS, WIDTH), lambda i: (i, 0, 0))
    worked = []
    for e in range(2):
        earlier = (worked[0][4], u[0]) if e else (x_all[1][2], u[1])
        outs = pl.pallas_call(
            expert_kernel,
            grid=(2,),
            out_shape=(acts, acts, acts, struct((2 * EXPERTS, WIDTH), f32)) + (slot_piece,) * 4,
            in_specs=[SMEM] + [VMEM] * 4 + [pair, expert_spec(e), VMEM, ANY, ANY],
            out_specs=(pair, pair, pair) + (VMEM,) * 5,
            scratch_shapes=[pltpu.VMEM((SLOTS, WIDTH), f32)],
            cost_estimate=pl.CostEstimate(
                flops=24 * 10**8, bytes_accessed=2 * 10**7, transcendentals=0
            ),
            compiler_params=pltpu.CompilerParams(vmem_limit_bytes=VMEM_LIMIT),
            name="expert",
        )((group * 2 + e).reshape(1), *x_all[e], u[e], expert_in, router_weight, *earlier)
        worked.append(outs)
    slot_terms, middles = zip(reduce4(worked[0][4:], 1), reduce4(worked[1][4:], -1))
    returned = to_experts(summed_slots(slot_terms))
    outputs = [
        call(
            output_kernel,
            (slot_piece,) * 4,
            (worked[e][0], expert_out, *middles),
            [VMEM, expert_spec(e), ANY, ANY],
            flops=12 * 10**8,
            name="expert_output",
        )
        for e in range(2)
    ]
    whole = struct((2, WIDTH, WIDTH), f32)
    expert_grads, tokens = (), []
    for e in range(2):
        ins = (worked[e][1], worked[e][2], *c_all[e], *x_all[e])
        *expert_grads, token = pl.pallas_call(
            weights_kernel,
            grid=(1,),
            out_shape=(whole, whole, struct((8, 128), f32)),
            in_specs=[VMEM] * 10 + [pl.BlockSpec(memory_space=pl.ANY)] * len(expert_grads),
            out_specs=(expert_spec(e), expert_spec(e), VMEM),
            input_output_aliases={10: 0, 11: 1} if expert_grads else {},
            cost_estimate=pl.CostEstimate(
                flops=24 * 10**8, bytes_accessed=2 * 10**7, transcendentals=0
            ),
            compiler_params=pltpu.CompilerParams(vmem_limit_bytes=VMEM_LIMIT),
            name="expert_weights",
        )(*ins, *expert_grads)
        tokens.append(token)
    grad_expert_out, grad_expert_in = expert_grads

    output_slots = summed_slots([reduce4(outputs[e], (1, -1)[e])[0] for e in range(2)])
    hidden_grad, h0, h1, gain2_grad = call(
        back_kernel,
        (struct((rows, width), f32), piece, piece, struct((1, width), f32)),
        (returned.reshape(SLOTS, width), place, hidden, upstream, gain2, tokens[0]),
        [VMEM] * 5 + [ANY],
        name="back",
    )
    grads = (gather4(h0, 1), gather4(h1, -1))
    attended_back = [
        call(
            attend_back_kernel,
            (
                struct((length, width), bf16),
                struct((length, QKV), bf16),
                struct((LOCAL_HEADS, BUCKETS, 128), f32),
                struct((1, width), f32),
                struct((length, width), bf16),
            ),
            (me, *grads[s], weights, tiles, *attended[s][:2], attended[s][3], grads[1 - s][2]),
            [SMEM] + [VMEM] * 9 + [ANY],
            scratch=[pltpu.VMEM((LOCAL_HEADS, len(TILE_STEPS), QUARTER, QUARTER), f32)],
            flops=4 * 10**9,
            name="attend_back",
        )
        for s in range(2)
    ]
    normed_grad = [
        lax.psum_scatter(attended_back[s][4], "mp", scatter_dimension=0, tiled=True)
        for s in range(2)
    ]
    input_grad = call(
        input_kernel,
        struct(inputs.shape, f32),
        (inputs, gain1, hidden_grad, *normed_grad),
        name="input_gradient",
    )

    router = call(
        router_kernel,
        struct((WIDTH, EXPERTS), bf16),
        (worked[0][3], worked[1][3], h0),
        [VMEM, VMEM, ANY],
        name="router_gradient",
    ).reshape(32, 16, 96)
    router = jnp.pad(router, ((0, 0), (0, 0), (0, 32)))
    output_slots = jnp.concatenate([output_slots, router], axis=2)
    output_back = to_experts(output_slots)
    router_rows = jnp.sum(output_back[:, :, width : width + 96].astype(f32), axis=0)
    result = call(
        result_kernel,
        struct((rows, width), f32),
        (output_back[:, :, :width].reshape(SLOTS, width), place, hidden, gate),
        name="result",
    )
    partial = call(
        projection_kernel,
        struct((WIDTH, QKV + CHANNELS), bf16),
        (
            attended[0][0], attended[1][0], attended_back[0][1], attended_back[1][1],
            attended_back[0][0], attended_back[1][0], attended[0][2], attended[1][2],
        ),
        flops=16 * 10**8,
        name="projection_gradient",
    )
    table_local = jnp.sum(attended_back[0][2] + attended_back[1][2], axis=-1).T
    table = lax.dynamic_update_slice(
        jnp.zeros((BUCKETS, HEADS), f32), table_local, (0, first_head[0])
    )
    gain1_grad = (attended_back[0][3] + attended_back[1][3]) / gain1
    small = jnp.concatenate(
        [t.reshape(-1) for t in (router_rows, gain1_grad, gain2_grad, table)]
    ).reshape(27, 128)
    small = added(small, shift(small, 1), shift(small, -1), shift(small, 2)).reshape(-1)
    lines = jnp.pad(small.astype(bf16), (0, 5 * width - small.size)).reshape(1, 5, width)
    lines = jnp.concatenate(
        [partial.reshape(32, 24, width), jnp.broadcast_to(lines, (32, 5, width))], axis=1
    )
    arrived = lax.all_to_all(lines, EXPERT, 0, 0, tiled=True)
    projections = jnp.sum(arrived[:, :24].astype(f32), axis=0)
    grad_projection_in = jnp.moveaxis(projections[:, :QKV].reshape(24, 3, CHANNELS), 1, 0)
    grad_projection_out = projections[:, QKV:].T
    grad_router = arrived[:, 24:26].astype(f32).reshape(WIDTH, EXPERTS)
    late = jnp.sum(arrived[:, 26:].astype(f32), axis=0).reshape(-1)
    grad_gain_attention = late[:width]
    grad_gain_experts = late[width : 2 * width]
    grad_table = late[2 * width : 2 * width + BUCKETS * HEADS].reshape(BUCKETS, HEADS)
    return (
        result.reshape(seq_here, quarter, width),
        input_grad,
        grad_projection_in,
        grad_projection_out,
        grad_gain_attention,
        grad_gain_experts,
        grad_router,
        grad_table,
        grad_expert_in,
        grad_expert_out,
    )


def solution(mesh):
    split = Mesh(
        mesh.devices.reshape(4, 4, 2, mesh.shape["mp"]), ("expert_0", "expert_1", "expert_2", "mp")
    )
    in_specs = (
        P(EXPERT, "mp", None),
        P(None, EXPERT, "mp"),
        P("mp", EXPERT),
        P(),
        P(),
        P(),
        P(),
        P(EXPERT, None, "mp"),
        P(EXPERT, "mp", None),
        P(EXPERT, "mp", None),
        P(EXPERT, "mp"),
        P(EXPERT, "mp", None),
    )
    out_specs = (
        P(EXPERT, "mp", None),
        P(EXPERT, "mp", None),
        P(None, EXPERT, "mp"),
        P("mp", EXPERT),
        P(),
        P(),
        P(),
        P(),
        P(EXPERT, None, "mp"),
        P(EXPERT, "mp", None),
    )
    return jax.shard_map(body, mesh=split, in_specs=in_specs, out_specs=out_specs, check_vma=False)
```

```python
import functools
import math

import jax
import jax.numpy as jnp
from jax import lax
from jax.experimental import pallas as pl
from jax.experimental.pallas import tpu as pltpu
from jax.sharding import Mesh
from jax.sharding import PartitionSpec as P

HEADS = 12
HEAD_DIM = 64
EXPERTS = 64
BUCKETS = 32
REACH = 128
EXPERT = ("expert_0", "expert_1", "expert_2")
QUARTER = 128
PARTS = 4
WIDTH = 768
CHANNELS = 192
LOCAL_HEADS = CHANNELS // HEAD_DIM
QKV = 3 * CHANNELS
CAPACITY = 4
SLOTS = 512
HALF_SLOTS = SLOTS // 2
TAGGED = WIDTH + 128
TILE_STEPS = (0, 1, -1, 2, -2)

epsilon = 1e-06
f32 = jnp.float32
bf16 = jnp.bfloat16
BLOCK = 512
VMEM_LIMIT = 56 * 1024 * 1024


def dot(a, b, ca=1, cb=0, precision=None):
    return lax.dot_general(
        a, b, (((ca,), (cb,)), ((), ())), preferred_element_type=f32, precision=precision
    )


def struct(shape, dtype):
    return jax.ShapeDtypeStruct(shape, dtype)


ANY = pl.BlockSpec(memory_space=pl.ANY)
SMEM = pl.BlockSpec(memory_space=pltpu.SMEM)
VMEM = pl.BlockSpec(memory_space=pltpu.VMEM)


def call(kernel, outs, ins, in_specs=None, scratch=(), flops=10**8, moved=4 * 10**6, name=None):
    return pl.pallas_call(
        kernel,
        grid=(1,),
        out_shape=outs,
        in_specs=in_specs or [VMEM] * len(ins),
        out_specs=jax.tree.map(lambda _: VMEM, outs),
        scratch_shapes=scratch,
        cost_estimate=pl.CostEstimate(flops=flops, bytes_accessed=moved, transcendentals=0),
        compiler_params=pltpu.CompilerParams(vmem_limit_bytes=VMEM_LIMIT),
        name=name,
    )(*ins)


def shift(x, step):
    return lax.ppermute(x, "mp", [(i, (i + step) % PARTS) for i in range(PARTS)])


def gather4(x, way):
    left, right = shift(x, 1), shift(x, -1)
    far = shift(left, 1) if way > 0 else shift(right, -1)
    return x, right, far, left


def added(*terms):
    return functools.reduce(lambda a, b: a + b, [t.astype(f32) for t in terms])


def reduce4(pieces, way):
    own, right, far, left = pieces
    if way > 0:
        middle = right = added(right, shift(far, 1)).astype(bf16)
    else:
        middle = left = added(left, shift(far, -1)).astype(bf16)
    return (own, shift(right, 1), shift(left, -1)), middle


def to_experts(x):
    return lax.all_to_all(x.reshape(32, -1, x.shape[-1]), EXPERT, 0, 0, tiled=True)


def by_expert(slots):
    return tuple(slots[:, 8 * e : 8 * e + 8, :WIDTH].reshape(HALF_SLOTS, WIDTH) for e in range(2))


def summed_slots(terms):
    pieces = [added(*terms[e]).astype(bf16).reshape(32, 8, WIDTH) for e in range(2)]
    return jnp.concatenate(pieces, axis=1)


def sent_to_all(x, axis):
    peers = lax.axis_size(axis)
    return lax.all_to_all(jnp.broadcast_to(x[None], (peers, *x.shape)), axis, 0, 0, tiled=True)


def bucket_of(offsets):
    halfway = BUCKETS // 2
    exact_span = halfway // 2
    distance = jnp.abs(offsets)
    far_part = jnp.full_like(distance, exact_span)
    for step in range(1, exact_span):
        cutoff_level = math.ceil(exact_span * (REACH / exact_span) ** (step / exact_span) - 1e-09)
        far_part = far_part + jnp.where(distance >= cutoff_level, 1, 0)
    nearby = jnp.where(distance < exact_span, distance, far_part)
    return nearby + jnp.where(offsets > 0, halfway, 0)


def tile_buckets(step):
    shape = (QUARTER, QUARTER)
    offsets = (
        step * QUARTER
        + lax.broadcasted_iota(jnp.int32, shape, 1)
        - lax.broadcasted_iota(jnp.int32, shape, 0)
    )
    return bucket_of(offsets)


def possible(step):
    if step == 0:
        return range(BUCKETS)
    if step == 1:
        return range(BUCKETS // 2 + 1, BUCKETS)
    if step == -1:
        return range(1, BUCKETS // 2)
    return (BUCKETS - 1,) if step > 0 else (BUCKETS // 2 - 1,)


def tile_at(row_block, key_block):
    step = key_block - row_block
    return TILE_STEPS.index(max(-2, min(2, step)))


def bias_kernel(head_ref, table_ref, out_ref):
    head = head_ref[0]
    for t, step in enumerate(TILE_STEPS):
        buckets = tile_buckets(step)
        tiles = [jnp.zeros((QUARTER, QUARTER), f32)] * LOCAL_HEADS
        for b in possible(step):
            mask = buckets == b
            tiles = [jnp.where(mask, table_ref[b, head + h], tile) for h, tile in enumerate(tiles)]
        for h, tile in enumerate(tiles):
            out_ref[h, t] = tile


def inverse_size(values):
    return lax.rsqrt(jnp.mean(values * values, axis=-1, keepdims=True) + epsilon)


def as_column(row):
    return jnp.transpose(jnp.broadcast_to(row, (QUARTER, QUARTER)))


def start_kernel(x_ref, gain_ref, seg_ref, n0, n1):
    gain = gain_ref[...]
    for s, out in ((0, n0), (1, n1)):
        x = x_ref[s]
        out[:, :WIDTH] = (x * inverse_size(x) * gain).astype(bf16)
        out[:, WIDTH:] = as_column(seg_ref[s : s + 1].astype(f32)).astype(bf16)


def place_kernel(route_ref, cot_ref, weights_ref, place_ref, lines_ref):
    tri = (
        lax.broadcasted_iota(jnp.int32, (QUARTER, QUARTER), 0)
        >= lax.broadcasted_iota(jnp.int32, (QUARTER, QUARTER), 1)
    ).astype(bf16)
    for s in range(2):
        chosen = as_column(route_ref[s : s + 1].astype(f32)).astype(jnp.int32)
        mask = jnp.where(
            chosen == lax.broadcasted_iota(jnp.int32, (QUARTER, QUARTER), 1), 1.0, 0.0
        )
        running = dot(tri, mask.astype(bf16))
        rank = jnp.sum(mask * running, axis=-1, keepdims=True).astype(jnp.int32) - 1
        place = chosen[:, :1] * 8 + s * CAPACITY + rank
        slots = lax.broadcasted_iota(jnp.int32, (QUARTER, SLOTS), 1)
        place_ref[s * QUARTER : (s + 1) * QUARTER] = jnp.where(slots == place, 1.0, 0.0).astype(bf16)
    slots = dot(place_ref[...], cot_ref[...].astype(bf16), 0, 0)
    weights = weights_ref[...].astype(f32)
    for n in range(32):
        lines_ref[n] = jnp.concatenate([weights, slots[16 * n : 16 * n + 16]]).astype(bf16)


def position(me, k):
    return pl.multiple_of(lax.rem(me + k, PARTS) * QUARTER, QUARTER)


def same_document(g_ref):
    column = g_ref[:, WIDTH:].astype(f32)
    return column, jnp.transpose(column)[:1]


def bias_rows(tiles_ref, h, i):
    per = BLOCK // QUARTER
    return jnp.concatenate(
        [
            jnp.concatenate([tiles_ref[h, tile_at(r, j)] for j in range(PARTS)], axis=1)
            for r in range(i * per, (i + 1) * per)
        ],
        axis=0,
    )


def attend_kernel(
    me_ref, a0, a1, a2, a3, w_ref, tiles_ref, g_ref, qkv_ref, att_ref, lse_ref, p0, p1, p2, p3
):
    me = me_ref[0]
    for k, piece in enumerate((a0, a1, a2, a3)):
        g_ref[pl.ds(position(me, k), QUARTER), :] = piece[...]
    qkv_ref[...] = dot(g_ref[:, :WIDTH], w_ref[:, :QKV]).astype(bf16)
    column, row = same_document(g_ref)
    lse_ref[...] = jnp.zeros_like(lse_ref)
    for h in range(LOCAL_HEADS):
        lo = h * HEAD_DIM
        key = qkv_ref[:, CHANNELS + lo : CHANNELS + lo + HEAD_DIM]
        value = qkv_ref[:, 2 * CHANNELS + lo : 2 * CHANNELS + lo + HEAD_DIM]
        for i in range(PARTS * QUARTER // BLOCK):
            rows = slice(i * BLOCK, (i + 1) * BLOCK)
            query = qkv_ref[rows, lo : lo + HEAD_DIM] * HEAD_DIM ** (-0.5)
            scores = dot(query, key, 1, 1) + bias_rows(tiles_ref, h, i)
            scores = jnp.where(column[rows, :1] == row, scores, -1000000000.0)
            row_max = jnp.max(scores, axis=-1, keepdims=True)
            expos = jnp.exp(scores - row_max)
            total = jnp.sum(expos, axis=-1, keepdims=True)
            weights = (expos * (1.0 / total)).astype(bf16)
            att_ref[rows, lo : lo + HEAD_DIM] = dot(weights, value).astype(bf16)
            lse_ref[rows, h : h + 1] = row_max + jnp.log(total)
    for k, out in enumerate((p0, p1, p2, p3)):
        mine = att_ref[pl.ds(position(me, k), QUARTER), :]
        out[...] = dot(mine, w_ref[:, QKV:], 1, 1).astype(bf16)


def dispatch_kernel(
    x_ref, t00, t01, t02, t10, t11, t12, gain_ref, router_ref, route_ref, place_ref,
    hidden_ref, gate_ref, slots_ref,
):
    for s, terms in ((0, (t00, t01, t02)), (1, (t10, t11, t12))):
        rows = slice(s * QUARTER, (s + 1) * QUARTER)
        hidden_ref[rows] = x_ref[s] + added(*[t[...] for t in terms])
    hidden = hidden_ref[...]
    mixed = hidden * inverse_size(hidden) * gain_ref[...]
    low = mixed.astype(bf16)
    slots_ref[...] = dot(place_ref[...], low, 0, 0).astype(bf16)
    logits = dot(mixed, router_ref[...], precision=lax.Precision.HIGHEST)
    expos = jnp.exp(logits - jnp.max(logits, axis=-1, keepdims=True))
    shares = expos / jnp.sum(expos, axis=-1, keepdims=True)
    for s in range(2):
        rows = slice(s * QUARTER, (s + 1) * QUARTER)
        chosen = as_column(route_ref[s : s + 1].astype(f32)).astype(jnp.int32)[:, :EXPERTS]
        mask = chosen == lax.broadcasted_iota(jnp.int32, (QUARTER, EXPERTS), 1)
        gate = jnp.sum(jnp.where(mask, shares[rows], 0.0), axis=-1, keepdims=True)
        gate_ref[rows] = jnp.broadcast_to(gate, (QUARTER, 128))


WORK_ORDER = (2, 1, 3, 0)


def upstream_kernel(c0, c1, c2, c3, w_ref, u_ref):
    pieces = (c0, c1, c2, c3)
    for n, k in enumerate(WORK_ORDER):
        u_ref[n] = dot(pieces[k][...], w_ref[0], 1, 1).astype(bf16)


def expert_kernel(
    own_ref, x0, x1, x2, x3, u_ref, w_ref, router_ref, _, __,
    active_ref, scaled_ref, grad_ref, logit_ref, s0, s1, s2, s3, pre_ref,
):
    own = own_ref[0]
    router = router_ref[...]
    router_hi = router.astype(bf16)
    router_lo = (router - router_hi.astype(f32)).astype(bf16)
    router_both = jnp.concatenate([router_hi, router_lo], axis=1)
    c = math.sqrt(2.0 / math.pi)
    ca = c * 0.044715

    def work(xs, outs, first):
        x = jnp.concatenate([x_ref[...] for x_ref in xs])
        logits = dot(x, router_both)
        logits = logits[:, :EXPERTS] + logits[:, EXPERTS:]
        expos = jnp.exp(logits - jnp.max(logits, axis=-1, keepdims=True))
        shares = expos / jnp.sum(expos, axis=-1, keepdims=True)
        chosen = jnp.where(lax.broadcasted_iota(jnp.int32, shares.shape, 1) == own, 1.0, 0.0)
        gate = jnp.sum(shares * chosen, axis=-1, keepdims=True)
        pre_ref[...] = dot(x, w_ref[0])
        gate_grads = []
        for n in range(2):
            for part in range(HALF_SLOTS // 64):
                rows = slice(part * 64, part * 64 + 64)
                at = slice(n * HALF_SLOTS + part * 64, n * HALF_SLOTS + part * 64 + 64)
                pre = pre_ref[at, :]
                u = u_ref[n, rows, :].astype(f32)
                square = pre * pre
                t = jnp.tanh(pre * (c + ca * square))
                half = 0.5 + 0.5 * t
                active = pre * half
                slope = half + (0.5 * pre) * (1.0 - t * t) * (c + 3.0 * ca * square)
                gate_grads.append(jnp.sum(active * u, axis=-1, keepdims=True))
                active_ref[n, rows, :] = active.astype(bf16)
                scaled_ref[n, rows, :] = (gate[at] * active).astype(bf16)
                grad_ref[n, rows, :] = (gate[at] * u * slope).astype(bf16)
        logit_grad = shares * (chosen - gate) * jnp.concatenate(gate_grads)
        logit_hi = logit_grad.astype(bf16)
        logit_lo = (logit_grad - logit_hi.astype(f32)).astype(bf16)
        pre_grad = jnp.concatenate([grad_ref[0], grad_ref[1]])
        slot_grad = dot(pre_grad, w_ref[0], 1, 1) + dot(logit_hi, router_hi, 1, 1)
        for n, out in enumerate(outs):
            out[...] = slot_grad[n * HALF_SLOTS : (n + 1) * HALF_SLOTS].astype(bf16)
        term = dot(jnp.concatenate([logit_hi, logit_lo], axis=1), x, 0, 0)
        if first:
            logit_ref[...] = term
        else:
            logit_ref[...] += term

    pl.when(pl.program_id(0) == 0)(lambda: work((x2, x1), (s2, s1), True))
    pl.when(pl.program_id(0) == 1)(lambda: work((x3, x0), (s3, s0), False))


def output_kernel(active_ref, w_ref, _, __, s0, s1, s2, s3):
    outs = (s0, s1, s2, s3)
    for n, k in enumerate(WORK_ORDER):
        outs[k][...] = dot(active_ref[n], w_ref[0]).astype(bf16)


def weights_kernel(scaled_ref, grad_ref, c0, c1, c2, c3, x0, x1, x2, x3, *rest):
    out_ref, in_ref, token_ref = rest[-3:]
    token_ref[...] = jnp.zeros_like(token_ref)
    upstream, entered = (c0, c1, c2, c3), (x0, x1, x2, x3)
    for n, k in enumerate(WORK_ORDER):
        out_term = dot(scaled_ref[n], upstream[k][...], 0, 0)
        in_term = dot(entered[k][...], grad_ref[n], 0, 0)
        if n == 0:
            out_ref[0] = out_term
            in_ref[0] = in_term
        else:
            out_ref[0] += out_term
            in_ref[0] += in_term


def router_kernel(a_ref, b_ref, _, out_ref):
    both = a_ref[...] + b_ref[...]
    rows = jnp.transpose(both[:EXPERTS] + both[EXPERTS:])
    none = jnp.zeros((8, EXPERTS), f32)
    for n in range(32):
        top, low = rows[24 * n : 24 * n + 16], rows[24 * n + 16 : 24 * n + 24]
        beside = jnp.concatenate([low, none])
        out_ref[n] = jnp.concatenate([top, beside], axis=1).astype(bf16)


def back_kernel(
    slots_ref, place_ref, hidden_ref, cot_ref, gain_ref, _, __, grad_ref, h0, h1, gain_grad_ref
):
    mixed_grad = dot(place_ref[...], slots_ref[...])
    hidden = hidden_ref[...]
    r = inverse_size(hidden)
    gain_grad_ref[...] = jnp.sum(mixed_grad * hidden * r, axis=0, keepdims=True)
    u = gain_ref[...] * mixed_grad
    grad = cot_ref[...] + r * u - hidden * (r * r * r * jnp.mean(hidden * u, axis=-1, keepdims=True))
    grad_ref[...] = grad
    h0[...] = grad[:QUARTER].astype(bf16)
    h1[...] = grad[QUARTER:].astype(bf16)


def result_kernel(slots_ref, place_ref, hidden_ref, gate_ref, out_ref):
    back = dot(place_ref[...], slots_ref[...])
    out_ref[...] = hidden_ref[...] + gate_ref[:, :1] * back


def attend_back_kernel(
    me_ref, a0, a1, a2, a3, w_ref, tiles_ref, g_ref, qkv_ref, lse_ref, _, __, ___,
    up_ref, dqkv_ref, sums_ref, gain_ref, out_ref, tile_sums,
):
    me = me_ref[0]
    for k, piece in enumerate((a0, a1, a2, a3)):
        up_ref[pl.ds(position(me, k), QUARTER), :] = piece[...]
    att_grad = dot(up_ref[...], w_ref[:, QKV:]).astype(bf16)
    column, row = same_document(g_ref)
    tile_sums[...] = jnp.zeros_like(tile_sums)
    for h in range(LOCAL_HEADS):
        lo = h * HEAD_DIM
        key = qkv_ref[:, CHANNELS + lo : CHANNELS + lo + HEAD_DIM]
        value = qkv_ref[:, 2 * CHANNELS + lo : 2 * CHANNELS + lo + HEAD_DIM]
        key_grad = jnp.zeros((HEAD_DIM, PARTS * QUARTER), f32)
        value_grad = jnp.zeros((HEAD_DIM, PARTS * QUARTER), f32)
        for i in range(PARTS * QUARTER // BLOCK):
            rows = slice(i * BLOCK, (i + 1) * BLOCK)
            query = qkv_ref[rows, lo : lo + HEAD_DIM] * HEAD_DIM ** (-0.5)
            scores = dot(query, key, 1, 1) + bias_rows(tiles_ref, h, i)
            scores = jnp.where(column[rows, :1] == row, scores, -1000000000.0)
            weights = jnp.exp(scores - lse_ref[rows, h : h + 1])
            out_grad = att_grad[rows, lo : lo + HEAD_DIM]
            weights_grad = dot(out_grad, value, 1, 1)
            inner = jnp.sum(weights * weights_grad, axis=-1, keepdims=True)
            score_grad = (weights * (weights_grad - inner)).astype(bf16)
            wide = score_grad.astype(f32)
            for r in range(BLOCK // QUARTER):
                for j in range(PARTS):
                    tile_sums[h, tile_at(i * (BLOCK // QUARTER) + r, j)] += wide[
                        r * QUARTER : (r + 1) * QUARTER, j * QUARTER : (j + 1) * QUARTER
                    ]
            dqkv_ref[rows, lo : lo + HEAD_DIM] = (
                dot(score_grad, key) * HEAD_DIM ** (-0.5)
            ).astype(bf16)
            key_grad += dot(query, score_grad, 0, 0)
            value_grad += dot(out_grad, weights.astype(bf16), 0, 0)
        dqkv_ref[:, CHANNELS + lo : CHANNELS + lo + HEAD_DIM] = jnp.transpose(key_grad).astype(bf16)
        dqkv_ref[:, 2 * CHANNELS + lo : 2 * CHANNELS + lo + HEAD_DIM] = jnp.transpose(
            value_grad
        ).astype(bf16)
    normed_grad = dot(dqkv_ref[...], w_ref[:, :QKV], 1, 1)
    out_ref[...] = normed_grad.astype(bf16)
    gain_ref[...] = jnp.sum(normed_grad * g_ref[:, :WIDTH].astype(f32), axis=0, keepdims=True)
    sums_ref[...] = jnp.zeros_like(sums_ref)
    for t, step in enumerate(TILE_STEPS):
        buckets = tile_buckets(step)
        for b in possible(step):
            mask = buckets == b
            for h in range(LOCAL_HEADS):
                sums_ref[h, b : b + 1] += jnp.sum(
                    jnp.where(mask, tile_sums[h, t], 0.0), axis=0, keepdims=True
                )


def projection_kernel(g0, g1, d0, d1, u0, u1, a0, a1, out_ref):
    out_ref[:, :QKV] = (
        dot(g0[:, :WIDTH], d0[...], 0, 0) + dot(g1[:, :WIDTH], d1[...], 0, 0)
    ).astype(bf16)
    out_ref[:, QKV:] = (dot(u0[...], a0[...], 0, 0) + dot(u1[...], a1[...], 0, 0)).astype(bf16)


def input_kernel(x_ref, gain_ref, grad_ref, t0, t1, out_ref):
    for s, term in ((0, t0), (1, t1)):
        x = x_ref[s]
        r = inverse_size(x)
        u = gain_ref[...] * term[...].astype(f32)
        out_ref[s] = (
            grad_ref[s * QUARTER : (s + 1) * QUARTER]
            + r * u
            - x * (r * r * r * jnp.mean(x * u, axis=-1, keepdims=True))
        )


def expert_spec(e):
    return pl.BlockSpec((1, WIDTH, WIDTH), lambda i: (e, 0, 0))


def body(
    inputs,
    projection_in,
    projection_out,
    gain_attention,
    gain_experts,
    router_weight,
    bias_table,
    expert_in,
    expert_out,
    routes,
    segments,
    cotangent,
):
    seq_here, quarter, width = inputs.shape
    rows = seq_here * quarter
    me = lax.axis_index("mp").reshape(1).astype(jnp.int32)
    first_head = me * LOCAL_HEADS
    gain1, gain2 = gain_attention.reshape(1, width), gain_experts.reshape(1, width)
    routes = routes.reshape(seq_here, quarter)
    upstream = cotangent.reshape(rows, width)
    piece = struct((QUARTER, WIDTH), bf16)
    slot_piece = struct((HALF_SLOTS, WIDTH), bf16)

    turned = jnp.concatenate(
        [jnp.moveaxis(projection_in, 1, 0).reshape(24, QKV), projection_out.T], axis=1
    )
    place, lines = call(
        place_kernel,
        (struct((rows, SLOTS), bf16), struct((32, 40, width), bf16)),
        (routes, upstream, turned),
        name="place",
    )
    lines = lax.all_to_all(lines, EXPERT, 0, 0, tiled=True)
    weights = lines[:, :24].reshape(WIDTH, QKV + CHANNELS)
    c_slots = by_expert(lines[:, 24:])

    tagged = struct((QUARTER, TAGGED), bf16)
    n0, n1 = call(start_kernel, (tagged, tagged), (inputs, gain1, segments), name="start")
    normed = (gather4(n0, 1), gather4(n1, -1))
    tiles = call(
        bias_kernel,
        struct((LOCAL_HEADS, len(TILE_STEPS), QUARTER, QUARTER), f32),
        (first_head, bias_table),
        [SMEM, SMEM],
        name="bias",
    )
    length = PARTS * QUARTER
    attended = [
        call(
            attend_kernel,
            (
                struct((length, TAGGED), bf16),
                struct((length, QKV), bf16),
                struct((length, CHANNELS), bf16),
                struct((length, 128), f32),
                piece, piece, piece, piece,
            ),
            (me, *normed[s], weights, tiles),
            [SMEM] + [VMEM] * 6,
            flops=2 * 10**9,
            name="attend",
        )
        for s in range(2)
    ]
    attention = [reduce4(attended[s][4:], (1, -1)[s])[0] for s in range(2)]

    c_all = [gather4(c, (1, -1)[e]) for e, c in enumerate(c_slots)]
    u = [
        call(
            upstream_kernel,
            struct((PARTS, HALF_SLOTS, WIDTH), bf16),
            (*c_all[e], expert_out),
            [VMEM] * 4 + [expert_spec(e)],
            flops=12 * 10**8,
            name="upstream",
        )
        for e in range(2)
    ]

    hidden, gate, slots = call(
        dispatch_kernel,
        (struct((rows, width), f32), struct((rows, 128), f32), struct((SLOTS, width), bf16)),
        (inputs, *attention[0], *attention[1], gain2, router_weight, routes, place),
        name="dispatch",
    )
    x_all = [gather4(x, (1, -1)[e]) for e, x in enumerate(by_expert(to_experts(slots)))]
    group = lax.axis_index(EXPERT).astype(jnp.int32)
    acts = struct((PARTS, HALF_SLOTS, WIDTH), bf16)
    pair = pl.BlockSpec((2, HALF_SLOTS, WIDTH), lambda i: (i, 0, 0))
    worked = []
    for e in range(2):
        earlier = (worked[0][4], u[0]) if e else (x_all[1][2], u[1])
        outs = pl.pallas_call(
            expert_kernel,
            grid=(2,),
            out_shape=(acts, acts, acts, struct((2 * EXPERTS, WIDTH), f32)) + (slot_piece,) * 4,
            in_specs=[SMEM] + [VMEM] * 4 + [pair, expert_spec(e), VMEM, ANY, ANY],
            out_specs=(pair, pair, pair) + (VMEM,) * 5,
            scratch_shapes=[pltpu.VMEM((SLOTS, WIDTH), f32)],
            cost_estimate=pl.CostEstimate(
                flops=24 * 10**8, bytes_accessed=2 * 10**7, transcendentals=0
            ),
            compiler_params=pltpu.CompilerParams(vmem_limit_bytes=VMEM_LIMIT),
            name="expert",
        )((group * 2 + e).reshape(1), *x_all[e], u[e], expert_in, router_weight, *earlier)
        worked.append(outs)
    slot_terms, middles = zip(reduce4(worked[0][4:], 1), reduce4(worked[1][4:], -1))
    returned = to_experts(summed_slots(slot_terms))
    outputs = [
        call(
            output_kernel,
            (slot_piece,) * 4,
            (worked[e][0], expert_out, *middles),
            [VMEM, expert_spec(e), ANY, ANY],
            flops=12 * 10**8,
            name="expert_output",
        )
        for e in range(2)
    ]
    whole = struct((2, WIDTH, WIDTH), f32)
    expert_grads, tokens = (), []
    for e in range(2):
        ins = (worked[e][1], worked[e][2], *c_all[e], *x_all[e])
        *expert_grads, token = pl.pallas_call(
            weights_kernel,
            grid=(1,),
            out_shape=(whole, whole, struct((8, 128), f32)),
            in_specs=[VMEM] * 10 + [pl.BlockSpec(memory_space=pl.ANY)] * len(expert_grads),
            out_specs=(expert_spec(e), expert_spec(e), VMEM),
            input_output_aliases={10: 0, 11: 1} if expert_grads else {},
            cost_estimate=pl.CostEstimate(
                flops=24 * 10**8, bytes_accessed=2 * 10**7, transcendentals=0
            ),
            compiler_params=pltpu.CompilerParams(vmem_limit_bytes=VMEM_LIMIT),
            name="expert_weights",
        )(*ins, *expert_grads)
        tokens.append(token)
    grad_expert_out, grad_expert_in = expert_grads

    output_slots = summed_slots([reduce4(outputs[e], (1, -1)[e])[0] for e in range(2)])
    router = call(
        router_kernel,
        struct((32, 16, 128), bf16),
        (worked[0][3], worked[1][3], middles[0]),
        [VMEM, VMEM, ANY],
        name="router_gradient",
    )
    hidden_grad, h0, h1, gain2_grad = call(
        back_kernel,
        (struct((rows, width), f32), piece, piece, struct((1, width), f32)),
        (returned.reshape(SLOTS, width), place, hidden, upstream, gain2, tokens[0], router),
        [VMEM] * 5 + [ANY] * 2,
        name="back",
    )
    grads = (gather4(h0, 1), gather4(h1, -1))
    attended_back = [
        call(
            attend_back_kernel,
            (
                struct((length, width), bf16),
                struct((length, QKV), bf16),
                struct((LOCAL_HEADS, BUCKETS, 128), f32),
                struct((1, width), f32),
                struct((length, width), bf16),
            ),
            (me, *grads[s], weights, tiles, *attended[s][:2], attended[s][3], *grads[1 - s][1:]),
            [SMEM] + [VMEM] * 9 + [ANY] * 3,
            scratch=[pltpu.VMEM((LOCAL_HEADS, len(TILE_STEPS), QUARTER, QUARTER), f32)],
            flops=4 * 10**9,
            name="attend_back",
        )
        for s in range(2)
    ]
    normed_grad = [
        lax.psum_scatter(attended_back[s][4], "mp", scatter_dimension=0, tiled=True)
        for s in range(2)
    ]
    input_grad = call(
        input_kernel,
        struct(inputs.shape, f32),
        (inputs, gain1, hidden_grad, *normed_grad),
        name="input_gradient",
    )

    output_slots = jnp.concatenate([output_slots, router], axis=2)
    output_back = to_experts(output_slots)
    router_rows = jnp.sum(output_back[:, :, width:].astype(f32), axis=0)
    router_rows = jnp.concatenate([router_rows[:, :EXPERTS], router_rows[:8, EXPERTS:]])
    result = call(
        result_kernel,
        struct((rows, width), f32),
        (output_back[:, :, :width].reshape(SLOTS, width), place, hidden, gate),
        name="result",
    )
    partial = call(
        projection_kernel,
        struct((WIDTH, QKV + CHANNELS), bf16),
        (
            attended[0][0], attended[1][0], attended_back[0][1], attended_back[1][1],
            attended_back[0][0], attended_back[1][0], attended[0][2], attended[1][2],
        ),
        flops=16 * 10**8,
        name="projection_gradient",
    )
    table_local = jnp.sum(attended_back[0][2] + attended_back[1][2], axis=-1).T
    table = lax.dynamic_update_slice(
        jnp.zeros((BUCKETS, HEADS), f32), table_local, (0, first_head[0])
    )
    gain1_grad = (attended_back[0][3] + attended_back[1][3]) / gain1
    small = jnp.concatenate(
        [t.reshape(-1) for t in (router_rows, gain1_grad, gain2_grad, table)]
    ).reshape(27, 128)
    small = added(small, shift(small, 1), shift(small, -1), shift(small, 2)).reshape(-1)
    lines = jnp.pad(small.astype(bf16), (0, 5 * width - small.size)).reshape(1, 5, width)
    lines = jnp.concatenate(
        [partial.reshape(32, 24, width), jnp.broadcast_to(lines, (32, 5, width))], axis=1
    )
    arrived = lax.all_to_all(lines, EXPERT, 0, 0, tiled=True)
    projections = jnp.sum(arrived[:, :24].astype(f32), axis=0)
    grad_projection_in = jnp.moveaxis(projections[:, :QKV].reshape(24, 3, CHANNELS), 1, 0)
    grad_projection_out = projections[:, QKV:].T
    grad_router = arrived[:, 24:26].astype(f32).reshape(WIDTH, EXPERTS)
    late = jnp.sum(arrived[:, 26:].astype(f32), axis=0).reshape(-1)
    grad_gain_attention = late[:width]
    grad_gain_experts = late[width : 2 * width]
    grad_table = late[2 * width : 2 * width + BUCKETS * HEADS].reshape(BUCKETS, HEADS)
    return (
        result.reshape(seq_here, quarter, width),
        input_grad,
        grad_projection_in,
        grad_projection_out,
        grad_gain_attention,
        grad_gain_experts,
        grad_router,
        grad_table,
        grad_expert_in,
        grad_expert_out,
    )


def solution(mesh):
    split = Mesh(
        mesh.devices.reshape(4, 4, 2, mesh.shape["mp"]), ("expert_0", "expert_1", "expert_2", "mp")
    )
    in_specs = (
        P(EXPERT, "mp", None),
        P(None, EXPERT, "mp"),
        P("mp", EXPERT),
        P(),
        P(),
        P(),
        P(),
        P(EXPERT, None, "mp"),
        P(EXPERT, "mp", None),
        P(EXPERT, "mp", None),
        P(EXPERT, "mp"),
        P(EXPERT, "mp", None),
    )
    out_specs = (
        P(EXPERT, "mp", None),
        P(EXPERT, "mp", None),
        P(None, EXPERT, "mp"),
        P("mp", EXPERT),
        P(),
        P(),
        P(),
        P(),
        P(EXPERT, None, "mp"),
        P(EXPERT, "mp", None),
    )
    return jax.shard_map(body, mesh=split, in_specs=in_specs, out_specs=out_specs, check_vma=False)
```

```python
import functools
import math

import jax
import jax.numpy as jnp
from jax import lax
from jax.experimental import pallas as pl
from jax.experimental.pallas import tpu as pltpu
from jax.sharding import Mesh
from jax.sharding import PartitionSpec as P

HEADS = 12
HEAD_DIM = 64
EXPERTS = 64
BUCKETS = 32
REACH = 128
EXPERT = ("expert_0", "expert_1", "expert_2")
QUARTER = 128
PARTS = 4
WIDTH = 768
CHANNELS = 192
LOCAL_HEADS = CHANNELS // HEAD_DIM
QKV = 3 * CHANNELS
CAPACITY = 4
SLOTS = 512
HALF_SLOTS = SLOTS // 2
TAGGED = WIDTH + 128
TILE_STEPS = (0, 1, -1, 2, -2)

epsilon = 1e-06
f32 = jnp.float32
bf16 = jnp.bfloat16
BLOCK = 512
VMEM_LIMIT = 56 * 1024 * 1024


def dot(a, b, ca=1, cb=0, precision=None):
    return lax.dot_general(
        a, b, (((ca,), (cb,)), ((), ())), preferred_element_type=f32, precision=precision
    )


def struct(shape, dtype):
    return jax.ShapeDtypeStruct(shape, dtype)


ANY = pl.BlockSpec(memory_space=pl.ANY)
SMEM = pl.BlockSpec(memory_space=pltpu.SMEM)
VMEM = pl.BlockSpec(memory_space=pltpu.VMEM)


def call(kernel, outs, ins, in_specs=None, scratch=(), flops=10**8, moved=4 * 10**6, name=None):
    return pl.pallas_call(
        kernel,
        grid=(1,),
        out_shape=outs,
        in_specs=in_specs or [VMEM] * len(ins),
        out_specs=jax.tree.map(lambda _: VMEM, outs),
        scratch_shapes=scratch,
        cost_estimate=pl.CostEstimate(flops=flops, bytes_accessed=moved, transcendentals=0),
        compiler_params=pltpu.CompilerParams(vmem_limit_bytes=VMEM_LIMIT),
        name=name,
    )(*ins)


def shift(x, step):
    return lax.ppermute(x, "mp", [(i, (i + step) % PARTS) for i in range(PARTS)])


def gather4(x, way):
    left, right = shift(x, 1), shift(x, -1)
    far = shift(left, 1) if way > 0 else shift(right, -1)
    return x, right, far, left


def added(*terms):
    return functools.reduce(lambda a, b: a + b, [t.astype(f32) for t in terms])


def reduce4(pieces, way):
    own, right, far, left = pieces
    if way > 0:
        middle = right = added(right, shift(far, 1)).astype(bf16)
    else:
        middle = left = added(left, shift(far, -1)).astype(bf16)
    return (own, shift(right, 1), shift(left, -1)), middle


def to_experts(x):
    return lax.all_to_all(x.reshape(32, -1, x.shape[-1]), EXPERT, 0, 0, tiled=True)


def by_expert(slots):
    return tuple(slots[:, 8 * e : 8 * e + 8, :WIDTH].reshape(HALF_SLOTS, WIDTH) for e in range(2))


def summed_slots(terms):
    pieces = [added(*terms[e]).astype(bf16).reshape(32, 8, WIDTH) for e in range(2)]
    return jnp.concatenate(pieces, axis=1)


def sent_to_all(x, axis):
    peers = lax.axis_size(axis)
    return lax.all_to_all(jnp.broadcast_to(x[None], (peers, *x.shape)), axis, 0, 0, tiled=True)


def bucket_of(offsets):
    halfway = BUCKETS // 2
    exact_span = halfway // 2
    distance = jnp.abs(offsets)
    far_part = jnp.full_like(distance, exact_span)
    for step in range(1, exact_span):
        cutoff_level = math.ceil(exact_span * (REACH / exact_span) ** (step / exact_span) - 1e-09)
        far_part = far_part + jnp.where(distance >= cutoff_level, 1, 0)
    nearby = jnp.where(distance < exact_span, distance, far_part)
    return nearby + jnp.where(offsets > 0, halfway, 0)


def tile_buckets(step):
    shape = (QUARTER, QUARTER)
    offsets = (
        step * QUARTER
        + lax.broadcasted_iota(jnp.int32, shape, 1)
        - lax.broadcasted_iota(jnp.int32, shape, 0)
    )
    return bucket_of(offsets)


def possible(step):
    if step == 0:
        return range(BUCKETS)
    if step == 1:
        return range(BUCKETS // 2 + 1, BUCKETS)
    if step == -1:
        return range(1, BUCKETS // 2)
    return (BUCKETS - 1,) if step > 0 else (BUCKETS // 2 - 1,)


def tile_at(row_block, key_block):
    step = key_block - row_block
    return TILE_STEPS.index(max(-2, min(2, step)))


def bias_kernel(head_ref, table_ref, out_ref):
    head = head_ref[0]
    for t, step in enumerate(TILE_STEPS):
        buckets = tile_buckets(step)
        tiles = [jnp.zeros((QUARTER, QUARTER), f32)] * LOCAL_HEADS
        for b in possible(step):
            mask = buckets == b
            tiles = [jnp.where(mask, table_ref[b, head + h], tile) for h, tile in enumerate(tiles)]
        for h, tile in enumerate(tiles):
            out_ref[h, t] = tile


def inverse_size(values):
    return lax.rsqrt(jnp.mean(values * values, axis=-1, keepdims=True) + epsilon)


def as_column(row):
    return jnp.transpose(jnp.broadcast_to(row, (QUARTER, QUARTER)))


def start_kernel(x_ref, gain_ref, seg_ref, n0, n1):
    gain = gain_ref[...]
    for s, out in ((0, n0), (1, n1)):
        x = x_ref[s]
        out[:, :WIDTH] = (x * inverse_size(x) * gain).astype(bf16)
        out[:, WIDTH:] = as_column(seg_ref[s : s + 1].astype(f32)).astype(bf16)


def place_kernel(route_ref, cot_ref, weights_ref, place_ref, lines_ref):
    tri = (
        lax.broadcasted_iota(jnp.int32, (QUARTER, QUARTER), 0)
        >= lax.broadcasted_iota(jnp.int32, (QUARTER, QUARTER), 1)
    ).astype(bf16)
    for s in range(2):
        chosen = as_column(route_ref[s : s + 1].astype(f32)).astype(jnp.int32)
        mask = jnp.where(
            chosen == lax.broadcasted_iota(jnp.int32, (QUARTER, QUARTER), 1), 1.0, 0.0
        )
        running = dot(tri, mask.astype(bf16))
        rank = jnp.sum(mask * running, axis=-1, keepdims=True).astype(jnp.int32) - 1
        place = chosen[:, :1] * 8 + s * CAPACITY + rank
        slots = lax.broadcasted_iota(jnp.int32, (QUARTER, SLOTS), 1)
        place_ref[s * QUARTER : (s + 1) * QUARTER] = jnp.where(slots == place, 1.0, 0.0).astype(bf16)
    slots = dot(place_ref[...], cot_ref[...].astype(bf16), 0, 0)
    weights = weights_ref[...].astype(f32)
    for n in range(32):
        lines_ref[n] = jnp.concatenate([weights, slots[16 * n : 16 * n + 16]]).astype(bf16)


def position(me, k):
    return pl.multiple_of(lax.rem(me + k, PARTS) * QUARTER, QUARTER)


def same_document(g_ref):
    column = g_ref[:, WIDTH:].astype(f32)
    return column, jnp.transpose(column)[:1]


def bias_rows(tiles_ref, h, i):
    per = BLOCK // QUARTER
    return jnp.concatenate(
        [
            jnp.concatenate([tiles_ref[h, tile_at(r, j)] for j in range(PARTS)], axis=1)
            for r in range(i * per, (i + 1) * per)
        ],
        axis=0,
    )


def attend_kernel(
    me_ref, a0, a1, a2, a3, w_ref, tiles_ref, g_ref, qkv_ref, att_ref, lse_ref, p0, p1, p2, p3
):
    me = me_ref[0]
    for k, piece in enumerate((a0, a1, a2, a3)):
        g_ref[pl.ds(position(me, k), QUARTER), :] = piece[...]
    qkv_ref[...] = dot(g_ref[:, :WIDTH], w_ref[:, :QKV]).astype(bf16)
    column, row = same_document(g_ref)
    lse_ref[...] = jnp.zeros_like(lse_ref)
    for h in range(LOCAL_HEADS):
        lo = h * HEAD_DIM
        key = qkv_ref[:, CHANNELS + lo : CHANNELS + lo + HEAD_DIM]
        value = qkv_ref[:, 2 * CHANNELS + lo : 2 * CHANNELS + lo + HEAD_DIM]
        for i in range(PARTS * QUARTER // BLOCK):
            rows = slice(i * BLOCK, (i + 1) * BLOCK)
            query = qkv_ref[rows, lo : lo + HEAD_DIM] * HEAD_DIM ** (-0.5)
            scores = dot(query, key, 1, 1) + bias_rows(tiles_ref, h, i)
            scores = jnp.where(column[rows, :1] == row, scores, -1000000000.0)
            row_max = jnp.max(scores, axis=-1, keepdims=True)
            expos = jnp.exp(scores - row_max)
            total = jnp.sum(expos, axis=-1, keepdims=True)
            weights = (expos * (1.0 / total)).astype(bf16)
            att_ref[rows, lo : lo + HEAD_DIM] = dot(weights, value).astype(bf16)
            lse_ref[rows, h : h + 1] = row_max + jnp.log(total)
    for k, out in enumerate((p0, p1, p2, p3)):
        mine = att_ref[pl.ds(position(me, k), QUARTER), :]
        out[...] = dot(mine, w_ref[:, QKV:], 1, 1).astype(bf16)


def dispatch_kernel(
    x_ref, t00, t01, t02, t10, t11, t12, gain_ref, router_ref, route_ref, place_ref,
    hidden_ref, gate_ref, slots_ref,
):
    for s, terms in ((0, (t00, t01, t02)), (1, (t10, t11, t12))):
        rows = slice(s * QUARTER, (s + 1) * QUARTER)
        hidden_ref[rows] = x_ref[s] + added(*[t[...] for t in terms])
    hidden = hidden_ref[...]
    mixed = hidden * inverse_size(hidden) * gain_ref[...]
    low = mixed.astype(bf16)
    slots_ref[...] = dot(place_ref[...], low, 0, 0).astype(bf16)
    logits = dot(mixed, router_ref[...], precision=lax.Precision.HIGHEST)
    expos = jnp.exp(logits - jnp.max(logits, axis=-1, keepdims=True))
    shares = expos / jnp.sum(expos, axis=-1, keepdims=True)
    for s in range(2):
        rows = slice(s * QUARTER, (s + 1) * QUARTER)
        chosen = as_column(route_ref[s : s + 1].astype(f32)).astype(jnp.int32)[:, :EXPERTS]
        mask = chosen == lax.broadcasted_iota(jnp.int32, (QUARTER, EXPERTS), 1)
        gate = jnp.sum(jnp.where(mask, shares[rows], 0.0), axis=-1, keepdims=True)
        gate_ref[rows] = jnp.broadcast_to(gate, (QUARTER, 128))


WORK_ORDER = (2, 1, 3, 0)


def upstream_kernel(c0, c1, c2, c3, w_ref, u_ref):
    pieces = (c0, c1, c2, c3)
    for n, k in enumerate(WORK_ORDER):
        u_ref[n] = dot(pieces[k][...], w_ref[0], 1, 1).astype(bf16)


def expert_kernel(
    own_ref, x0, x1, x2, x3, u_ref, w_ref, router_ref, _, __,
    active_ref, scaled_ref, grad_ref, logit_ref, s0, s1, s2, s3, pre_ref,
):
    own = own_ref[0]
    router = router_ref[...]
    router_hi = router.astype(bf16)
    router_lo = (router - router_hi.astype(f32)).astype(bf16)
    router_both = jnp.concatenate([router_hi, router_lo], axis=1)
    c = math.sqrt(2.0 / math.pi)
    ca = c * 0.044715

    def work(xs, outs, first):
        x = jnp.concatenate([x_ref[...] for x_ref in xs])
        logits = dot(x, router_both)
        logits = logits[:, :EXPERTS] + logits[:, EXPERTS:]
        expos = jnp.exp(logits - jnp.max(logits, axis=-1, keepdims=True))
        shares = expos / jnp.sum(expos, axis=-1, keepdims=True)
        chosen = jnp.where(lax.broadcasted_iota(jnp.int32, shares.shape, 1) == own, 1.0, 0.0)
        gate = jnp.sum(shares * chosen, axis=-1, keepdims=True)
        pre_ref[...] = dot(x, w_ref[0])
        gate_grads = []
        for n in range(2):
            for part in range(HALF_SLOTS // 64):
                rows = slice(part * 64, part * 64 + 64)
                at = slice(n * HALF_SLOTS + part * 64, n * HALF_SLOTS + part * 64 + 64)
                pre = pre_ref[at, :]
                u = u_ref[n, rows, :].astype(f32)
                square = pre * pre
                t = jnp.tanh(pre * (c + ca * square))
                half = 0.5 + 0.5 * t
                active = pre * half
                slope = half + (0.5 * pre) * (1.0 - t * t) * (c + 3.0 * ca * square)
                gate_grads.append(jnp.sum(active * u, axis=-1, keepdims=True))
                active_ref[n, rows, :] = active.astype(bf16)
                scaled_ref[n, rows, :] = (gate[at] * active).astype(bf16)
                grad_ref[n, rows, :] = (gate[at] * u * slope).astype(bf16)
        logit_grad = shares * (chosen - gate) * jnp.concatenate(gate_grads)
        logit_hi = logit_grad.astype(bf16)
        logit_lo = (logit_grad - logit_hi.astype(f32)).astype(bf16)
        pre_grad = jnp.concatenate([grad_ref[0], grad_ref[1]])
        slot_grad = dot(pre_grad, w_ref[0], 1, 1) + dot(logit_hi, router_hi, 1, 1)
        for n, out in enumerate(outs):
            out[...] = slot_grad[n * HALF_SLOTS : (n + 1) * HALF_SLOTS].astype(bf16)
        term = dot(jnp.concatenate([logit_hi, logit_lo], axis=1), x, 0, 0)
        if first:
            logit_ref[...] = term
        else:
            logit_ref[...] += term

    pl.when(pl.program_id(0) == 0)(lambda: work((x2, x1), (s2, s1), True))
    pl.when(pl.program_id(0) == 1)(lambda: work((x3, x0), (s3, s0), False))


def output_kernel(active_ref, w_ref, _, __, s0, s1, s2, s3):
    outs = (s0, s1, s2, s3)
    for n, k in enumerate(WORK_ORDER):
        outs[k][...] = dot(active_ref[n], w_ref[0]).astype(bf16)


def weights_kernel(scaled_ref, grad_ref, c0, c1, c2, c3, x0, x1, x2, x3, *rest):
    out_ref, in_ref, token_ref = rest[-3:]
    token_ref[...] = jnp.zeros_like(token_ref)
    upstream, entered = (c0, c1, c2, c3), (x0, x1, x2, x3)
    for n, k in enumerate(WORK_ORDER):
        out_term = dot(scaled_ref[n], upstream[k][...], 0, 0)
        in_term = dot(entered[k][...], grad_ref[n], 0, 0)
        if n == 0:
            out_ref[0] = out_term
            in_ref[0] = in_term
        else:
            out_ref[0] += out_term
            in_ref[0] += in_term


def router_kernel(a_ref, b_ref, _, out_ref):
    both = a_ref[...] + b_ref[...]
    rows = jnp.transpose(both[:EXPERTS] + both[EXPERTS:])
    none = jnp.zeros((8, EXPERTS), f32)
    for n in range(32):
        top, low = rows[24 * n : 24 * n + 16], rows[24 * n + 16 : 24 * n + 24]
        beside = jnp.concatenate([low, none])
        out_ref[n] = jnp.concatenate([top, beside], axis=1).astype(bf16)


def back_kernel(
    slots_ref, place_ref, hidden_ref, cot_ref, gain_ref, _, __, grad_ref, h0, h1, gain_grad_ref
):
    mixed_grad = dot(place_ref[...], slots_ref[...])
    hidden = hidden_ref[...]
    r = inverse_size(hidden)
    gain_grad_ref[...] = jnp.sum(mixed_grad * hidden * r, axis=0, keepdims=True)
    u = gain_ref[...] * mixed_grad
    grad = cot_ref[...] + r * u - hidden * (r * r * r * jnp.mean(hidden * u, axis=-1, keepdims=True))
    grad_ref[...] = grad
    h0[...] = grad[:QUARTER].astype(bf16)
    h1[...] = grad[QUARTER:].astype(bf16)


def result_kernel(slots_ref, place_ref, hidden_ref, gate_ref, out_ref):
    back = dot(place_ref[...], slots_ref[...])
    out_ref[...] = hidden_ref[...] + gate_ref[:, :1] * back


def attend_back_kernel(
    me_ref, a0, a1, a2, a3, w_ref, tiles_ref, g_ref, qkv_ref, lse_ref, _, __, ___,
    up_ref, dqkv_ref, sums_ref, gain_ref, p0, p1, p2, p3, tile_sums,
):
    me = me_ref[0]
    for k, piece in enumerate((a0, a1, a2, a3)):
        up_ref[pl.ds(position(me, k), QUARTER), :] = piece[...]
    att_grad = dot(up_ref[...], w_ref[:, QKV:]).astype(bf16)
    column, row = same_document(g_ref)
    tile_sums[...] = jnp.zeros_like(tile_sums)
    for h in range(LOCAL_HEADS):
        lo = h * HEAD_DIM
        key = qkv_ref[:, CHANNELS + lo : CHANNELS + lo + HEAD_DIM]
        value = qkv_ref[:, 2 * CHANNELS + lo : 2 * CHANNELS + lo + HEAD_DIM]
        key_grad = jnp.zeros((HEAD_DIM, PARTS * QUARTER), f32)
        value_grad = jnp.zeros((HEAD_DIM, PARTS * QUARTER), f32)
        for i in range(PARTS * QUARTER // BLOCK):
            rows = slice(i * BLOCK, (i + 1) * BLOCK)
            query = qkv_ref[rows, lo : lo + HEAD_DIM] * HEAD_DIM ** (-0.5)
            scores = dot(query, key, 1, 1) + bias_rows(tiles_ref, h, i)
            scores = jnp.where(column[rows, :1] == row, scores, -1000000000.0)
            weights = jnp.exp(scores - lse_ref[rows, h : h + 1])
            out_grad = att_grad[rows, lo : lo + HEAD_DIM]
            weights_grad = dot(out_grad, value, 1, 1)
            inner = jnp.sum(weights * weights_grad, axis=-1, keepdims=True)
            score_grad = (weights * (weights_grad - inner)).astype(bf16)
            wide = score_grad.astype(f32)
            for r in range(BLOCK // QUARTER):
                for j in range(PARTS):
                    tile_sums[h, tile_at(i * (BLOCK // QUARTER) + r, j)] += wide[
                        r * QUARTER : (r + 1) * QUARTER, j * QUARTER : (j + 1) * QUARTER
                    ]
            dqkv_ref[rows, lo : lo + HEAD_DIM] = (
                dot(score_grad, key) * HEAD_DIM ** (-0.5)
            ).astype(bf16)
            key_grad += dot(query, score_grad, 0, 0)
            value_grad += dot(out_grad, weights.astype(bf16), 0, 0)
        dqkv_ref[:, CHANNELS + lo : CHANNELS + lo + HEAD_DIM] = jnp.transpose(key_grad).astype(bf16)
        dqkv_ref[:, 2 * CHANNELS + lo : 2 * CHANNELS + lo + HEAD_DIM] = jnp.transpose(
            value_grad
        ).astype(bf16)
    gain = jnp.zeros((1, WIDTH), f32)
    for k, out in ((2, p2), (1, p1), (3, p3), (0, p0)):
        at = pl.ds(position(me, k), QUARTER)
        normed_grad = dot(dqkv_ref[at, :], w_ref[:, :QKV], 1, 1)
        out[...] = normed_grad.astype(bf16)
        gain += jnp.sum(normed_grad * g_ref[at, :WIDTH].astype(f32), axis=0, keepdims=True)
    gain_ref[...] = gain
    sums_ref[...] = jnp.zeros_like(sums_ref)
    for t, step in enumerate(TILE_STEPS):
        buckets = tile_buckets(step)
        for b in possible(step):
            mask = buckets == b
            for h in range(LOCAL_HEADS):
                sums_ref[h, b : b + 1] += jnp.sum(
                    jnp.where(mask, tile_sums[h, t], 0.0), axis=0, keepdims=True
                )


def projection_kernel(g0, g1, d0, d1, u0, u1, a0, a1, out_ref):
    out_ref[:, :QKV] = (
        dot(g0[:, :WIDTH], d0[...], 0, 0) + dot(g1[:, :WIDTH], d1[...], 0, 0)
    ).astype(bf16)
    out_ref[:, QKV:] = (dot(u0[...], a0[...], 0, 0) + dot(u1[...], a1[...], 0, 0)).astype(bf16)


def input_kernel(x_ref, gain_ref, grad_ref, t00, t01, t02, t10, t11, t12, out_ref):
    for s, terms in ((0, (t00, t01, t02)), (1, (t10, t11, t12))):
        x = x_ref[s]
        r = inverse_size(x)
        u = gain_ref[...] * added(*[t[...] for t in terms])
        out_ref[s] = (
            grad_ref[s * QUARTER : (s + 1) * QUARTER]
            + r * u
            - x * (r * r * r * jnp.mean(x * u, axis=-1, keepdims=True))
        )


def expert_spec(e):
    return pl.BlockSpec((1, WIDTH, WIDTH), lambda i: (e, 0, 0))


def body(
    inputs,
    projection_in,
    projection_out,
    gain_attention,
    gain_experts,
    router_weight,
    bias_table,
    expert_in,
    expert_out,
    routes,
    segments,
    cotangent,
):
    seq_here, quarter, width = inputs.shape
    rows = seq_here * quarter
    me = lax.axis_index("mp").reshape(1).astype(jnp.int32)
    first_head = me * LOCAL_HEADS
    gain1, gain2 = gain_attention.reshape(1, width), gain_experts.reshape(1, width)
    routes = routes.reshape(seq_here, quarter)
    upstream = cotangent.reshape(rows, width)
    piece = struct((QUARTER, WIDTH), bf16)
    slot_piece = struct((HALF_SLOTS, WIDTH), bf16)

    turned = jnp.concatenate(
        [jnp.moveaxis(projection_in, 1, 0).reshape(24, QKV), projection_out.T], axis=1
    )
    place, lines = call(
        place_kernel,
        (struct((rows, SLOTS), bf16), struct((32, 40, width), bf16)),
        (routes, upstream, turned),
        name="place",
    )
    lines = lax.all_to_all(lines, EXPERT, 0, 0, tiled=True)
    weights = lines[:, :24].reshape(WIDTH, QKV + CHANNELS)
    c_slots = by_expert(lines[:, 24:])

    tagged = struct((QUARTER, TAGGED), bf16)
    n0, n1 = call(start_kernel, (tagged, tagged), (inputs, gain1, segments), name="start")
    normed = (gather4(n0, 1), gather4(n1, -1))
    tiles = call(
        bias_kernel,
        struct((LOCAL_HEADS, len(TILE_STEPS), QUARTER, QUARTER), f32),
        (first_head, bias_table),
        [SMEM, SMEM],
        name="bias",
    )
    length = PARTS * QUARTER
    attended = [
        call(
            attend_kernel,
            (
                struct((length, TAGGED), bf16),
                struct((length, QKV), bf16),
                struct((length, CHANNELS), bf16),
                struct((length, 128), f32),
                piece, piece, piece, piece,
            ),
            (me, *normed[s], weights, tiles),
            [SMEM] + [VMEM] * 6,
            flops=2 * 10**9,
            name="attend",
        )
        for s in range(2)
    ]
    attention = [reduce4(attended[s][4:], (1, -1)[s])[0] for s in range(2)]

    c_all = [gather4(c, (1, -1)[e]) for e, c in enumerate(c_slots)]
    u = [
        call(
            upstream_kernel,
            struct((PARTS, HALF_SLOTS, WIDTH), bf16),
            (*c_all[e], expert_out),
            [VMEM] * 4 + [expert_spec(e)],
            flops=12 * 10**8,
            name="upstream",
        )
        for e in range(2)
    ]

    hidden, gate, slots = call(
        dispatch_kernel,
        (struct((rows, width), f32), struct((rows, 128), f32), struct((SLOTS, width), bf16)),
        (inputs, *attention[0], *attention[1], gain2, router_weight, routes, place),
        name="dispatch",
    )
    x_all = [gather4(x, (1, -1)[e]) for e, x in enumerate(by_expert(to_experts(slots)))]
    group = lax.axis_index(EXPERT).astype(jnp.int32)
    acts = struct((PARTS, HALF_SLOTS, WIDTH), bf16)
    pair = pl.BlockSpec((2, HALF_SLOTS, WIDTH), lambda i: (i, 0, 0))
    worked = []
    for e in range(2):
        earlier = (worked[0][4], u[0]) if e else (x_all[1][2], u[1])
        outs = pl.pallas_call(
            expert_kernel,
            grid=(2,),
            out_shape=(acts, acts, acts, struct((2 * EXPERTS, WIDTH), f32)) + (slot_piece,) * 4,
            in_specs=[SMEM] + [VMEM] * 4 + [pair, expert_spec(e), VMEM, ANY, ANY],
            out_specs=(pair, pair, pair) + (VMEM,) * 5,
            scratch_shapes=[pltpu.VMEM((SLOTS, WIDTH), f32)],
            cost_estimate=pl.CostEstimate(
                flops=24 * 10**8, bytes_accessed=2 * 10**7, transcendentals=0
            ),
            compiler_params=pltpu.CompilerParams(vmem_limit_bytes=VMEM_LIMIT),
            name="expert",
        )((group * 2 + e).reshape(1), *x_all[e], u[e], expert_in, router_weight, *earlier)
        worked.append(outs)
    slot_terms, middles = zip(reduce4(worked[0][4:], 1), reduce4(worked[1][4:], -1))
    returned = to_experts(summed_slots(slot_terms))
    outputs = [
        call(
            output_kernel,
            (slot_piece,) * 4,
            (worked[e][0], expert_out, *middles),
            [VMEM, expert_spec(e), ANY, ANY],
            flops=12 * 10**8,
            name="expert_output",
        )
        for e in range(2)
    ]
    whole = struct((2, WIDTH, WIDTH), f32)
    expert_grads, tokens = (), []
    for e in range(2):
        ins = (worked[e][1], worked[e][2], *c_all[e], *x_all[e])
        *expert_grads, token = pl.pallas_call(
            weights_kernel,
            grid=(1,),
            out_shape=(whole, whole, struct((8, 128), f32)),
            in_specs=[VMEM] * 10 + [pl.BlockSpec(memory_space=pl.ANY)] * len(expert_grads),
            out_specs=(expert_spec(e), expert_spec(e), VMEM),
            input_output_aliases={10: 0, 11: 1} if expert_grads else {},
            cost_estimate=pl.CostEstimate(
                flops=24 * 10**8, bytes_accessed=2 * 10**7, transcendentals=0
            ),
            compiler_params=pltpu.CompilerParams(vmem_limit_bytes=VMEM_LIMIT),
            name="expert_weights",
        )(*ins, *expert_grads)
        tokens.append(token)
    grad_expert_out, grad_expert_in = expert_grads

    output_slots = summed_slots([reduce4(outputs[e], (1, -1)[e])[0] for e in range(2)])
    router = call(
        router_kernel,
        struct((32, 16, 128), bf16),
        (worked[0][3], worked[1][3], middles[0]),
        [VMEM, VMEM, ANY],
        name="router_gradient",
    )
    hidden_grad, h0, h1, gain2_grad = call(
        back_kernel,
        (struct((rows, width), f32), piece, piece, struct((1, width), f32)),
        (returned.reshape(SLOTS, width), place, hidden, upstream, gain2, tokens[0], router),
        [VMEM] * 5 + [ANY] * 2,
        name="back",
    )
    grads = (gather4(h0, 1), gather4(h1, -1))
    attended_back = [
        call(
            attend_back_kernel,
            (
                struct((length, width), bf16),
                struct((length, QKV), bf16),
                struct((LOCAL_HEADS, BUCKETS, 128), f32),
                struct((1, width), f32),
                piece, piece, piece, piece,
            ),
            (me, *grads[s], weights, tiles, *attended[s][:2], attended[s][3], *grads[1 - s][1:]),
            [SMEM] + [VMEM] * 9 + [ANY] * 3,
            scratch=[pltpu.VMEM((LOCAL_HEADS, len(TILE_STEPS), QUARTER, QUARTER), f32)],
            flops=4 * 10**9,
            name="attend_back",
        )
        for s in range(2)
    ]
    normed_grad = [reduce4(attended_back[s][4:], (1, -1)[s])[0] for s in range(2)]
    input_grad = call(
        input_kernel,
        struct(inputs.shape, f32),
        (inputs, gain1, hidden_grad, *normed_grad[0], *normed_grad[1]),
        name="input_gradient",
    )

    output_slots = jnp.concatenate([output_slots, router], axis=2)
    output_back = to_experts(output_slots)
    router_rows = jnp.sum(output_back[:, :, width:].astype(f32), axis=0)
    router_rows = jnp.concatenate([router_rows[:, :EXPERTS], router_rows[:8, EXPERTS:]])
    result = call(
        result_kernel,
        struct((rows, width), f32),
        (output_back[:, :, :width].reshape(SLOTS, width), place, hidden, gate),
        name="result",
    )
    partial = call(
        projection_kernel,
        struct((WIDTH, QKV + CHANNELS), bf16),
        (
            attended[0][0], attended[1][0], attended_back[0][1], attended_back[1][1],
            attended_back[0][0], attended_back[1][0], attended[0][2], attended[1][2],
        ),
        flops=16 * 10**8,
        name="projection_gradient",
    )
    table_local = jnp.sum(attended_back[0][2] + attended_back[1][2], axis=-1).T
    table = lax.dynamic_update_slice(
        jnp.zeros((BUCKETS, HEADS), f32), table_local, (0, first_head[0])
    )
    gain1_grad = (attended_back[0][3] + attended_back[1][3]) / gain1
    small = jnp.concatenate(
        [t.reshape(-1) for t in (router_rows, gain1_grad, gain2_grad, table)]
    ).reshape(27, 128)
    small = added(small, shift(small, 1), shift(small, -1), shift(small, 2)).reshape(-1)
    lines = jnp.pad(small.astype(bf16), (0, 5 * width - small.size)).reshape(1, 5, width)
    lines = jnp.concatenate(
        [partial.reshape(32, 24, width), jnp.broadcast_to(lines, (32, 5, width))], axis=1
    )
    arrived = lax.all_to_all(lines, EXPERT, 0, 0, tiled=True)
    projections = jnp.sum(arrived[:, :24].astype(f32), axis=0)
    grad_projection_in = jnp.moveaxis(projections[:, :QKV].reshape(24, 3, CHANNELS), 1, 0)
    grad_projection_out = projections[:, QKV:].T
    grad_router = arrived[:, 24:26].astype(f32).reshape(WIDTH, EXPERTS)
    late = jnp.sum(arrived[:, 26:].astype(f32), axis=0).reshape(-1)
    grad_gain_attention = late[:width]
    grad_gain_experts = late[width : 2 * width]
    grad_table = late[2 * width : 2 * width + BUCKETS * HEADS].reshape(BUCKETS, HEADS)
    return (
        result.reshape(seq_here, quarter, width),
        input_grad,
        grad_projection_in,
        grad_projection_out,
        grad_gain_attention,
        grad_gain_experts,
        grad_router,
        grad_table,
        grad_expert_in,
        grad_expert_out,
    )


def solution(mesh):
    split = Mesh(
        mesh.devices.reshape(4, 4, 2, mesh.shape["mp"]), ("expert_0", "expert_1", "expert_2", "mp")
    )
    in_specs = (
        P(EXPERT, "mp", None),
        P(None, EXPERT, "mp"),
        P("mp", EXPERT),
        P(),
        P(),
        P(),
        P(),
        P(EXPERT, None, "mp"),
        P(EXPERT, "mp", None),
        P(EXPERT, "mp", None),
        P(EXPERT, "mp"),
        P(EXPERT, "mp", None),
    )
    out_specs = (
        P(EXPERT, "mp", None),
        P(EXPERT, "mp", None),
        P(None, EXPERT, "mp"),
        P("mp", EXPERT),
        P(),
        P(),
        P(),
        P(),
        P(EXPERT, None, "mp"),
        P(EXPERT, "mp", None),
    )
    return jax.shard_map(body, mesh=split, in_specs=in_specs, out_specs=out_specs, check_vma=False)
```

```python
import functools
import math

import jax
import jax.numpy as jnp
from jax import lax
from jax.experimental import pallas as pl
from jax.experimental.pallas import tpu as pltpu
from jax.sharding import Mesh
from jax.sharding import PartitionSpec as P

HEADS = 12
HEAD_DIM = 64
EXPERTS = 64
BUCKETS = 32
REACH = 128
EXPERT = ("expert_0", "expert_1", "expert_2")
QUARTER = 128
PARTS = 4
WIDTH = 768
CHANNELS = 192
LOCAL_HEADS = CHANNELS // HEAD_DIM
QKV = 3 * CHANNELS
CAPACITY = 4
SLOTS = 512
HALF_SLOTS = SLOTS // 2
TAGGED = WIDTH + 128
TILE_STEPS = (0, 1, -1, 2, -2)

epsilon = 1e-06
f32 = jnp.float32
bf16 = jnp.bfloat16
BLOCK = 512
VMEM_LIMIT = 56 * 1024 * 1024


def dot(a, b, ca=1, cb=0, precision=None):
    return lax.dot_general(
        a, b, (((ca,), (cb,)), ((), ())), preferred_element_type=f32, precision=precision
    )


def struct(shape, dtype):
    return jax.ShapeDtypeStruct(shape, dtype)


ANY = pl.BlockSpec(memory_space=pl.ANY)
SMEM = pl.BlockSpec(memory_space=pltpu.SMEM)
VMEM = pl.BlockSpec(memory_space=pltpu.VMEM)


def call(kernel, outs, ins, in_specs=None, scratch=(), flops=10**8, moved=4 * 10**6, name=None):
    return pl.pallas_call(
        kernel,
        grid=(1,),
        out_shape=outs,
        in_specs=in_specs or [VMEM] * len(ins),
        out_specs=jax.tree.map(lambda _: VMEM, outs),
        scratch_shapes=scratch,
        cost_estimate=pl.CostEstimate(flops=flops, bytes_accessed=moved, transcendentals=0),
        compiler_params=pltpu.CompilerParams(vmem_limit_bytes=VMEM_LIMIT),
        name=name,
    )(*ins)


def shift(x, step):
    return lax.ppermute(x, "mp", [(i, (i + step) % PARTS) for i in range(PARTS)])


def gather4(x, way):
    left, right = shift(x, 1), shift(x, -1)
    far = shift(left, 1) if way > 0 else shift(right, -1)
    return x, right, far, left


def added(*terms):
    return functools.reduce(lambda a, b: a + b, [t.astype(f32) for t in terms])


def reduce4(pieces, way):
    own, right, far, left = pieces
    if way > 0:
        middle = right = added(right, shift(far, 1)).astype(bf16)
    else:
        middle = left = added(left, shift(far, -1)).astype(bf16)
    return (own, shift(right, 1), shift(left, -1)), middle


def to_experts(x):
    return lax.all_to_all(x.reshape(32, -1, x.shape[-1]), EXPERT, 0, 0, tiled=True)


def by_expert(slots):
    return tuple(slots[:, 8 * e : 8 * e + 8, :WIDTH].reshape(HALF_SLOTS, WIDTH) for e in range(2))


def summed_slots(terms):
    pieces = [added(*terms[e]).astype(bf16).reshape(32, 8, WIDTH) for e in range(2)]
    return jnp.concatenate(pieces, axis=1)


def sent_to_all(x, axis):
    peers = lax.axis_size(axis)
    return lax.all_to_all(jnp.broadcast_to(x[None], (peers, *x.shape)), axis, 0, 0, tiled=True)


def bucket_of(offsets):
    halfway = BUCKETS // 2
    exact_span = halfway // 2
    distance = jnp.abs(offsets)
    far_part = jnp.full_like(distance, exact_span)
    for step in range(1, exact_span):
        cutoff_level = math.ceil(exact_span * (REACH / exact_span) ** (step / exact_span) - 1e-09)
        far_part = far_part + jnp.where(distance >= cutoff_level, 1, 0)
    nearby = jnp.where(distance < exact_span, distance, far_part)
    return nearby + jnp.where(offsets > 0, halfway, 0)


def tile_buckets(step):
    shape = (QUARTER, QUARTER)
    offsets = (
        step * QUARTER
        + lax.broadcasted_iota(jnp.int32, shape, 1)
        - lax.broadcasted_iota(jnp.int32, shape, 0)
    )
    return bucket_of(offsets)


def possible(step):
    if step == 0:
        return range(BUCKETS)
    if step == 1:
        return range(BUCKETS // 2 + 1, BUCKETS)
    if step == -1:
        return range(1, BUCKETS // 2)
    return (BUCKETS - 1,) if step > 0 else (BUCKETS // 2 - 1,)


def tile_at(row_block, key_block):
    step = key_block - row_block
    return TILE_STEPS.index(max(-2, min(2, step)))


def bias_kernel(head_ref, table_ref, out_ref):
    head = head_ref[0]
    for t, step in enumerate(TILE_STEPS):
        buckets = tile_buckets(step)
        tiles = [jnp.zeros((QUARTER, QUARTER), f32)] * LOCAL_HEADS
        for b in possible(step):
            mask = buckets == b
            tiles = [jnp.where(mask, table_ref[b, head + h], tile) for h, tile in enumerate(tiles)]
        for h, tile in enumerate(tiles):
            out_ref[h, t] = tile


def inverse_size(values):
    return lax.rsqrt(jnp.mean(values * values, axis=-1, keepdims=True) + epsilon)


def as_column(row):
    return jnp.transpose(jnp.broadcast_to(row, (QUARTER, QUARTER)))


def start_kernel(x_ref, gain_ref, seg_ref, n0, n1):
    gain = gain_ref[...]
    for s, out in ((0, n0), (1, n1)):
        x = x_ref[s]
        out[:, :WIDTH] = (x * inverse_size(x) * gain).astype(bf16)
        out[:, WIDTH:] = as_column(seg_ref[s : s + 1].astype(f32)).astype(bf16)


def place_kernel(route_ref, cot_ref, weights_ref, place_ref, lines_ref):
    tri = (
        lax.broadcasted_iota(jnp.int32, (QUARTER, QUARTER), 0)
        >= lax.broadcasted_iota(jnp.int32, (QUARTER, QUARTER), 1)
    ).astype(bf16)
    for s in range(2):
        chosen = as_column(route_ref[s : s + 1].astype(f32)).astype(jnp.int32)
        mask = jnp.where(
            chosen == lax.broadcasted_iota(jnp.int32, (QUARTER, QUARTER), 1), 1.0, 0.0
        )
        running = dot(tri, mask.astype(bf16))
        rank = jnp.sum(mask * running, axis=-1, keepdims=True).astype(jnp.int32) - 1
        place = chosen[:, :1] * 8 + s * CAPACITY + rank
        slots = lax.broadcasted_iota(jnp.int32, (QUARTER, SLOTS), 1)
        place_ref[s * QUARTER : (s + 1) * QUARTER] = jnp.where(slots == place, 1.0, 0.0).astype(bf16)
    slots = dot(place_ref[...], cot_ref[...].astype(bf16), 0, 0)
    weights = weights_ref[...].astype(f32)
    for n in range(32):
        lines_ref[n] = jnp.concatenate([weights, slots[16 * n : 16 * n + 16]]).astype(bf16)


def position(me, k):
    return pl.multiple_of(lax.rem(me + k, PARTS) * QUARTER, QUARTER)


def same_document(g_ref):
    column = g_ref[:, WIDTH:].astype(f32)
    return column, jnp.transpose(column)[:1]


def bias_rows(tiles_ref, h, i):
    per = BLOCK // QUARTER
    return jnp.concatenate(
        [
            jnp.concatenate([tiles_ref[h, tile_at(r, j)] for j in range(PARTS)], axis=1)
            for r in range(i * per, (i + 1) * per)
        ],
        axis=0,
    )


def attend_kernel(
    me_ref, a0, a1, a2, a3, w_ref, tiles_ref, g_ref, qkv_ref, att_ref, lse_ref, p0, p1, p2, p3
):
    me = me_ref[0]
    for k, piece in enumerate((a0, a1, a2, a3)):
        g_ref[pl.ds(position(me, k), QUARTER), :] = piece[...]
    qkv_ref[...] = dot(g_ref[:, :WIDTH], w_ref[:, :QKV]).astype(bf16)
    column, row = same_document(g_ref)
    lse_ref[...] = jnp.zeros_like(lse_ref)
    for h in range(LOCAL_HEADS):
        lo = h * HEAD_DIM
        key = qkv_ref[:, CHANNELS + lo : CHANNELS + lo + HEAD_DIM]
        value = qkv_ref[:, 2 * CHANNELS + lo : 2 * CHANNELS + lo + HEAD_DIM]
        for i in range(PARTS * QUARTER // BLOCK):
            rows = slice(i * BLOCK, (i + 1) * BLOCK)
            query = qkv_ref[rows, lo : lo + HEAD_DIM] * HEAD_DIM ** (-0.5)
            scores = dot(query, key, 1, 1) + bias_rows(tiles_ref, h, i)
            scores = jnp.where(column[rows, :1] == row, scores, -1000000000.0)
            row_max = jnp.max(scores, axis=-1, keepdims=True)
            expos = jnp.exp(scores - row_max)
            total = jnp.sum(expos, axis=-1, keepdims=True)
            weights = (expos * (1.0 / total)).astype(bf16)
            att_ref[rows, lo : lo + HEAD_DIM] = dot(weights, value).astype(bf16)
            lse_ref[rows, h : h + 1] = row_max + jnp.log(total)
    for k, out in enumerate((p0, p1, p2, p3)):
        mine = att_ref[pl.ds(position(me, k), QUARTER), :]
        out[...] = dot(mine, w_ref[:, QKV:], 1, 1).astype(bf16)


def dispatch_kernel(
    x_ref, t00, t01, t02, t10, t11, t12, gain_ref, router_ref, route_ref, place_ref,
    hidden_ref, gate_ref, slots_ref,
):
    for s, terms in ((0, (t00, t01, t02)), (1, (t10, t11, t12))):
        rows = slice(s * QUARTER, (s + 1) * QUARTER)
        hidden_ref[rows] = x_ref[s] + added(*[t[...] for t in terms])
    hidden = hidden_ref[...]
    mixed = hidden * inverse_size(hidden) * gain_ref[...]
    low = mixed.astype(bf16)
    slots_ref[...] = dot(place_ref[...], low, 0, 0).astype(bf16)
    logits = dot(mixed, router_ref[...], precision=lax.Precision.HIGHEST)
    expos = jnp.exp(logits - jnp.max(logits, axis=-1, keepdims=True))
    shares = expos / jnp.sum(expos, axis=-1, keepdims=True)
    for s in range(2):
        rows = slice(s * QUARTER, (s + 1) * QUARTER)
        chosen = as_column(route_ref[s : s + 1].astype(f32)).astype(jnp.int32)[:, :EXPERTS]
        mask = chosen == lax.broadcasted_iota(jnp.int32, (QUARTER, EXPERTS), 1)
        gate = jnp.sum(jnp.where(mask, shares[rows], 0.0), axis=-1, keepdims=True)
        gate_ref[rows] = jnp.broadcast_to(gate, (QUARTER, 128))


WORK_ORDER = (2, 1, 3, 0)


def upstream_kernel(c0, c1, c2, c3, w_ref, u_ref):
    pieces = (c0, c1, c2, c3)
    for n, k in enumerate(WORK_ORDER):
        u_ref[n] = dot(pieces[k][...], w_ref[0], 1, 1).astype(bf16)


def expert_kernel(
    own_ref, x0, x1, x2, x3, u_ref, w_ref, router_ref, _, __,
    active_ref, scaled_ref, grad_ref, logit_ref, s0, s1, s2, s3, pre_ref,
):
    own = own_ref[0]
    router = router_ref[...]
    router_hi = router.astype(bf16)
    router_lo = (router - router_hi.astype(f32)).astype(bf16)
    router_both = jnp.concatenate([router_hi, router_lo], axis=1)
    c = math.sqrt(2.0 / math.pi)
    ca = c * 0.044715

    def work(xs, outs, first):
        x = jnp.concatenate([x_ref[...] for x_ref in xs])
        logits = dot(x, router_both)
        logits = logits[:, :EXPERTS] + logits[:, EXPERTS:]
        expos = jnp.exp(logits - jnp.max(logits, axis=-1, keepdims=True))
        shares = expos / jnp.sum(expos, axis=-1, keepdims=True)
        chosen = jnp.where(lax.broadcasted_iota(jnp.int32, shares.shape, 1) == own, 1.0, 0.0)
        gate = jnp.sum(shares * chosen, axis=-1, keepdims=True)
        pre_ref[...] = dot(x, w_ref[0])
        gate_grads = []
        for n in range(2):
            for part in range(HALF_SLOTS // 64):
                rows = slice(part * 64, part * 64 + 64)
                at = slice(n * HALF_SLOTS + part * 64, n * HALF_SLOTS + part * 64 + 64)
                pre = pre_ref[at, :]
                u = u_ref[n, rows, :].astype(f32)
                square = pre * pre
                t = jnp.tanh(pre * (c + ca * square))
                half = 0.5 + 0.5 * t
                active = pre * half
                slope = half + (0.5 * pre) * (1.0 - t * t) * (c + 3.0 * ca * square)
                gate_grads.append(jnp.sum(active * u, axis=-1, keepdims=True))
                active_ref[n, rows, :] = active.astype(bf16)
                scaled_ref[n, rows, :] = (gate[at] * active).astype(bf16)
                grad_ref[n, rows, :] = (gate[at] * u * slope).astype(bf16)
        logit_grad = shares * (chosen - gate) * jnp.concatenate(gate_grads)
        logit_hi = logit_grad.astype(bf16)
        logit_lo = (logit_grad - logit_hi.astype(f32)).astype(bf16)
        pre_grad = jnp.concatenate([grad_ref[0], grad_ref[1]])
        slot_grad = dot(pre_grad, w_ref[0], 1, 1) + dot(logit_hi, router_hi, 1, 1)
        for n, out in enumerate(outs):
            out[...] = slot_grad[n * HALF_SLOTS : (n + 1) * HALF_SLOTS].astype(bf16)
        term = dot(jnp.concatenate([logit_hi, logit_lo], axis=1), x, 0, 0)
        if first:
            logit_ref[...] = term
        else:
            logit_ref[...] += term

    pl.when(pl.program_id(0) == 0)(lambda: work((x2, x1), (s2, s1), True))
    pl.when(pl.program_id(0) == 1)(lambda: work((x3, x0), (s3, s0), False))


def output_kernel(active_ref, w_ref, _, __, ___, s0, s1, s2, s3):
    outs = (s0, s1, s2, s3)
    for n, k in enumerate(WORK_ORDER):
        outs[k][...] = dot(active_ref[n], w_ref[0]).astype(bf16)


def weights_kernel(scaled_ref, grad_ref, c0, c1, c2, c3, x0, x1, x2, x3, *rest):
    out_ref, in_ref, token_ref = rest[-3:]
    token_ref[...] = jnp.zeros_like(token_ref)
    upstream = jnp.concatenate([(c0, c1, c2, c3)[k][...] for k in WORK_ORDER])
    entered = jnp.concatenate([(x0, x1, x2, x3)[k][...] for k in WORK_ORDER])
    rows = (PARTS * HALF_SLOTS, WIDTH)
    out_ref[0] = dot(scaled_ref[...].reshape(rows), upstream, 0, 0)
    in_ref[0] = dot(entered, grad_ref[...].reshape(rows), 0, 0)


def router_kernel(a_ref, b_ref, _, out_ref):
    both = a_ref[...] + b_ref[...]
    rows = jnp.transpose(both[:EXPERTS] + both[EXPERTS:])
    none = jnp.zeros((8, EXPERTS), f32)
    for n in range(32):
        top, low = rows[24 * n : 24 * n + 16], rows[24 * n + 16 : 24 * n + 24]
        beside = jnp.concatenate([low, none])
        out_ref[n] = jnp.concatenate([top, beside], axis=1).astype(bf16)


def back_kernel(
    slots_ref, place_ref, hidden_ref, cot_ref, gain_ref, _, grad_ref, h0, h1, gain_grad_ref
):
    mixed_grad = dot(place_ref[...], slots_ref[...])
    hidden = hidden_ref[...]
    r = inverse_size(hidden)
    gain_grad_ref[...] = jnp.sum(mixed_grad * hidden * r, axis=0, keepdims=True)
    u = gain_ref[...] * mixed_grad
    grad = cot_ref[...] + r * u - hidden * (r * r * r * jnp.mean(hidden * u, axis=-1, keepdims=True))
    grad_ref[...] = grad
    h0[...] = grad[:QUARTER].astype(bf16)
    h1[...] = grad[QUARTER:].astype(bf16)


def result_kernel(slots_ref, place_ref, hidden_ref, gate_ref, out_ref):
    slots = slots_ref[...].reshape(SLOTS, WIDTH)
    back = dot(place_ref[...], slots)
    out_ref[...] = hidden_ref[...] + gate_ref[:, :1] * back


def attend_back_kernel(
    me_ref, a0, a1, a2, a3, w_ref, tiles_ref, g_ref, qkv_ref, lse_ref, _, __, ___,
    up_ref, dqkv_ref, sums_ref, gain_ref, p0, p1, p2, p3, tile_sums,
):
    me = me_ref[0]
    for k, piece in enumerate((a0, a1, a2, a3)):
        up_ref[pl.ds(position(me, k), QUARTER), :] = piece[...]
    att_grad = dot(up_ref[...], w_ref[:, QKV:]).astype(bf16)
    column, row = same_document(g_ref)
    tile_sums[...] = jnp.zeros_like(tile_sums)
    for h in range(LOCAL_HEADS):
        lo = h * HEAD_DIM
        key = qkv_ref[:, CHANNELS + lo : CHANNELS + lo + HEAD_DIM]
        value = qkv_ref[:, 2 * CHANNELS + lo : 2 * CHANNELS + lo + HEAD_DIM]
        key_grad = jnp.zeros((HEAD_DIM, PARTS * QUARTER), f32)
        value_grad = jnp.zeros((HEAD_DIM, PARTS * QUARTER), f32)
        for i in range(PARTS * QUARTER // BLOCK):
            rows = slice(i * BLOCK, (i + 1) * BLOCK)
            query = qkv_ref[rows, lo : lo + HEAD_DIM] * HEAD_DIM ** (-0.5)
            scores = dot(query, key, 1, 1) + bias_rows(tiles_ref, h, i)
            scores = jnp.where(column[rows, :1] == row, scores, -1000000000.0)
            weights = jnp.exp(scores - lse_ref[rows, h : h + 1])
            out_grad = att_grad[rows, lo : lo + HEAD_DIM]
            weights_grad = dot(out_grad, value, 1, 1)
            inner = jnp.sum(weights * weights_grad, axis=-1, keepdims=True)
            score_grad = (weights * (weights_grad - inner)).astype(bf16)
            wide = score_grad.astype(f32)
            for r in range(BLOCK // QUARTER):
                for j in range(PARTS):
                    tile_sums[h, tile_at(i * (BLOCK // QUARTER) + r, j)] += wide[
                        r * QUARTER : (r + 1) * QUARTER, j * QUARTER : (j + 1) * QUARTER
                    ]
            dqkv_ref[rows, lo : lo + HEAD_DIM] = (
                dot(score_grad, key) * HEAD_DIM ** (-0.5)
            ).astype(bf16)
            key_grad += dot(query, score_grad, 0, 0)
            value_grad += dot(out_grad, weights.astype(bf16), 0, 0)
        dqkv_ref[:, CHANNELS + lo : CHANNELS + lo + HEAD_DIM] = jnp.transpose(key_grad).astype(bf16)
        dqkv_ref[:, 2 * CHANNELS + lo : 2 * CHANNELS + lo + HEAD_DIM] = jnp.transpose(
            value_grad
        ).astype(bf16)
    gain = jnp.zeros((1, WIDTH), f32)
    for k, out in ((2, p2), (1, p1), (3, p3), (0, p0)):
        at = pl.ds(position(me, k), QUARTER)
        normed_grad = dot(dqkv_ref[at, :], w_ref[:, :QKV], 1, 1)
        out[...] = normed_grad.astype(bf16)
        gain += jnp.sum(normed_grad * g_ref[at, :WIDTH].astype(f32), axis=0, keepdims=True)
    gain_ref[...] = gain
    sums_ref[...] = jnp.zeros_like(sums_ref)
    for t, step in enumerate(TILE_STEPS):
        buckets = tile_buckets(step)
        for b in possible(step):
            mask = buckets == b
            for h in range(LOCAL_HEADS):
                sums_ref[h, b : b + 1] += jnp.sum(
                    jnp.where(mask, tile_sums[h, t], 0.0), axis=0, keepdims=True
                )


def projection_kernel(g0, g1, d0, d1, u0, u1, a0, a1, out_ref):
    out_ref[:, :QKV] = (
        dot(g0[:, :WIDTH], d0[...], 0, 0) + dot(g1[:, :WIDTH], d1[...], 0, 0)
    ).astype(bf16)
    out_ref[:, QKV:] = (dot(u0[...], a0[...], 0, 0) + dot(u1[...], a1[...], 0, 0)).astype(bf16)


def input_kernel(x_ref, gain_ref, grad_ref, t00, t01, t02, t10, t11, t12, out_ref):
    for s, terms in ((0, (t00, t01, t02)), (1, (t10, t11, t12))):
        x = x_ref[s]
        r = inverse_size(x)
        u = gain_ref[...] * added(*[t[...] for t in terms])
        out_ref[s] = (
            grad_ref[s * QUARTER : (s + 1) * QUARTER]
            + r * u
            - x * (r * r * r * jnp.mean(x * u, axis=-1, keepdims=True))
        )


def expert_spec(e):
    return pl.BlockSpec((1, WIDTH, WIDTH), lambda i: (e, 0, 0))


def body(
    inputs,
    projection_in,
    projection_out,
    gain_attention,
    gain_experts,
    router_weight,
    bias_table,
    expert_in,
    expert_out,
    routes,
    segments,
    cotangent,
):
    seq_here, quarter, width = inputs.shape
    rows = seq_here * quarter
    me = lax.axis_index("mp").reshape(1).astype(jnp.int32)
    first_head = me * LOCAL_HEADS
    gain1, gain2 = gain_attention.reshape(1, width), gain_experts.reshape(1, width)
    routes = routes.reshape(seq_here, quarter)
    upstream = cotangent.reshape(rows, width)
    piece = struct((QUARTER, WIDTH), bf16)
    slot_piece = struct((HALF_SLOTS, WIDTH), bf16)

    turned = jnp.concatenate(
        [jnp.moveaxis(projection_in, 1, 0).reshape(24, QKV), projection_out.T], axis=1
    )
    place, lines = call(
        place_kernel,
        (struct((rows, SLOTS), bf16), struct((32, 40, width), bf16)),
        (routes, upstream, turned),
        name="place",
    )
    lines = lax.all_to_all(lines, EXPERT, 0, 0, tiled=True)
    weights = lines[:, :24].reshape(WIDTH, QKV + CHANNELS)
    c_slots = by_expert(lines[:, 24:])

    tagged = struct((QUARTER, TAGGED), bf16)
    n0, n1 = call(start_kernel, (tagged, tagged), (inputs, gain1, segments), name="start")
    normed = (gather4(n0, 1), gather4(n1, -1))
    tiles = call(
        bias_kernel,
        struct((LOCAL_HEADS, len(TILE_STEPS), QUARTER, QUARTER), f32),
        (first_head, bias_table),
        [SMEM, SMEM],
        name="bias",
    )
    length = PARTS * QUARTER
    attended = [
        call(
            attend_kernel,
            (
                struct((length, TAGGED), bf16),
                struct((length, QKV), bf16),
                struct((length, CHANNELS), bf16),
                struct((length, 128), f32),
                piece, piece, piece, piece,
            ),
            (me, *normed[s], weights, tiles),
            [SMEM] + [VMEM] * 6,
            flops=2 * 10**9,
            name="attend",
        )
        for s in range(2)
    ]
    attention = [reduce4(attended[s][4:], (1, -1)[s])[0] for s in range(2)]

    c_all = [gather4(c, (1, -1)[e]) for e, c in enumerate(c_slots)]
    u = [
        call(
            upstream_kernel,
            struct((PARTS, HALF_SLOTS, WIDTH), bf16),
            (*c_all[e], expert_out),
            [VMEM] * 4 + [expert_spec(e)],
            flops=12 * 10**8,
            name="upstream",
        )
        for e in range(2)
    ]

    hidden, gate, slots = call(
        dispatch_kernel,
        (struct((rows, width), f32), struct((rows, 128), f32), struct((SLOTS, width), bf16)),
        (inputs, *attention[0], *attention[1], gain2, router_weight, routes, place),
        name="dispatch",
    )
    x_all = [gather4(x, (1, -1)[e]) for e, x in enumerate(by_expert(to_experts(slots)))]
    group = lax.axis_index(EXPERT).astype(jnp.int32)
    acts = struct((PARTS, HALF_SLOTS, WIDTH), bf16)
    pair = pl.BlockSpec((2, HALF_SLOTS, WIDTH), lambda i: (i, 0, 0))
    worked = []
    for e in range(2):
        earlier = (worked[0][4], u[0]) if e else (x_all[1][2], u[1])
        outs = pl.pallas_call(
            expert_kernel,
            grid=(2,),
            out_shape=(acts, acts, acts, struct((2 * EXPERTS, WIDTH), f32)) + (slot_piece,) * 4,
            in_specs=[SMEM] + [VMEM] * 4 + [pair, expert_spec(e), VMEM, ANY, ANY],
            out_specs=(pair, pair, pair) + (VMEM,) * 5,
            scratch_shapes=[pltpu.VMEM((SLOTS, WIDTH), f32)],
            cost_estimate=pl.CostEstimate(
                flops=24 * 10**8, bytes_accessed=2 * 10**7, transcendentals=0
            ),
            compiler_params=pltpu.CompilerParams(vmem_limit_bytes=VMEM_LIMIT),
            name="expert",
        )((group * 2 + e).reshape(1), *x_all[e], u[e], expert_in, router_weight, *earlier)
        worked.append(outs)
    slot_terms, middles = zip(reduce4(worked[0][4:], 1), reduce4(worked[1][4:], -1))
    returned = to_experts(summed_slots(slot_terms))
    whole = struct((2, WIDTH, WIDTH), f32)
    expert_grads, tokens = (), []
    for e in range(2):
        ins = (worked[e][1], worked[e][2], *c_all[e], *x_all[e])
        *expert_grads, token = pl.pallas_call(
            weights_kernel,
            grid=(1,),
            out_shape=(whole, whole, struct((8, 128), f32)),
            in_specs=[VMEM] * 10 + [pl.BlockSpec(memory_space=pl.ANY)] * len(expert_grads),
            out_specs=(expert_spec(e), expert_spec(e), VMEM),
            input_output_aliases={10: 0, 11: 1} if expert_grads else {},
            cost_estimate=pl.CostEstimate(
                flops=24 * 10**8, bytes_accessed=2 * 10**7, transcendentals=0
            ),
            compiler_params=pltpu.CompilerParams(vmem_limit_bytes=VMEM_LIMIT),
            name="expert_weights",
        )(*ins, *expert_grads)
        tokens.append(token)
    grad_expert_out, grad_expert_in = expert_grads

    outputs = [
        call(
            output_kernel,
            (slot_piece,) * 4,
            (worked[e][0], expert_out, *middles, tokens[0]),
            [VMEM, expert_spec(e), ANY, ANY, ANY],
            flops=12 * 10**8,
            name="expert_output",
        )
        for e in range(2)
    ]
    output_slots = summed_slots([reduce4(outputs[e], (1, -1)[e])[0] for e in range(2)])
    router = call(
        router_kernel,
        struct((32, 16, 128), bf16),
        (worked[0][3], worked[1][3], middles[0]),
        [VMEM, VMEM, ANY],
        name="router_gradient",
    )
    hidden_grad, h0, h1, gain2_grad = call(
        back_kernel,
        (struct((rows, width), f32), piece, piece, struct((1, width), f32)),
        (returned.reshape(SLOTS, width), place, hidden, upstream, gain2, tokens[1]),
        [VMEM] * 5 + [ANY],
        name="back",
    )
    grads = (gather4(h0, 1), gather4(h1, -1))
    attended_back = [
        call(
            attend_back_kernel,
            (
                struct((length, width), bf16),
                struct((length, QKV), bf16),
                struct((LOCAL_HEADS, BUCKETS, 128), f32),
                struct((1, width), f32),
                piece, piece, piece, piece,
            ),
            (me, *grads[s], weights, tiles, *attended[s][:2], attended[s][3], *grads[1 - s][1:]),
            [SMEM] + [VMEM] * 9 + [ANY] * 3,
            scratch=[pltpu.VMEM((LOCAL_HEADS, len(TILE_STEPS), QUARTER, QUARTER), f32)],
            flops=4 * 10**9,
            name="attend_back",
        )
        for s in range(2)
    ]
    normed_grad = [reduce4(attended_back[s][4:], (1, -1)[s])[0] for s in range(2)]
    input_grad = call(
        input_kernel,
        struct(inputs.shape, f32),
        (inputs, gain1, hidden_grad, *normed_grad[0], *normed_grad[1]),
        name="input_gradient",
    )

    output_slots = jnp.concatenate([output_slots, router], axis=2)
    output_back = to_experts(output_slots)
    router_rows = jnp.sum(output_back[:, :, width:].astype(f32), axis=0)
    router_rows = jnp.concatenate([router_rows[:, :EXPERTS], router_rows[:8, EXPERTS:]])
    result = call(
        result_kernel,
        struct((rows, width), f32),
        (output_back, place, hidden, gate),
        [pl.BlockSpec((32, 16, WIDTH), lambda i: (0, 0, 0)), VMEM, VMEM, VMEM],
        name="result",
    )
    partial = call(
        projection_kernel,
        struct((WIDTH, QKV + CHANNELS), bf16),
        (
            attended[0][0], attended[1][0], attended_back[0][1], attended_back[1][1],
            attended_back[0][0], attended_back[1][0], attended[0][2], attended[1][2],
        ),
        flops=16 * 10**8,
        name="projection_gradient",
    )
    table_local = jnp.sum(attended_back[0][2] + attended_back[1][2], axis=-1).T
    table = lax.dynamic_update_slice(
        jnp.zeros((BUCKETS, HEADS), f32), table_local, (0, first_head[0])
    )
    gain1_grad = (attended_back[0][3] + attended_back[1][3]) / gain1
    small = jnp.concatenate(
        [t.reshape(-1) for t in (router_rows, gain1_grad, gain2_grad, table)]
    ).reshape(27, 128)
    small = added(small, shift(small, 1), shift(small, -1), shift(small, 2)).reshape(-1)
    lines = jnp.pad(small.astype(bf16), (0, 5 * width - small.size)).reshape(1, 5, width)
    lines = jnp.concatenate(
        [partial.reshape(32, 24, width), jnp.broadcast_to(lines, (32, 5, width))], axis=1
    )
    arrived = lax.all_to_all(lines, EXPERT, 0, 0, tiled=True)
    projections = jnp.sum(arrived[:, :24].astype(f32), axis=0)
    grad_projection_in = jnp.moveaxis(projections[:, :QKV].reshape(24, 3, CHANNELS), 1, 0)
    grad_projection_out = projections[:, QKV:].T
    grad_router = arrived[:, 24:26].astype(f32).reshape(WIDTH, EXPERTS)
    late = jnp.sum(arrived[:, 26:].astype(f32), axis=0).reshape(-1)
    grad_gain_attention = late[:width]
    grad_gain_experts = late[width : 2 * width]
    grad_table = late[2 * width : 2 * width + BUCKETS * HEADS].reshape(BUCKETS, HEADS)
    return (
        result.reshape(seq_here, quarter, width),
        input_grad,
        grad_projection_in,
        grad_projection_out,
        grad_gain_attention,
        grad_gain_experts,
        grad_router,
        grad_table,
        grad_expert_in,
        grad_expert_out,
    )


def solution(mesh):
    split = Mesh(
        mesh.devices.reshape(4, 4, 2, mesh.shape["mp"]), ("expert_0", "expert_1", "expert_2", "mp")
    )
    in_specs = (
        P(EXPERT, "mp", None),
        P(None, EXPERT, "mp"),
        P("mp", EXPERT),
        P(),
        P(),
        P(),
        P(),
        P(EXPERT, None, "mp"),
        P(EXPERT, "mp", None),
        P(EXPERT, "mp", None),
        P(EXPERT, "mp"),
        P(EXPERT, "mp", None),
    )
    out_specs = (
        P(EXPERT, "mp", None),
        P(EXPERT, "mp", None),
        P(None, EXPERT, "mp"),
        P("mp", EXPERT),
        P(),
        P(),
        P(),
        P(),
        P(EXPERT, None, "mp"),
        P(EXPERT, "mp", None),
    )
    return jax.shard_map(body, mesh=split, in_specs=in_specs, out_specs=out_specs, check_vma=False)
```

```python
import functools
import math

import jax
import jax.numpy as jnp
from jax import lax
from jax.experimental import pallas as pl
from jax.experimental.pallas import tpu as pltpu
from jax.sharding import Mesh
from jax.sharding import PartitionSpec as P

HEADS = 12
HEAD_DIM = 64
EXPERTS = 64
BUCKETS = 32
REACH = 128
EXPERT = ("expert_0", "expert_1", "expert_2")
QUARTER = 128
PARTS = 4
WIDTH = 768
CHANNELS = 192
LOCAL_HEADS = CHANNELS // HEAD_DIM
QKV = 3 * CHANNELS
CAPACITY = 4
SLOTS = 512
HALF_SLOTS = SLOTS // 2
TAGGED = WIDTH + 128
TILE_STEPS = (0, 1, -1, 2, -2)

epsilon = 1e-06
f32 = jnp.float32
bf16 = jnp.bfloat16
BLOCK = 512
VMEM_LIMIT = 56 * 1024 * 1024


def dot(a, b, ca=1, cb=0, precision=None):
    return lax.dot_general(
        a, b, (((ca,), (cb,)), ((), ())), preferred_element_type=f32, precision=precision
    )


def struct(shape, dtype):
    return jax.ShapeDtypeStruct(shape, dtype)


ANY = pl.BlockSpec(memory_space=pl.ANY)
SMEM = pl.BlockSpec(memory_space=pltpu.SMEM)
VMEM = pl.BlockSpec(memory_space=pltpu.VMEM)


def call(kernel, outs, ins, in_specs=None, scratch=(), flops=10**8, moved=4 * 10**6, name=None):
    return pl.pallas_call(
        kernel,
        grid=(1,),
        out_shape=outs,
        in_specs=in_specs or [VMEM] * len(ins),
        out_specs=jax.tree.map(lambda _: VMEM, outs),
        scratch_shapes=scratch,
        cost_estimate=pl.CostEstimate(flops=flops, bytes_accessed=moved, transcendentals=0),
        compiler_params=pltpu.CompilerParams(vmem_limit_bytes=VMEM_LIMIT),
        name=name,
    )(*ins)


def shift(x, step):
    return lax.ppermute(x, "mp", [(i, (i + step) % PARTS) for i in range(PARTS)])


def gather4(x, way):
    left, right = shift(x, 1), shift(x, -1)
    far = shift(left, 1) if way > 0 else shift(right, -1)
    return x, right, far, left


def added(*terms):
    return functools.reduce(lambda a, b: a + b, [t.astype(f32) for t in terms])


def reduce4(pieces, way):
    own, right, far, left = pieces
    if way > 0:
        middle = right = added(right, shift(far, 1)).astype(bf16)
    else:
        middle = left = added(left, shift(far, -1)).astype(bf16)
    return (own, shift(right, 1), shift(left, -1)), middle


def to_experts(x):
    return lax.all_to_all(x.reshape(32, -1, x.shape[-1]), EXPERT, 0, 0, tiled=True)


def by_expert(slots):
    return tuple(slots[:, 8 * e : 8 * e + 8, :WIDTH].reshape(HALF_SLOTS, WIDTH) for e in range(2))


def summed_slots(terms):
    pieces = [added(*terms[e]).astype(bf16).reshape(32, 8, WIDTH) for e in range(2)]
    return jnp.concatenate(pieces, axis=1)


def sent_to_all(x, axis):
    peers = lax.axis_size(axis)
    return lax.all_to_all(jnp.broadcast_to(x[None], (peers, *x.shape)), axis, 0, 0, tiled=True)


def bucket_of(offsets):
    halfway = BUCKETS // 2
    exact_span = halfway // 2
    distance = jnp.abs(offsets)
    far_part = jnp.full_like(distance, exact_span)
    for step in range(1, exact_span):
        cutoff_level = math.ceil(exact_span * (REACH / exact_span) ** (step / exact_span) - 1e-09)
        far_part = far_part + jnp.where(distance >= cutoff_level, 1, 0)
    nearby = jnp.where(distance < exact_span, distance, far_part)
    return nearby + jnp.where(offsets > 0, halfway, 0)


def tile_buckets(step):
    shape = (QUARTER, QUARTER)
    offsets = (
        step * QUARTER
        + lax.broadcasted_iota(jnp.int32, shape, 1)
        - lax.broadcasted_iota(jnp.int32, shape, 0)
    )
    return bucket_of(offsets)


def possible(step):
    if step == 0:
        return range(BUCKETS)
    if step == 1:
        return range(BUCKETS // 2 + 1, BUCKETS)
    if step == -1:
        return range(1, BUCKETS // 2)
    return (BUCKETS - 1,) if step > 0 else (BUCKETS // 2 - 1,)


def tile_at(row_block, key_block):
    step = key_block - row_block
    return TILE_STEPS.index(max(-2, min(2, step)))


def bias_kernel(head_ref, table_ref, out_ref):
    head = head_ref[0]
    for t, step in enumerate(TILE_STEPS):
        buckets = tile_buckets(step)
        tiles = [jnp.zeros((QUARTER, QUARTER), f32)] * LOCAL_HEADS
        for b in possible(step):
            mask = buckets == b
            tiles = [jnp.where(mask, table_ref[b, head + h], tile) for h, tile in enumerate(tiles)]
        for h, tile in enumerate(tiles):
            out_ref[h, t] = tile


def inverse_size(values):
    return lax.rsqrt(jnp.mean(values * values, axis=-1, keepdims=True) + epsilon)


def as_column(row):
    return jnp.transpose(jnp.broadcast_to(row, (QUARTER, QUARTER)))


def start_kernel(x_ref, gain_ref, seg_ref, n0, n1):
    gain = gain_ref[...]
    for s, out in ((0, n0), (1, n1)):
        x = x_ref[s]
        out[:, :WIDTH] = (x * inverse_size(x) * gain).astype(bf16)
        out[:, WIDTH:] = as_column(seg_ref[s : s + 1].astype(f32)).astype(bf16)


def place_kernel(route_ref, cot_ref, weights_ref, place_ref, lines_ref):
    tri = (
        lax.broadcasted_iota(jnp.int32, (QUARTER, QUARTER), 0)
        >= lax.broadcasted_iota(jnp.int32, (QUARTER, QUARTER), 1)
    ).astype(bf16)
    for s in range(2):
        chosen = as_column(route_ref[s : s + 1].astype(f32)).astype(jnp.int32)
        mask = jnp.where(
            chosen == lax.broadcasted_iota(jnp.int32, (QUARTER, QUARTER), 1), 1.0, 0.0
        )
        running = dot(tri, mask.astype(bf16))
        rank = jnp.sum(mask * running, axis=-1, keepdims=True).astype(jnp.int32) - 1
        place = chosen[:, :1] * 8 + s * CAPACITY + rank
        slots = lax.broadcasted_iota(jnp.int32, (QUARTER, SLOTS), 1)
        place_ref[s * QUARTER : (s + 1) * QUARTER] = jnp.where(slots == place, 1.0, 0.0).astype(bf16)
    slots = dot(place_ref[...], cot_ref[...].astype(bf16), 0, 0)
    weights = weights_ref[...].astype(f32)
    for n in range(32):
        lines_ref[n] = jnp.concatenate([weights, slots[16 * n : 16 * n + 16]]).astype(bf16)


def position(me, k):
    return pl.multiple_of(lax.rem(me + k, PARTS) * QUARTER, QUARTER)


def same_document(g_ref):
    column = g_ref[:, WIDTH:].astype(f32)
    return column, jnp.transpose(column)[:1]


def bias_rows(tiles_ref, h, i):
    per = BLOCK // QUARTER
    return jnp.concatenate(
        [
            jnp.concatenate([tiles_ref[h, tile_at(r, j)] for j in range(PARTS)], axis=1)
            for r in range(i * per, (i + 1) * per)
        ],
        axis=0,
    )


def attend_kernel(
    me_ref, a0, a1, a2, a3, w_ref, tiles_ref, g_ref, qkv_ref, att_ref, lse_ref, p0, p1, p2, p3
):
    me = me_ref[0]
    for k, piece in enumerate((a0, a1, a2, a3)):
        g_ref[pl.ds(position(me, k), QUARTER), :] = piece[...]
    qkv_ref[...] = dot(g_ref[:, :WIDTH], w_ref[:, :QKV]).astype(bf16)
    column, row = same_document(g_ref)
    lse_ref[...] = jnp.zeros_like(lse_ref)
    for h in range(LOCAL_HEADS):
        lo = h * HEAD_DIM
        key = qkv_ref[:, CHANNELS + lo : CHANNELS + lo + HEAD_DIM]
        value = qkv_ref[:, 2 * CHANNELS + lo : 2 * CHANNELS + lo + HEAD_DIM]
        for i in range(PARTS * QUARTER // BLOCK):
            rows = slice(i * BLOCK, (i + 1) * BLOCK)
            query = qkv_ref[rows, lo : lo + HEAD_DIM] * HEAD_DIM ** (-0.5)
            scores = dot(query, key, 1, 1) + bias_rows(tiles_ref, h, i)
            scores = jnp.where(column[rows, :1] == row, scores, -1000000000.0)
            row_max = jnp.max(scores, axis=-1, keepdims=True)
            expos = jnp.exp(scores - row_max)
            total = jnp.sum(expos, axis=-1, keepdims=True)
            weights = (expos * (1.0 / total)).astype(bf16)
            att_ref[rows, lo : lo + HEAD_DIM] = dot(weights, value).astype(bf16)
            lse_ref[rows, h : h + 1] = row_max + jnp.log(total)
    for k, out in enumerate((p0, p1, p2, p3)):
        mine = att_ref[pl.ds(position(me, k), QUARTER), :]
        out[...] = dot(mine, w_ref[:, QKV:], 1, 1).astype(bf16)


def dispatch_kernel(
    x_ref, t00, t01, t02, t10, t11, t12, gain_ref, router_ref, route_ref, place_ref,
    hidden_ref, gate_ref, slots_ref,
):
    for s, terms in ((0, (t00, t01, t02)), (1, (t10, t11, t12))):
        rows = slice(s * QUARTER, (s + 1) * QUARTER)
        hidden_ref[rows] = x_ref[s] + added(*[t[...] for t in terms])
    hidden = hidden_ref[...]
    mixed = hidden * inverse_size(hidden) * gain_ref[...]
    low = mixed.astype(bf16)
    slots_ref[...] = dot(place_ref[...], low, 0, 0).astype(bf16)
    logits = dot(mixed, router_ref[...], precision=lax.Precision.HIGHEST)
    expos = jnp.exp(logits - jnp.max(logits, axis=-1, keepdims=True))
    shares = expos / jnp.sum(expos, axis=-1, keepdims=True)
    for s in range(2):
        rows = slice(s * QUARTER, (s + 1) * QUARTER)
        chosen = as_column(route_ref[s : s + 1].astype(f32)).astype(jnp.int32)[:, :EXPERTS]
        mask = chosen == lax.broadcasted_iota(jnp.int32, (QUARTER, EXPERTS), 1)
        gate = jnp.sum(jnp.where(mask, shares[rows], 0.0), axis=-1, keepdims=True)
        gate_ref[rows] = jnp.broadcast_to(gate, (QUARTER, 128))


WORK_ORDER = (2, 1, 3, 0)


def upstream_kernel(c0, c1, c2, c3, w_ref, u_ref):
    pieces = (c0, c1, c2, c3)
    for n, k in enumerate(WORK_ORDER):
        u_ref[n] = dot(pieces[k][...], w_ref[0], 1, 1).astype(bf16)


def expert_kernel(
    own_ref, x0, x1, x2, x3, u_ref, w_ref, router_ref, _, __,
    active_ref, scaled_ref, grad_ref, logit_ref, s0, s1, s2, s3, pre_ref,
):
    own = own_ref[0]
    router = router_ref[...]
    router_hi = router.astype(bf16)
    router_lo = (router - router_hi.astype(f32)).astype(bf16)
    router_both = jnp.concatenate([router_hi, router_lo], axis=1)
    c = math.sqrt(2.0 / math.pi)
    ca = c * 0.044715

    def work(xs, outs, first):
        x = jnp.concatenate([x_ref[...] for x_ref in xs])
        logits = dot(x, router_both)
        logits = logits[:, :EXPERTS] + logits[:, EXPERTS:]
        expos = jnp.exp(logits - jnp.max(logits, axis=-1, keepdims=True))
        shares = expos / jnp.sum(expos, axis=-1, keepdims=True)
        chosen = jnp.where(lax.broadcasted_iota(jnp.int32, shares.shape, 1) == own, 1.0, 0.0)
        gate = jnp.sum(shares * chosen, axis=-1, keepdims=True)
        pre_ref[...] = dot(x, w_ref[0])
        gate_grads = []
        for n in range(2):
            for part in range(HALF_SLOTS // 64):
                rows = slice(part * 64, part * 64 + 64)
                at = slice(n * HALF_SLOTS + part * 64, n * HALF_SLOTS + part * 64 + 64)
                pre = pre_ref[at, :]
                u = u_ref[n, rows, :].astype(f32)
                square = pre * pre
                t = jnp.tanh(pre * (c + ca * square))
                half = 0.5 + 0.5 * t
                active = pre * half
                slope = half + (0.5 * pre) * (1.0 - t * t) * (c + 3.0 * ca * square)
                gate_grads.append(jnp.sum(active * u, axis=-1, keepdims=True))
                active_ref[n, rows, :] = active.astype(bf16)
                scaled_ref[n, rows, :] = (gate[at] * active).astype(bf16)
                grad_ref[n, rows, :] = (gate[at] * u * slope).astype(bf16)
        logit_grad = shares * (chosen - gate) * jnp.concatenate(gate_grads)
        logit_hi = logit_grad.astype(bf16)
        logit_lo = (logit_grad - logit_hi.astype(f32)).astype(bf16)
        pre_grad = jnp.concatenate([grad_ref[0], grad_ref[1]])
        slot_grad = dot(pre_grad, w_ref[0], 1, 1) + dot(logit_hi, router_hi, 1, 1)
        for n, out in enumerate(outs):
            out[...] = slot_grad[n * HALF_SLOTS : (n + 1) * HALF_SLOTS].astype(bf16)
        term = dot(jnp.concatenate([logit_hi, logit_lo], axis=1), x, 0, 0)
        if first:
            logit_ref[...] = term
        else:
            logit_ref[...] += term

    pl.when(pl.program_id(0) == 0)(lambda: work((x2, x1), (s2, s1), True))
    pl.when(pl.program_id(0) == 1)(lambda: work((x3, x0), (s3, s0), False))


def output_kernel(active_ref, w_ref, _, __, ___, s0, s1, s2, s3):
    outs = (s0, s1, s2, s3)
    for n, k in enumerate(WORK_ORDER):
        outs[k][...] = dot(active_ref[n], w_ref[0]).astype(bf16)


def weights_kernel(scaled_ref, grad_ref, c0, c1, c2, c3, x0, x1, x2, x3, *rest):
    out_ref, in_ref, token_ref = rest[-3:]
    token_ref[...] = jnp.zeros_like(token_ref)
    upstream = jnp.concatenate([(c0, c1, c2, c3)[k][...] for k in WORK_ORDER])
    entered = jnp.concatenate([(x0, x1, x2, x3)[k][...] for k in WORK_ORDER])
    rows = (PARTS * HALF_SLOTS, WIDTH)
    out_ref[0] = dot(scaled_ref[...].reshape(rows), upstream, 0, 0)
    in_ref[0] = dot(entered, grad_ref[...].reshape(rows), 0, 0)


def router_kernel(a_ref, b_ref, _, out_ref):
    both = a_ref[...] + b_ref[...]
    rows = jnp.transpose(both[:EXPERTS] + both[EXPERTS:])
    none = jnp.zeros((8, EXPERTS), f32)
    for n in range(32):
        top, low = rows[24 * n : 24 * n + 16], rows[24 * n + 16 : 24 * n + 24]
        beside = jnp.concatenate([low, none])
        out_ref[n] = jnp.concatenate([top, beside], axis=1).astype(bf16)


def back_kernel(
    slots_ref, place_ref, hidden_ref, cot_ref, gain_ref, _, grad_ref, h0, h1, gain_grad_ref
):
    mixed_grad = dot(place_ref[...], slots_ref[...])
    hidden = hidden_ref[...]
    r = inverse_size(hidden)
    gain_grad_ref[...] = jnp.sum(mixed_grad * hidden * r, axis=0, keepdims=True)
    u = gain_ref[...] * mixed_grad
    grad = cot_ref[...] + r * u - hidden * (r * r * r * jnp.mean(hidden * u, axis=-1, keepdims=True))
    grad_ref[...] = grad
    h0[...] = grad[:QUARTER].astype(bf16)
    h1[...] = grad[QUARTER:].astype(bf16)


def result_kernel(slots_ref, place_ref, hidden_ref, gate_ref, out_ref):
    slots = slots_ref[...].reshape(SLOTS, WIDTH)
    back = dot(place_ref[...], slots)
    out_ref[...] = hidden_ref[...] + gate_ref[:, :1] * back


def attend_back_kernel(
    me_ref, a0, a1, a2, a3, w_ref, tiles_ref, g_ref, qkv_ref, lse_ref, _, __, ___,
    up_ref, dqkv_ref, sums_ref, gain_ref, p0, p1, p2, p3, tile_sums,
):
    me = me_ref[0]
    for k, piece in enumerate((a0, a1, a2, a3)):
        up_ref[pl.ds(position(me, k), QUARTER), :] = piece[...]
    att_grad = dot(up_ref[...], w_ref[:, QKV:]).astype(bf16)
    column, row = same_document(g_ref)
    tile_sums[...] = jnp.zeros_like(tile_sums)
    for h in range(LOCAL_HEADS):
        lo = h * HEAD_DIM
        key = qkv_ref[:, CHANNELS + lo : CHANNELS + lo + HEAD_DIM]
        value = qkv_ref[:, 2 * CHANNELS + lo : 2 * CHANNELS + lo + HEAD_DIM]
        key_grad = jnp.zeros((HEAD_DIM, PARTS * QUARTER), f32)
        value_grad = jnp.zeros((HEAD_DIM, PARTS * QUARTER), f32)
        for i in range(PARTS * QUARTER // BLOCK):
            rows = slice(i * BLOCK, (i + 1) * BLOCK)
            query = qkv_ref[rows, lo : lo + HEAD_DIM] * HEAD_DIM ** (-0.5)
            scores = dot(query, key, 1, 1) + bias_rows(tiles_ref, h, i)
            scores = jnp.where(column[rows, :1] == row, scores, -1000000000.0)
            weights = jnp.exp(scores - lse_ref[rows, h : h + 1])
            out_grad = att_grad[rows, lo : lo + HEAD_DIM]
            weights_grad = dot(out_grad, value, 1, 1)
            inner = jnp.sum(weights * weights_grad, axis=-1, keepdims=True)
            score_grad = (weights * (weights_grad - inner)).astype(bf16)
            wide = score_grad.astype(f32)
            for r in range(BLOCK // QUARTER):
                for j in range(PARTS):
                    tile_sums[h, tile_at(i * (BLOCK // QUARTER) + r, j)] += wide[
                        r * QUARTER : (r + 1) * QUARTER, j * QUARTER : (j + 1) * QUARTER
                    ]
            dqkv_ref[rows, lo : lo + HEAD_DIM] = (
                dot(score_grad, key) * HEAD_DIM ** (-0.5)
            ).astype(bf16)
            key_grad += dot(query, score_grad, 0, 0)
            value_grad += dot(out_grad, weights.astype(bf16), 0, 0)
        dqkv_ref[:, CHANNELS + lo : CHANNELS + lo + HEAD_DIM] = jnp.transpose(key_grad).astype(bf16)
        dqkv_ref[:, 2 * CHANNELS + lo : 2 * CHANNELS + lo + HEAD_DIM] = jnp.transpose(
            value_grad
        ).astype(bf16)
    gain = jnp.zeros((1, WIDTH), f32)
    for k, out in ((2, p2), (1, p1), (3, p3), (0, p0)):
        at = pl.ds(position(me, k), QUARTER)
        normed_grad = dot(dqkv_ref[at, :], w_ref[:, :QKV], 1, 1)
        out[...] = normed_grad.astype(bf16)
        gain += jnp.sum(normed_grad * g_ref[at, :WIDTH].astype(f32), axis=0, keepdims=True)
    gain_ref[...] = gain
    sums_ref[...] = jnp.zeros_like(sums_ref)
    for t, step in enumerate(TILE_STEPS):
        buckets = tile_buckets(step)
        for b in possible(step):
            mask = buckets == b
            for h in range(LOCAL_HEADS):
                sums_ref[h, b : b + 1] += jnp.sum(
                    jnp.where(mask, tile_sums[h, t], 0.0), axis=0, keepdims=True
                )


def projection_kernel(g0, g1, d0, d1, u0, u1, a0, a1, out_ref):
    out_ref[:, :QKV] = (
        dot(g0[:, :WIDTH], d0[...], 0, 0) + dot(g1[:, :WIDTH], d1[...], 0, 0)
    ).astype(bf16)
    out_ref[:, QKV:] = (dot(u0[...], a0[...], 0, 0) + dot(u1[...], a1[...], 0, 0)).astype(bf16)


def input_kernel(x_ref, gain_ref, grad_ref, t00, t01, t02, t10, t11, t12, out_ref):
    for s, terms in ((0, (t00, t01, t02)), (1, (t10, t11, t12))):
        x = x_ref[s]
        r = inverse_size(x)
        u = gain_ref[...] * added(*[t[...] for t in terms])
        out_ref[s] = (
            grad_ref[s * QUARTER : (s + 1) * QUARTER]
            + r * u
            - x * (r * r * r * jnp.mean(x * u, axis=-1, keepdims=True))
        )


def expert_spec(e):
    return pl.BlockSpec((1, WIDTH, WIDTH), lambda i: (e, 0, 0))


def body(
    inputs,
    projection_in,
    projection_out,
    gain_attention,
    gain_experts,
    router_weight,
    bias_table,
    expert_in,
    expert_out,
    routes,
    segments,
    cotangent,
):
    seq_here, quarter, width = inputs.shape
    rows = seq_here * quarter
    me = lax.axis_index("mp").reshape(1).astype(jnp.int32)
    first_head = me * LOCAL_HEADS
    gain1, gain2 = gain_attention.reshape(1, width), gain_experts.reshape(1, width)
    routes = routes.reshape(seq_here, quarter)
    upstream = cotangent.reshape(rows, width)
    piece = struct((QUARTER, WIDTH), bf16)
    slot_piece = struct((HALF_SLOTS, WIDTH), bf16)

    turned = jnp.concatenate(
        [jnp.moveaxis(projection_in, 1, 0).reshape(24, QKV), projection_out.T], axis=1
    )
    place, lines = call(
        place_kernel,
        (struct((rows, SLOTS), bf16), struct((32, 40, width), bf16)),
        (routes, upstream, turned),
        name="place",
    )
    lines = lax.all_to_all(lines, EXPERT, 0, 0, tiled=True)
    weights = lines[:, :24].reshape(WIDTH, QKV + CHANNELS)
    c_slots = by_expert(lines[:, 24:])

    tagged = struct((QUARTER, TAGGED), bf16)
    n0, n1 = call(start_kernel, (tagged, tagged), (inputs, gain1, segments), name="start")
    normed = (gather4(n0, 1), gather4(n1, -1))
    tiles = call(
        bias_kernel,
        struct((LOCAL_HEADS, len(TILE_STEPS), QUARTER, QUARTER), f32),
        (first_head, bias_table),
        [SMEM, SMEM],
        name="bias",
    )
    length = PARTS * QUARTER
    attended = [
        call(
            attend_kernel,
            (
                struct((length, TAGGED), bf16),
                struct((length, QKV), bf16),
                struct((length, CHANNELS), bf16),
                struct((length, 128), f32),
                piece, piece, piece, piece,
            ),
            (me, *normed[s], weights, tiles),
            [SMEM] + [VMEM] * 6,
            flops=2 * 10**9,
            name="attend",
        )
        for s in range(2)
    ]
    attention = [reduce4(attended[s][4:], (1, -1)[s])[0] for s in range(2)]

    c_all = [gather4(c, (1, -1)[e]) for e, c in enumerate(c_slots)]
    u = [
        call(
            upstream_kernel,
            struct((PARTS, HALF_SLOTS, WIDTH), bf16),
            (*c_all[e], expert_out),
            [VMEM] * 4 + [expert_spec(e)],
            flops=12 * 10**8,
            name="upstream",
        )
        for e in range(2)
    ]

    hidden, gate, slots = call(
        dispatch_kernel,
        (struct((rows, width), f32), struct((rows, 128), f32), struct((SLOTS, width), bf16)),
        (inputs, *attention[0], *attention[1], gain2, router_weight, routes, place),
        name="dispatch",
    )
    x_all = [gather4(x, (1, -1)[e]) for e, x in enumerate(by_expert(to_experts(slots)))]
    group = lax.axis_index(EXPERT).astype(jnp.int32)
    acts = struct((PARTS, HALF_SLOTS, WIDTH), bf16)
    pair = pl.BlockSpec((2, HALF_SLOTS, WIDTH), lambda i: (i, 0, 0))
    worked = []
    for e in range(2):
        earlier = (worked[0][4], u[0]) if e else (x_all[1][1], u[1])
        outs = pl.pallas_call(
            expert_kernel,
            grid=(2,),
            out_shape=(acts, acts, acts, struct((2 * EXPERTS, WIDTH), f32)) + (slot_piece,) * 4,
            in_specs=[SMEM] + [VMEM] * 4 + [pair, expert_spec(e), VMEM, ANY, ANY],
            out_specs=(pair, pair, pair) + (VMEM,) * 5,
            scratch_shapes=[pltpu.VMEM((SLOTS, WIDTH), f32)],
            cost_estimate=pl.CostEstimate(
                flops=24 * 10**8, bytes_accessed=2 * 10**7, transcendentals=0
            ),
            compiler_params=pltpu.CompilerParams(vmem_limit_bytes=VMEM_LIMIT),
            name="expert",
        )((group * 2 + e).reshape(1), *x_all[e], u[e], expert_in, router_weight, *earlier)
        worked.append(outs)
    slot_terms, middles = zip(reduce4(worked[0][4:], 1), reduce4(worked[1][4:], -1))
    returned = to_experts(summed_slots(slot_terms))
    whole = struct((2, WIDTH, WIDTH), f32)
    expert_grads, tokens = (), []
    for e in range(2):
        ins = (worked[e][1], worked[e][2], *c_all[e], *x_all[e])
        *expert_grads, token = pl.pallas_call(
            weights_kernel,
            grid=(1,),
            out_shape=(whole, whole, struct((8, 128), f32)),
            in_specs=[VMEM] * 10 + [pl.BlockSpec(memory_space=pl.ANY)] * len(expert_grads),
            out_specs=(expert_spec(e), expert_spec(e), VMEM),
            input_output_aliases={10: 0, 11: 1} if expert_grads else {},
            cost_estimate=pl.CostEstimate(
                flops=24 * 10**8, bytes_accessed=2 * 10**7, transcendentals=0
            ),
            compiler_params=pltpu.CompilerParams(vmem_limit_bytes=VMEM_LIMIT),
            name="expert_weights",
        )(*ins, *expert_grads)
        tokens.append(token)
    grad_expert_out, grad_expert_in = expert_grads

    outputs = [
        call(
            output_kernel,
            (slot_piece,) * 4,
            (worked[e][0], expert_out, *middles, tokens[0]),
            [VMEM, expert_spec(e), ANY, ANY, ANY],
            flops=12 * 10**8,
            name="expert_output",
        )
        for e in range(2)
    ]
    output_slots = summed_slots([reduce4(outputs[e], (1, -1)[e])[0] for e in range(2)])
    router = call(
        router_kernel,
        struct((32, 16, 128), bf16),
        (worked[0][3], worked[1][3], middles[0]),
        [VMEM, VMEM, ANY],
        name="router_gradient",
    )
    hidden_grad, h0, h1, gain2_grad = call(
        back_kernel,
        (struct((rows, width), f32), piece, piece, struct((1, width), f32)),
        (returned.reshape(SLOTS, width), place, hidden, upstream, gain2, tokens[1]),
        [VMEM] * 5 + [ANY],
        name="back",
    )
    grads = (gather4(h0, 1), gather4(h1, -1))
    attended_back = [
        call(
            attend_back_kernel,
            (
                struct((length, width), bf16),
                struct((length, QKV), bf16),
                struct((LOCAL_HEADS, BUCKETS, 128), f32),
                struct((1, width), f32),
                piece, piece, piece, piece,
            ),
            (me, *grads[s], weights, tiles, *attended[s][:2], attended[s][3], *grads[1 - s][1:]),
            [SMEM] + [VMEM] * 9 + [ANY] * 3,
            scratch=[pltpu.VMEM((LOCAL_HEADS, len(TILE_STEPS), QUARTER, QUARTER), f32)],
            flops=4 * 10**9,
            name="attend_back",
        )
        for s in range(2)
    ]
    normed_grad = [reduce4(attended_back[s][4:], (1, -1)[s])[0] for s in range(2)]
    input_grad = call(
        input_kernel,
        struct(inputs.shape, f32),
        (inputs, gain1, hidden_grad, *normed_grad[0], *normed_grad[1]),
        name="input_gradient",
    )

    output_slots = jnp.concatenate([output_slots, router], axis=2)
    output_back = to_experts(output_slots)
    router_rows = jnp.sum(output_back[:, :, width:].astype(f32), axis=0)
    router_rows = jnp.concatenate([router_rows[:, :EXPERTS], router_rows[:8, EXPERTS:]])
    result = call(
        result_kernel,
        struct((rows, width), f32),
        (output_back, place, hidden, gate),
        [pl.BlockSpec((32, 16, WIDTH), lambda i: (0, 0, 0)), VMEM, VMEM, VMEM],
        name="result",
    )
    partial = call(
        projection_kernel,
        struct((WIDTH, QKV + CHANNELS), bf16),
        (
            attended[0][0], attended[1][0], attended_back[0][1], attended_back[1][1],
            attended_back[0][0], attended_back[1][0], attended[0][2], attended[1][2],
        ),
        flops=16 * 10**8,
        name="projection_gradient",
    )
    table_local = jnp.sum(attended_back[0][2] + attended_back[1][2], axis=-1).T
    table = lax.dynamic_update_slice(
        jnp.zeros((BUCKETS, HEADS), f32), table_local, (0, first_head[0])
    )
    gain1_grad = (attended_back[0][3] + attended_back[1][3]) / gain1
    small = jnp.concatenate(
        [t.reshape(-1) for t in (router_rows, gain1_grad, gain2_grad, table)]
    ).reshape(27, 128)
    small = added(small, shift(small, 1), shift(small, -1), shift(small, 2)).reshape(-1)
    lines = jnp.pad(small.astype(bf16), (0, 5 * width - small.size)).reshape(1, 5, width)
    lines = jnp.concatenate(
        [partial.reshape(32, 24, width), jnp.broadcast_to(lines, (32, 5, width))], axis=1
    )
    arrived = lax.all_to_all(lines, EXPERT, 0, 0, tiled=True)
    projections = jnp.sum(arrived[:, :24].astype(f32), axis=0)
    grad_projection_in = jnp.moveaxis(projections[:, :QKV].reshape(24, 3, CHANNELS), 1, 0)
    grad_projection_out = projections[:, QKV:].T
    grad_router = arrived[:, 24:26].astype(f32).reshape(WIDTH, EXPERTS)
    late = jnp.sum(arrived[:, 26:].astype(f32), axis=0).reshape(-1)
    grad_gain_attention = late[:width]
    grad_gain_experts = late[width : 2 * width]
    grad_table = late[2 * width : 2 * width + BUCKETS * HEADS].reshape(BUCKETS, HEADS)
    return (
        result.reshape(seq_here, quarter, width),
        input_grad,
        grad_projection_in,
        grad_projection_out,
        grad_gain_attention,
        grad_gain_experts,
        grad_router,
        grad_table,
        grad_expert_in,
        grad_expert_out,
    )


def solution(mesh):
    split = Mesh(
        mesh.devices.reshape(4, 4, 2, mesh.shape["mp"]), ("expert_0", "expert_1", "expert_2", "mp")
    )
    in_specs = (
        P(EXPERT, "mp", None),
        P(None, EXPERT, "mp"),
        P("mp", EXPERT),
        P(),
        P(),
        P(),
        P(),
        P(EXPERT, None, "mp"),
        P(EXPERT, "mp", None),
        P(EXPERT, "mp", None),
        P(EXPERT, "mp"),
        P(EXPERT, "mp", None),
    )
    out_specs = (
        P(EXPERT, "mp", None),
        P(EXPERT, "mp", None),
        P(None, EXPERT, "mp"),
        P("mp", EXPERT),
        P(),
        P(),
        P(),
        P(),
        P(EXPERT, None, "mp"),
        P(EXPERT, "mp", None),
    )
    return jax.shard_map(body, mesh=split, in_specs=in_specs, out_specs=out_specs, check_vma=False)
```
